32 devices in a mesh: dp: 4 (over x, core), expert: 8 (over z, y).
Axes of the slice: x: 2, y: 2, z: 4, core: 2. Of those that a mesh axis runs over, the one named last changes fastest.
Arguments:
- patches: bfloat16 [18432, 768], P(('dp', 'expert')), may hold values from -6 to 6
- padding: int32 [18432], P(('dp', 'expert')), may hold values from 0 to 1, as said below
- expert_ids: int32 [18432, 2], P(('dp', 'expert')), may hold values from 0 to 7, all different within a row; in each aligned block of 576 rows (0 to 575, 576 to 1151, ...) at most 192 rows name the same one
- priority: int32 [18432], P(('dp', 'expert')), may hold values from 0 to 18431, each once
- norm1_gain: float32 [768], replicated, may hold values from 0.5 to 1.5
- norm1_bias: float32 [768], replicated, may hold values from -0.875 to 0.875
- qkv_weight: bfloat16 [768, 2304], replicated, may hold values from -0.21875 to 0.21875
- qv_bias: float32 [1536], replicated, may hold values from -0.1875 to 0.1875
- out_weight: bfloat16 [768, 768], replicated, may hold values from -2.5 to 2.5
- out_bias: float32 [768], replicated, may hold values from -0.875 to 0.875
- norm2_gain: float32 [768], replicated, may hold values from 0.5 to 1.5
- norm2_bias: float32 [768], replicated, may hold values from -0.875 to 0.875
- router: bfloat16 [768, 8], replicated, may hold values from -0.15625 to 0.15625
- expert_in: bfloat16 [8, 768, 3072], P('expert'), may hold values from -0.21875 to 0.21875
- expert_in_bias: float32 [8, 3072], P('expert'), may hold values from -0.625 to 0.625
- expert_out: bfloat16 [8, 3072, 768], P('expert'), may hold values from -0.21875 to 0.21875
- expert_out_bias: float32 [8, 768], P('expert'), may hold values from -0.875 to 0.875
- cotangent: bfloat16 [18432, 768], P(('dp', 'expert')), may hold values from -6 to 6
Outputs:
- output: bfloat16 [18432, 768], P(('dp', 'expert'))
- grad_patches: bfloat16 [18432, 768], P(('dp', 'expert'))
- grad_norm1_gain: float32 [768], P('expert')
- grad_norm1_bias: float32 [768], P('expert')
- grad_qkv_weight: float32 [768, 2304], P('expert')
- grad_qv_bias: float32 [1536], P('expert')
- grad_out_weight: float32 [768, 768], P('expert')
- grad_out_bias: float32 [768], P('expert')
- grad_norm2_gain: float32 [768], P('expert')
- grad_norm2_bias: float32 [768], P('expert')
- grad_router: float32 [768, 8], P('expert')
- grad_expert_in: float32 [8, 768, 3072], P('expert', None, 'dp')
- grad_expert_in_bias: float32 [8, 3072], P('expert', 'dp')
- grad_expert_out: float32 [8, 3072, 768], P('expert', 'dp')
- grad_expert_out_bias: float32 [8, 768], P('expert', 'dp')
The draws below stay inside these ranges and needn't reach their ends.
Inputs may be any that keep to these rules, and one draw needn't show every extreme that they name: `padding`: 1 marks a real patch; in each image of 576 patches the ones form a prefix of 504 patches or more. `expert_ids`: each patch names two different experts; among the patches of one device no expert is named by more than 192 of them, a bound that some block reaches. `priority`: every rank occurs once; a lower rank is served first.
All inputs are finite; a program needn't handle non-finite values.
Results may differ from the reference program's by a relative error of at most 0.02.
Values may be sent and summed in bfloat16 or wider, within the bound.
A program may use at most 384 MiB of HBM per device.

```python
import math
import jax
import jax.numpy as jnp
import numpy as np
from jax import lax

D = 768
HEADS = 12
HEAD_DIM = 64
FF = 3072
SEQ_LEN = 576
TOK_DEV = 576
EXPERTS = 8
TOKENS = 18432
MOST = 192
CAP = 4839


def draw_padding(key, part):
    key = jax.random.fold_in(key, 11)
    images = TOKENS // SEQ_LEN
    lengths = jax.random.randint(key, (images,), SEQ_LEN - SEQ_LEN // 8, SEQ_LEN + 1, dtype=jnp.int32)
    positions = jnp.arange(SEQ_LEN, dtype=jnp.int32)
    return (positions[None, :] < lengths[:, None]).astype(jnp.int32).reshape(TOKENS)


def level_of(stream_key, dims, cuts, low, largest):
    def one(dim, parts):
        draws = jax.random.uniform(jax.random.fold_in(jax.random.fold_in(stream_key, 6), dim), (parts,), jnp.float32, low / len(cuts), largest / len(cuts))
        return jnp.repeat(jnp.exp(draws), dims[dim] // parts).reshape((-1,) + (1,) * (len(dims) - dim - 1))

    loudness = one(*cuts[0])
    for cut in cuts[1:]:
        loudness = loudness * one(*cut)
    return loudness


def assign_block(own_key, own, number, rows, count, top, reach, skew):
    ranking = jax.random.permutation(own_key, count)
    crowded, usual = load_shares(count, rows * top, reach, skew, True), load_shares(count, rows * top, reach, skew, False)
    places = jnp.arange(count)

    def named(sizes, offset_by):
        used = int((sizes > 0).sum())
        fixed = max(1, used // 4)
        moved = fixed + (places - fixed + offset_by * (used - fixed)) % max(1, count - fixed)
        return jnp.zeros((count,), jnp.int32).at[ranking[jnp.where(places < fixed, places, moved)]].set(jnp.asarray(sizes, jnp.int32))

    sizes = jnp.where(number % 4 == 0, named(crowded, number // 4), named(usual, number - number // 4 - 1))
    mixed = jax.random.permutation(jax.random.fold_in(own, 3), count)
    giver, taker = mixed[0:count // 2 * 2:2], mixed[1:count // 2 * 2:2]
    margin = jnp.minimum(sizes[giver] - 1, reach - sizes[taker]) // 2
    margin = jnp.where((giver == ranking[0]) | (taker == ranking[0]) | (sizes[taker] == 0), 0, jnp.maximum(margin, 0))
    moved = jax.random.randint(jax.random.fold_in(own, 4), (count // 2,), 0, 1 << 20) % (margin + 1)
    sizes = sizes.at[giver].add(-moved).at[taker].add(moved)
    labels = jnp.searchsorted(jnp.cumsum(sizes), jnp.arange(rows * top), side="right").astype(jnp.int32)
    grid = labels.reshape(top, rows).T
    grid = grid[jax.random.permutation(jax.random.fold_in(own, 1), rows)]
    offset_by = jax.random.randint(jax.random.fold_in(own, 2), (rows, 1), 0, top)
    return jnp.take_along_axis(grid, (jnp.arange(top)[None, :] + offset_by) % top, axis=1)


def load_shares(number_of, total, most, lean, full):
    portions = [(1 << 20) // math.isqrt(rank ** lean) + 1 for rank in range(1, number_of + 1)]
    largest = most if full else min(most, max(-(-total // number_of), total * portions[0] // sum(portions)))
    least = 1 if total - largest >= number_of - 1 else 0
    holding, surplus = [largest] + [least] * (number_of - 1), total - largest - least * (number_of - 1)
    while surplus > 0:
        free = [i for i in range(1, number_of) if holding[i] < largest] or [i for i in range(1, number_of) if holding[i] < most]
        pool, budget = sum([portions[i] for i in free]), surplus
        for i in free:
            extra = min(most - holding[i], max(1, budget * portions[i] // pool), surplus)
            holding[i] = holding[i] + extra
            surplus = surplus - extra
    return np.array(holding)


def scatter_about(stream_key, dims, deviation, bound, split=(), kind=jnp.bfloat16):
    array = jax.random.normal(stream_key, dims, jnp.float32) * deviation
    if len(split) > 0:
        array = level_of(stream_key, dims, split, -0.22, 0.18) * array
    return jnp.clip(array, min=-bound, max=bound).astype(kind)


def setup_inputs(seed: int = 0) -> dict:
    seeds = jax.random.split(jax.random.key(seed), 19)
    patches = scatter_about(seeds[0], (TOKENS, D), 1.0, 6.0, ((0, 32),))
    padding = draw_padding(jax.random.fold_in(seeds[18], 71), 0)
    expert_ids_keys = jax.random.split(jax.random.fold_in(seeds[2], 1), TOKENS // TOK_DEV)
    expert_ids_turns = jax.random.permutation(jax.random.fold_in(seeds[2], 3), TOKENS // TOK_DEV)
    expert_ids = jax.vmap(lambda own, number: assign_block(jax.random.fold_in(seeds[2], 2), own, number, TOK_DEV, EXPERTS, 2, MOST, 2))(expert_ids_keys, expert_ids_turns).reshape((TOKENS, 2))
    priority = jax.random.permutation(seeds[3], TOKENS).astype(jnp.int32)
    norm1_gain = jnp.clip(1.0 + 0.1 * jax.random.normal(seeds[4], (D,), jnp.float32), 0.5, 1.5)
    norm1_bias = scatter_about(seeds[5], (D,), 0.15, 0.875, (), jnp.float32)
    qkv_weight = scatter_about(seeds[6], (D, 3 * D), D ** -0.5, 0.21875)
    qv_bias = scatter_about(seeds[7], (2 * D,), 0.03, 0.1875, (), jnp.float32)
    out_weight = scatter_about(seeds[8], (D, D), (D * 4 // SEQ_LEN) ** -0.5, 2.5)
    out_bias = scatter_about(seeds[9], (D,), 0.15, 0.875, (), jnp.float32)
    norm2_gain = jnp.clip(1.0 + 0.1 * jax.random.normal(seeds[10], (D,), jnp.float32), 0.5, 1.5)
    norm2_bias = scatter_about(seeds[11], (D,), 0.15, 0.875, (), jnp.float32)
    router = scatter_about(seeds[12], (D, EXPERTS), 0.025, 0.15625)
    expert_in = scatter_about(seeds[13], (EXPERTS, D, FF), D ** -0.5, 0.21875, ((0, 8),))
    expert_in_bias = scatter_about(seeds[14], (EXPERTS, FF), 0.1, 0.625, ((0, 8),), jnp.float32)
    expert_out = scatter_about(seeds[15], (EXPERTS, FF, D), (FF // 4) ** -0.5, 0.21875, ((0, 8),))
    expert_out_bias = scatter_about(seeds[16], (EXPERTS, D), 0.15, 0.875, ((0, 8),), jnp.float32)
    cotangent = scatter_about(seeds[17], (TOKENS, D), 1.0, 6.0, ((0, 32),))
    return {"patches": patches, "padding": padding, "expert_ids": expert_ids, "priority": priority, "norm1_gain": norm1_gain, "norm1_bias": norm1_bias, "qkv_weight": qkv_weight, "qv_bias": qv_bias, "out_weight": out_weight, "out_bias": out_bias, "norm2_gain": norm2_gain, "norm2_bias": norm2_bias, "router": router, "expert_in": expert_in, "expert_in_bias": expert_in_bias, "expert_out": expert_out, "expert_out_bias": expert_out_bias, "cotangent": cotangent}


PRECISION_TOP = lax.Precision.HIGHEST

@jax.custom_vjp
def reduced_input(v):
    return lax.optimization_barrier(v.astype(jnp.bfloat16)).astype(jnp.float32)

@jax.custom_vjp
def reduced_gradient(v):
    return v

def low_keep(v):
    return (reduced_input(v), None)

def low_pass(kept, grad):
    return (grad,)

def back_keep(v):
    return (v, None)

def back_low(kept, grad):
    return (reduced_input(grad),)
reduced_input.defvjp(low_keep, low_pass)
reduced_gradient.defvjp(back_keep, back_low)

def normalize(values, gain, shift):
    centred = values - lax.optimization_barrier(jnp.mean(values, axis=-1, keepdims=True))
    inverse = lax.rsqrt(lax.optimization_barrier(jnp.mean(centred * centred, axis=-1, keepdims=True)) + 1e-06)
    return centred * inverse * gain + shift

def reference(patches, padding, expert_ids, priority, norm1_gain, norm1_bias, qkv_weight, qv_bias, out_weight, out_bias, norm2_gain, norm2_bias, router, expert_in, expert_in_bias, expert_out, expert_out_bias, cotangent):
    valid_rows = padding > 0
    pair_expert = jnp.concatenate([expert_ids[:, 0], expert_ids[:, 1]])
    pair_valid = jnp.concatenate([valid_rows, valid_rows])
    pair_token = jnp.concatenate([jnp.arange(TOKENS, dtype=jnp.int32), jnp.arange(TOKENS, dtype=jnp.int32)])
    rank_order = jnp.argsort(jnp.concatenate([priority, priority + TOKENS]))
    pair_code = jnp.where(pair_valid[rank_order], pair_expert[rank_order], EXPERTS)
    expert_hits = (pair_code[:, None] == jnp.arange(EXPERTS, dtype=jnp.int32)[None, :]).astype(jnp.int32)
    ahead_count = lax.optimization_barrier(jnp.sum((jnp.cumsum(expert_hits, axis=0) - expert_hits) * expert_hits, axis=1)).astype(jnp.int32)
    position = jnp.zeros((2 * TOKENS,), jnp.int32).at[rank_order].set(ahead_count)
    kept_pairs = pair_valid & (position < CAP)
    flat_slot = pair_expert * CAP + position
    slot_target = jnp.where(kept_pairs, flat_slot, EXPERTS * CAP)
    slot_token = jnp.zeros((EXPERTS * CAP,), jnp.int32).at[slot_target].set(pair_token, mode='drop')
    slot_live = jnp.zeros((EXPERTS * CAP,), jnp.float32).at[slot_target].set(1.0, mode='drop')
    pair_slot = jnp.where(kept_pairs, flat_slot, 0).reshape(2, TOKENS).T
    pair_keep = kept_pairs.astype(jnp.float32).reshape(2, TOKENS).T
    groups = TOKENS // (4 * SEQ_LEN)

    def forward(inputs, first_gain, first_shift, query_key_value_weight, qv_shift, output_weight, output_bias, second_gain, second_shift, router_matrix, in_matrices, in_shifts, out_matrices, out_shifts):
        projection_bias = jnp.concatenate([qv_shift[:D], jnp.zeros((D,), jnp.float32), qv_shift[D:]])

        def attention_group(pieces):
            group_rows, group_valid = pieces
            layer_normalized = reduced_input(normalize(group_rows, first_gain, first_shift))
            projected_output = reduced_input(reduced_gradient(jnp.einsum('apf,fo->apo', layer_normalized, query_key_value_weight, precision=PRECISION_TOP) + projection_bias))
            queries = projected_output[..., :D].reshape(4, SEQ_LEN, HEADS, HEAD_DIM)
            key_rows = projected_output[..., D:2 * D].reshape(4, SEQ_LEN, HEADS, HEAD_DIM)
            value_rows = projected_output[..., 2 * D:].reshape(4, SEQ_LEN, HEADS, HEAD_DIM)
            scores = jnp.einsum('sqhd,skhd->shqk', queries, key_rows, precision=PRECISION_TOP) * HEAD_DIM ** (-0.5)
            scores = reduced_gradient(jnp.where(group_valid[:, None, None, :], scores, -1000000000.0))
            row_peak = lax.optimization_barrier(jnp.max(scores, axis=-1, keepdims=True))
            raised = jnp.exp(scores - row_peak)
            weights = reduced_input(raised / lax.optimization_barrier(jnp.sum(raised, axis=-1, keepdims=True)))
            attention_output = reduced_input(reduced_gradient(jnp.einsum('shqk,skhd->sqhd', weights, value_rows, precision=PRECISION_TOP))).reshape(4, SEQ_LEN, D)
            residual_branch = reduced_gradient(jnp.einsum('apf,fo->apo', attention_output, output_weight, precision=PRECISION_TOP) + output_bias)
            return group_rows + residual_branch
        residual = lax.map(jax.checkpoint(attention_group), (inputs.reshape(groups, 4, SEQ_LEN, D), valid_rows.reshape(groups, 4, SEQ_LEN))).reshape(TOKENS, D)
        second_normed = reduced_input(normalize(residual, second_gain, second_shift))
        logits = reduced_gradient(jnp.dot(second_normed, router_matrix, precision=PRECISION_TOP))
        logit_peak = lax.optimization_barrier(jnp.max(logits, axis=-1, keepdims=True))
        raised_logits = jnp.exp(logits - logit_peak)
        probabilities = raised_logits / lax.optimization_barrier(jnp.sum(raised_logits, axis=-1, keepdims=True))
        picked = jnp.take_along_axis(probabilities, expert_ids, axis=1)
        gate_values = picked / lax.optimization_barrier(jnp.sum(picked, axis=1, keepdims=True))
        slot_rows = reduced_gradient(second_normed[slot_token] * slot_live[:, None]).reshape(EXPERTS, CAP, D)

        def expert_block(pieces):
            expert_rows, first_matrix, first_shifts, second_matrix, second_shifts = pieces
            hidden_pre = reduced_gradient(jnp.dot(expert_rows, first_matrix, precision=PRECISION_TOP) + first_shifts)
            hidden = reduced_input(jax.nn.gelu(hidden_pre, approximate=False))
            return reduced_input(reduced_gradient(jnp.dot(hidden, second_matrix, precision=PRECISION_TOP) + second_shifts))
        produced = lax.map(jax.checkpoint(expert_block), (slot_rows, in_matrices, in_shifts, out_matrices, out_shifts)).reshape(EXPERTS * CAP, D)
        combined = gate_values[:, 0:1] * (produced[pair_slot[:, 0]] * pair_keep[:, 0:1])
        combined = combined + gate_values[:, 1:2] * (produced[pair_slot[:, 1]] * pair_keep[:, 1:2])
        return residual + combined
    floats = (patches.astype(jnp.float32), norm1_gain.astype(jnp.float32), norm1_bias.astype(jnp.float32), qkv_weight.astype(jnp.float32), qv_bias.astype(jnp.float32), out_weight.astype(jnp.float32), out_bias.astype(jnp.float32), norm2_gain.astype(jnp.float32), norm2_bias.astype(jnp.float32), router.astype(jnp.float32), expert_in.astype(jnp.float32), expert_in_bias.astype(jnp.float32), expert_out.astype(jnp.float32), expert_out_bias.astype(jnp.float32))
    output, pullback = jax.vjp(forward, *floats)
    gradients = pullback(cotangent.astype(jnp.float32))
    return (output.astype(jnp.bfloat16), gradients[0].astype(jnp.bfloat16), gradients[1], gradients[2], gradients[3], gradients[4], gradients[5], gradients[6], gradients[7], gradients[8], gradients[9], gradients[10], gradients[11], gradients[12], gradients[13])
```

```python
from functools import partial

import jax
import jax.numpy as jnp
from jax import lax
from jax.experimental import pallas as pl
from jax.experimental.pallas import tpu as pltpu
from jax.sharding import PartitionSpec as P

HEADS = 12
HEAD_DIM = 64
SEQ_LEN = 576
LOG2E = 1.4426950408889634
EPS = 1e-06
MESH = pl.DeviceIdType.MESH
NN = (((1,), (0,)), ((), ()))
NT = (((1,), (1,)), ((), ()))
TN = (((0,), (0,)), ((), ()))
VMEM_BYTES = 60 << 20
bf16 = jnp.bfloat16
f32 = jnp.float32
i32 = jnp.int32


def dot(a, b, dims=NN):
    return lax.dot_general(a, b, dims, preferred_element_type=f32)


def iota(shape, axis):
    return lax.broadcasted_iota(i32, shape, axis)


def ones_where(mask):
    return jnp.where(mask, 1.0, 0.0).astype(bf16)


def standardize(values):
    centred = values - jnp.mean(values, axis=-1, keepdims=True)
    inverse = lax.rsqrt(jnp.mean(centred * centred, axis=-1, keepdims=True) + EPS)
    return centred * inverse, inverse


def greet(peers):
    barrier = pltpu.get_barrier_semaphore()
    for peer in peers:
        pl.semaphore_signal(barrier, inc=1, device_id=peer, device_id_type=MESH)
    pl.semaphore_wait(barrier, len(peers))


def send(src, dst, send_sem, recv_sem, peer):
    copy = pltpu.make_async_remote_copy(
        src_ref=src, dst_ref=dst, send_sem=send_sem, recv_sem=recv_sem,
        device_id=peer, device_id_type=MESH,
    )
    copy.start()
    return copy


def front_kernel(
    copies, experts, most, capacity,
    patches_ref, cot_ref, rows_ref, cols_ref, gain1_ref, bias1_ref, qkv_w_ref, qv_bias_ref,
    out_w_ref, out_bias_ref, gain2_ref, bias2_ref, router_ref,
    recv_cot_ref, x_slots_ref, gate_slots_ref, qkv_ref, att_t_ref, lse_ref, residual_ref,
    second_ref, first_ref, pairs_ref, probs_ref,
    cot_send, table, counts, cot_ss, cot_rs, near_ss, near_rs, far_ss, far_rs,
):
    me_dp = lax.axis_index("dp")
    me = lax.axis_index("expert")
    rows, width = patches_ref.shape
    greet(
        [(me_dp, me ^ o) for o in range(1, experts)]
        + [(me_dp ^ p, me) for p in range(1, copies)]
    )
    near = [
        send(rows_ref, table.at[0, o], near_ss.at[o], near_rs.at[o], (me_dp, me ^ o))
        for o in range(1, experts)
    ]
    table[0, 0] = rows_ref[...]
    id0_row, id1_row = rows_ref[1:2, :] ^ me, rows_ref[2:3, :] ^ me
    expert_rows = iota((experts, rows), 0)
    named_t = ones_where((expert_rows == id0_row) | (expert_rows == id1_row))
    before_t = ones_where(iota((rows, rows), 0) < iota((rows, rows), 1))
    place_t = dot(named_t, before_t).astype(i32) + expert_rows * most
    slot0_row = jnp.sum(jnp.where(expert_rows == id0_row, place_t, 0), axis=0, keepdims=True)
    slot1_row = jnp.sum(jnp.where(expert_rows == id1_row, place_t, 0), axis=0, keepdims=True)
    id0_col, id1_col = cols_ref[:, 1:2], cols_ref[:, 2:3]
    rel0_col, rel1_col = id0_col ^ me, id1_col ^ me
    expert_cols = iota((rows, experts), 1)
    named = ones_where((expert_cols == rel0_col) | (expert_cols == rel1_col))
    before = ones_where(iota((rows, rows), 1) < iota((rows, rows), 0))
    place = dot(before, named).astype(i32) + expert_cols * most
    slot0_col = jnp.sum(jnp.where(expert_cols == rel0_col, place, 0), axis=1, keepdims=True)
    slot1_col = jnp.sum(jnp.where(expert_cols == rel1_col, place, 0), axis=1, keepdims=True)

    def taken(o):
        slots = iota((most, rows), 0) + o * most
        return ones_where((slots == slot0_row) | (slots == slot1_row))

    cot_value = cot_ref[...]
    cots = []
    for o in [*range(1, experts), 0]:
        picked = dot(taken(o), cot_value).astype(bf16)
        if o == 0:
            recv_cot_ref[0:most, :] = picked
            continue
        part = pl.ds(o * most, most)
        cot_send[part, :] = picked
        cots.append(
            send(cot_send.at[part], recv_cot_ref.at[part], cot_ss.at[o], cot_rs.at[o], (me_dp, me ^ o))
        )
    inputs = patches_ref[...].astype(f32)
    first = (standardize(inputs)[0] * gain1_ref[...] + bias1_ref[...]).astype(bf16)
    first_ref[...] = first
    qkv_ref[:, :width] = (dot(first, qkv_w_ref[:, :width]) + qv_bias_ref[:, :width]).astype(bf16)
    qkv_ref[:, width : 2 * width] = dot(first, qkv_w_ref[:, width : 2 * width]).astype(bf16)
    qkv_ref[:, 2 * width :] = (
        dot(first, qkv_w_ref[:, 2 * width :]) + qv_bias_ref[:, width:]
    ).astype(bf16)
    key_bias = jnp.where(cols_ref[:, 3:4] > 0, 0.0, -1e30)
    scale = LOG2E * HEAD_DIM ** (-0.5)
    pair_width = 2 * HEAD_DIM

    for near_copy in near:
        near_copy.wait_recv()
    far = [
        send(table.at[0], table.at[p], far_ss.at[p], far_rs.at[p], (me_dp ^ p, me))
        for p in range(1, copies)
    ]

    def attend(pair, _):
        base = pl.multiple_of(pair * pair_width, pair_width)
        q = qkv_ref[:, pl.ds(base, pair_width)]
        k = qkv_ref[:, pl.ds(base + width, pair_width)]
        v_t = qkv_ref[:, pl.ds(base + 2 * width, pair_width)].T
        lanes = iota((rows, pair_width), 1)
        outs, stats = [], []
        for a in range(2):
            k_a = jnp.where((lanes >= HEAD_DIM) == (a == 1), k, jnp.zeros((), bf16))
            scores = dot(k_a, q, NT) + key_bias
            peak = jnp.max(scores, axis=0, keepdims=True)
            raised = jnp.exp2(scores * scale - peak * scale)
            total = jnp.sum(raised, axis=0, keepdims=True)
            out = dot(v_t[a * HEAD_DIM : (a + 1) * HEAD_DIM, :], raised.astype(bf16))
            outs.append(out / total)
            stats.append(peak * scale + jnp.log2(total))
        att_t_ref[pl.ds(base, pair_width), :] = jnp.concatenate(outs, axis=0).astype(bf16)
        lse_ref[pair] = jnp.concatenate(stats + [jnp.zeros((6, rows), f32)], axis=0)
        return 0

    lax.fori_loop(0, HEADS // 2, attend, 0)
    residual = inputs + dot(att_t_ref[...], out_w_ref[...], TN) + out_bias_ref[...]
    residual_ref[...] = residual
    second = (standardize(residual)[0] * gain2_ref[...] + bias2_ref[...]).astype(bf16)
    second_ref[...] = second
    for o in range(experts):
        x_slots_ref[pl.ds(o * most, most), :] = dot(taken(o), second).astype(bf16)
    logits = dot(second, router_ref[...])
    raised = jnp.exp(logits - jnp.max(logits, axis=-1, keepdims=True))
    probs = raised / jnp.sum(raised, axis=-1, keepdims=True)
    probs_ref[...] = probs
    prob0 = jnp.sum(jnp.where(expert_cols == id0_col, probs, 0.0), axis=1, keepdims=True)
    prob1 = jnp.sum(jnp.where(expert_cols == id1_col, probs, 0.0), axis=1, keepdims=True)
    both = prob0 + prob1
    gate0, gate1 = prob0 / both, prob1 / both
    for far_copy in far:
        far_copy.wait_recv()
    counts[...] = jnp.zeros_like(counts)
    rank_col = cols_ref[:, 0:1]

    def count(block, _):
        entry = table[block // experts, block % experts]
        real = entry[3:4, :] > 0
        hits = jnp.concatenate(
            [
                ones_where((expert_rows == entry[1:2, :]) & real),
                ones_where((expert_rows == entry[2:3, :]) & real),
            ],
            axis=0,
        )
        lower = ones_where(entry[0:1, :] < rank_col)
        counts[:rows, :] += dot(lower, hits, NT)
        counts[rows:, :] += dot(jnp.ones((8, rows), bf16), hits, NT)
        return 0

    lax.fori_loop(0, copies * experts, count, 0)
    both_cols = iota((rows, 2 * experts), 1)
    ahead = counts[:rows, :]
    loads = counts[rows : rows + 1, :]
    position0 = jnp.sum(jnp.where(both_cols == id0_col, ahead, 0.0), axis=1, keepdims=True)
    position1 = jnp.sum(
        jnp.where(both_cols == id1_col + experts, ahead, 0.0)
        + jnp.where(both_cols == id1_col, loads, 0.0),
        axis=1,
        keepdims=True,
    )
    real_col = cols_ref[:, 3:4] > 0
    kept0 = jnp.where(real_col & (position0 < capacity), 1.0, 0.0)
    kept1 = jnp.where(real_col & (position1 < capacity), 1.0, 0.0)
    gate0, gate1 = gate0 * kept0, gate1 * kept1
    for o in range(experts):
        slots = iota((rows, most), 1) + o * most
        gates = jnp.where(slots == slot0_col, gate0, 0.0) + jnp.where(slots == slot1_col, gate1, 0.0)
        gate_slots_ref[o] = jnp.broadcast_to(jnp.sum(gates, axis=0, keepdims=True), (8, most))
    lanes = iota((rows, 8), 1)
    columns = [slot0_col.astype(f32), slot1_col.astype(f32), gate0, gate1, kept0, kept1, both]
    packed = jnp.zeros((rows, 8), f32)
    for i, column in enumerate(columns):
        packed = jnp.where(lanes == i, column, packed)
    pairs_ref[...] = packed
    for copy in near + far:
        copy.wait_send()
    for copy in cots:
        copy.wait()


VMEM = pl.BlockSpec(memory_space=pltpu.VMEM)
HBM = pl.BlockSpec(memory_space=pl.ANY)
DMA = pltpu.SemaphoreType.DMA


def run_front(copies, experts, most, capacity, *operands):
    rows, width = operands[0].shape
    slots = experts * most
    shape = jax.ShapeDtypeStruct
    return pl.pallas_call(
        partial(front_kernel, copies, experts, most, capacity),
        out_shape=(
            shape((slots, width), bf16),
            shape((slots, width), bf16),
            shape((experts, 8, most), f32),
            shape((rows, 3 * width), bf16),
            shape((width, rows), bf16),
            shape((HEADS // 2, 8, rows), f32),
            shape((rows, width), f32),
            shape((rows, width), bf16),
            shape((rows, width), bf16),
            shape((rows, 8), f32),
            shape((rows, experts), f32),
        ),
        in_specs=[VMEM] * 13,
        out_specs=(VMEM,) * 11,
        scratch_shapes=[
            pltpu.VMEM((slots, width), bf16),
            pltpu.VMEM((copies, experts, 8, rows), i32),
            pltpu.VMEM((rows + 8, 2 * experts), f32),
            DMA((experts,)), DMA((experts,)),
            DMA((experts,)), DMA((experts,)),
            DMA((copies,)), DMA((copies,)),
        ],
        compiler_params=pltpu.CompilerParams(
            collective_id=0, has_side_effects=True, vmem_limit_bytes=VMEM_BYTES
        ),
        name="front",
    )(*operands)


def exact_gelu(values):
    return jax.nn.gelu(values, approximate=False)


def normalize(values, gain, shift):
    return standardize(values)[0] * gain + shift


def attend_backward(pieces):
    queries, key_rows, value_rows, key_valid, lse2, d_attended = pieces
    scores = jnp.einsum("qhd,khd->hqk", queries, key_rows, preferred_element_type=f32) * HEAD_DIM ** (-0.5)
    scores = jnp.where(key_valid[None, None, :], scores, -1000000000.0)
    probabilities = jnp.exp2(scores * LOG2E - lse2[:, :, None])
    weights = probabilities.astype(jnp.bfloat16)
    d_values = jnp.einsum("hqk,qhd->khd", weights, d_attended, preferred_element_type=jnp.float32)
    d_weights = jnp.einsum("qhd,khd->hqk", d_attended, value_rows, preferred_element_type=jnp.float32)
    centre = jnp.sum(probabilities * d_weights, axis=-1, keepdims=True)
    d_scores = (probabilities * (d_weights - centre)).astype(jnp.bfloat16)
    scaling = HEAD_DIM ** (-0.5)
    d_queries = jnp.einsum("hqk,khd->qhd", d_scores, key_rows, preferred_element_type=jnp.float32) * scaling
    d_keys = jnp.einsum("hqk,qhd->khd", d_scores, queries, preferred_element_type=jnp.float32) * scaling
    return (d_queries, d_keys, d_values)


def local(
    patches, padding, expert_ids, priority, norm1_gain, norm1_bias, qkv_weight, qv_bias, out_weight,
    out_bias, norm2_gain, norm2_bias, router, expert_in, expert_in_bias, expert_out, expert_out_bias,
    cotangent,
):
    row_count, width = patches.shape
    copies, experts = lax.axis_size("dp"), lax.axis_size("expert")
    total_rows = row_count * copies * experts
    capacity = (210 * total_rows + 100 * experts - 1) // (100 * experts)
    most = 8 * row_count // (3 * experts)
    me = lax.axis_index("expert")
    facts = [priority, expert_ids[:, 0], expert_ids[:, 1], padding]
    facts = facts + [jnp.zeros_like(padding)] * 4
    (recv_cot, x_slots, gate_slots, qkv, att_t, lse, residual, second, first, pairs, probs) = run_front(
        copies, experts, most, capacity,
        patches, cotangent, jnp.stack(facts), jnp.stack(facts, axis=1),
        norm1_gain[None, :], norm1_bias[None, :], qkv_weight, qv_bias[None, :],
        out_weight, out_bias[None, :], norm2_gain[None, :], norm2_bias[None, :], router,
    )
    order = jnp.arange(experts) ^ me

    def exchange(block):
        block = jnp.take(block.reshape(experts, -1, block.shape[-1]), order, axis=0)
        out = lax.all_to_all(block, "expert", split_axis=0, concat_axis=0, tiled=True)
        return jnp.take(out, order, axis=0)

    received = exchange(x_slots).reshape(-1, width)
    gates = exchange(gate_slots[:, :1, :].reshape(experts, most, 1)).reshape(-1, 1)
    w1, w2 = expert_in[0], expert_out[0]
    hidden_pre = jnp.dot(received, w1, preferred_element_type=f32) + expert_in_bias
    hidden = exact_gelu(hidden_pre).astype(bf16)
    produced = (jnp.dot(hidden, w2, preferred_element_type=f32) + expert_out_bias).astype(bf16)
    d_gate_slots = jnp.sum(produced.astype(f32) * recv_cot.astype(f32), axis=-1, keepdims=True)
    d_produced = (gates * recv_cot.astype(f32)).astype(bf16)
    d_hidden = lax.dot_general(d_produced, w2, NT, preferred_element_type=f32)
    gelu_value, gelu_pull = jax.vjp(exact_gelu, hidden_pre)
    d_pre = gelu_pull(d_hidden)[0].astype(jnp.bfloat16)
    d_rows = lax.dot_general(d_pre, w1, NT, preferred_element_type=f32).astype(bf16)
    g1 = lax.dot_general(received, d_pre, TN, preferred_element_type=f32)
    gb1 = jnp.sum(d_pre.astype(f32), axis=0)
    g2 = lax.dot_general(hidden, d_produced, TN, preferred_element_type=f32)
    gb2 = jnp.sum(d_produced.astype(f32), axis=0)
    scatter = lambda v, d: lax.psum_scatter(v.astype(bf16), "dp", scatter_dimension=d, tiled=True).astype(f32)[None]
    grad_expert_in, grad_expert_in_bias = scatter(g1, 1), scatter(gb1, 0)
    grad_expert_out, grad_expert_out_bias = scatter(g2, 0), scatter(gb2, 0)
    ret_produced = exchange(produced).reshape(-1, width)
    ret_rows = exchange(d_rows).reshape(-1, width)
    ret_gate = exchange(d_gate_slots).reshape(-1, 1)
    slot = pairs[:, :2].astype(i32)
    gk, kept, both = pairs[:, 2:4], pairs[:, 4:6], pairs[:, 6:7]
    chosen = jnp.take(ret_produced, slot.reshape(-1), axis=0).reshape(row_count, 2, width).astype(f32)
    output = (residual + jnp.sum(gk[:, :, None] * chosen, axis=1)).astype(bf16)
    d_gate = jnp.take(ret_gate[:, 0], slot.reshape(-1), axis=0).reshape(row_count, 2) * kept
    matches = expert_ids[:, :, None] == jnp.arange(experts)[None, None, :]
    picked = jnp.sum(jnp.where(matches, probs[:, None, :], 0.0), axis=-1)
    gate = picked / both
    d_picked = (d_gate - jnp.sum(d_gate * gate, axis=1, keepdims=True)) / both
    d_probs = jnp.sum(jnp.where(matches, d_picked[:, :, None], 0.0), axis=1)
    d_logits = (probs * (d_probs - jnp.sum(probs * d_probs, axis=1, keepdims=True))).astype(bf16)
    grad_router = jnp.dot(second.T, d_logits, preferred_element_type=jnp.float32)
    d_pairs = jnp.take(ret_rows, slot.reshape(-1), axis=0).reshape(row_count, 2, width).astype(f32)
    d_second = jnp.sum(d_pairs * kept[:, :, None], axis=1) + jnp.dot(d_logits, router.T, preferred_element_type=f32)
    second_value, second_pull = jax.vjp(normalize, residual, norm2_gain, norm2_bias)
    d_residual_norm, grad_norm2_gain, grad_norm2_bias = second_pull(d_second)
    d_residual = cotangent.astype(f32) + d_residual_norm
    d_branch = d_residual.astype(jnp.bfloat16)
    grad_out_weight = jnp.dot(att_t, d_branch, preferred_element_type=jnp.float32)
    grad_out_bias = jnp.sum(d_branch.astype(jnp.float32), axis=0)
    d_att = jnp.dot(d_branch, out_weight.T, preferred_element_type=jnp.float32).astype(bf16)
    d_att = d_att.reshape(SEQ_LEN, HEADS, HEAD_DIM)
    heads = qkv.reshape(SEQ_LEN, 3, HEADS, HEAD_DIM)
    lse2 = lse[:, :2].reshape(HEADS, row_count)
    d_q, d_k, d_v = attend_backward((heads[:, 0], heads[:, 1], heads[:, 2], padding > 0, lse2, d_att))
    d_projected = jnp.stack([d_q, d_k, d_v], axis=1).reshape(row_count, 3 * width).astype(bf16)
    grad_qkv_weight = jnp.dot(first.T, d_projected, preferred_element_type=jnp.float32)
    column_sums = jnp.sum(d_projected.astype(jnp.float32), axis=0)
    grad_qv_bias = jnp.concatenate([column_sums[:width], column_sums[2 * width :]])
    d_first = jnp.dot(d_projected, qkv_weight.T, preferred_element_type=jnp.float32)
    first_value, first_pull = jax.vjp(normalize, patches.astype(f32), norm1_gain, norm1_bias)
    d_inputs, grad_norm1_gain, grad_norm1_bias = first_pull(d_first)
    grad_patches = (d_residual + d_inputs).astype(jnp.bfloat16)
    dense = [grad_norm1_gain, grad_norm1_bias, grad_qkv_weight, grad_qv_bias, grad_out_weight, grad_out_bias,
             grad_norm2_gain, grad_norm2_bias, grad_router]
    dense = [lax.psum_scatter(g.astype(bf16), "expert", scatter_dimension=0, tiled=True) for g in dense]
    dense = [lax.psum(g, "dp").astype(f32) for g in dense]
    return (output, grad_patches, *dense, grad_expert_in, grad_expert_in_bias, grad_expert_out, grad_expert_out_bias)


def solution(mesh):
    tokens = P(("dp", "expert"))
    wide = P(("dp", "expert"), None)
    return jax.shard_map(
        local,
        mesh=mesh,
        in_specs=(
            wide, tokens, wide, tokens, P(), P(), P(), P(), P(), P(), P(), P(), P(),
            P("expert", None, None), P("expert", None), P("expert", None, None), P("expert", None), wide,
        ),
        out_specs=(
            wide, wide, P("expert"), P("expert"), P("expert", None), P("expert"), P("expert", None),
            P("expert"), P("expert"), P("expert"), P("expert", None), P("expert", None, "dp"),
            P("expert", "dp"), P("expert", "dp", None), P("expert", "dp"),
        ),
        check_vma=False,
    )
```

```python
from functools import partial

import jax
import jax.numpy as jnp
from jax import lax
from jax.experimental import pallas as pl
from jax.experimental.pallas import tpu as pltpu
from jax.sharding import PartitionSpec as P

HEADS = 12
HEAD_DIM = 64
SEQ_LEN = 576
LOG2E = 1.4426950408889634
EPS = 1e-06
MESH = pl.DeviceIdType.MESH
NN = (((1,), (0,)), ((), ()))
NT = (((1,), (1,)), ((), ()))
TN = (((0,), (0,)), ((), ()))
VMEM_BYTES = 60 << 20
bf16 = jnp.bfloat16
f32 = jnp.float32
i32 = jnp.int32


def dot(a, b, dims=NN):
    return lax.dot_general(a, b, dims, preferred_element_type=f32)


def iota(shape, axis):
    return lax.broadcasted_iota(i32, shape, axis)


def ones_where(mask):
    return jnp.where(mask, 1.0, 0.0).astype(bf16)


def standardize(values):
    centred = values - jnp.mean(values, axis=-1, keepdims=True)
    inverse = lax.rsqrt(jnp.mean(centred * centred, axis=-1, keepdims=True) + EPS)
    return centred * inverse, inverse


def greet(peers):
    barrier = pltpu.get_barrier_semaphore()
    for peer in peers:
        pl.semaphore_signal(barrier, inc=1, device_id=peer, device_id_type=MESH)
    pl.semaphore_wait(barrier, len(peers))


def send(src, dst, send_sem, recv_sem, peer):
    copy = pltpu.make_async_remote_copy(
        src_ref=src, dst_ref=dst, send_sem=send_sem, recv_sem=recv_sem,
        device_id=peer, device_id_type=MESH,
    )
    copy.start()
    return copy


def front_kernel(
    copies, experts, most, capacity,
    patches_ref, cot_ref, rows_ref, cols_ref, gain1_ref, bias1_ref, qkv_w_ref, qv_bias_ref,
    out_w_ref, out_bias_ref, gain2_ref, bias2_ref, router_ref,
    recv_cot_ref, x_slots_ref, gate_slots_ref, qkv_ref, att_t_ref, lse_ref, residual_ref,
    second_ref, first_ref, pairs_ref, probs_ref,
    cot_send, table, counts, cot_ss, cot_rs, near_ss, near_rs, far_ss, far_rs,
):
    me_dp = lax.axis_index("dp")
    me = lax.axis_index("expert")
    rows, width = patches_ref.shape
    greet(
        [(me_dp, me ^ o) for o in range(1, experts)]
        + [(me_dp ^ p, me) for p in range(1, copies)]
    )
    near = [
        send(rows_ref, table.at[0, o], near_ss.at[o], near_rs.at[o], (me_dp, me ^ o))
        for o in range(1, experts)
    ]
    table[0, 0] = rows_ref[...]
    id0_row, id1_row = rows_ref[1:2, :] ^ me, rows_ref[2:3, :] ^ me
    expert_rows = iota((experts, rows), 0)
    named_t = ones_where((expert_rows == id0_row) | (expert_rows == id1_row))
    before_t = ones_where(iota((rows, rows), 0) < iota((rows, rows), 1))
    place_t = dot(named_t, before_t).astype(i32) + expert_rows * most
    slot0_row = jnp.sum(jnp.where(expert_rows == id0_row, place_t, 0), axis=0, keepdims=True)
    slot1_row = jnp.sum(jnp.where(expert_rows == id1_row, place_t, 0), axis=0, keepdims=True)
    id0_col, id1_col = cols_ref[:, 1:2], cols_ref[:, 2:3]
    rel0_col, rel1_col = id0_col ^ me, id1_col ^ me
    expert_cols = iota((rows, experts), 1)
    named = ones_where((expert_cols == rel0_col) | (expert_cols == rel1_col))
    before = ones_where(iota((rows, rows), 1) < iota((rows, rows), 0))
    place = dot(before, named).astype(i32) + expert_cols * most
    slot0_col = jnp.sum(jnp.where(expert_cols == rel0_col, place, 0), axis=1, keepdims=True)
    slot1_col = jnp.sum(jnp.where(expert_cols == rel1_col, place, 0), axis=1, keepdims=True)

    def taken(o):
        slots = iota((most, rows), 0) + o * most
        return ones_where((slots == slot0_row) | (slots == slot1_row))

    cot_value = cot_ref[...]
    cots = []
    for o in [*range(1, experts), 0]:
        picked = dot(taken(o), cot_value).astype(bf16)
        if o == 0:
            recv_cot_ref[0:most, :] = picked
            continue
        part = pl.ds(o * most, most)
        cot_send[part, :] = picked
        cots.append(
            send(cot_send.at[part], recv_cot_ref.at[part], cot_ss.at[o], cot_rs.at[o], (me_dp, me ^ o))
        )
    inputs = patches_ref[...].astype(f32)
    first = (standardize(inputs)[0] * gain1_ref[...] + bias1_ref[...]).astype(bf16)
    first_ref[...] = first
    qkv_ref[:, :width] = (dot(first, qkv_w_ref[:, :width]) + qv_bias_ref[:, :width]).astype(bf16)
    qkv_ref[:, width : 2 * width] = dot(first, qkv_w_ref[:, width : 2 * width]).astype(bf16)
    qkv_ref[:, 2 * width :] = (
        dot(first, qkv_w_ref[:, 2 * width :]) + qv_bias_ref[:, width:]
    ).astype(bf16)
    key_bias = jnp.where(cols_ref[:, 3:4] > 0, 0.0, -1e30)
    scale = LOG2E * HEAD_DIM ** (-0.5)
    pair_width = 2 * HEAD_DIM

    for near_copy in near:
        near_copy.wait_recv()
    far = [
        send(table.at[0], table.at[p], far_ss.at[p], far_rs.at[p], (me_dp ^ p, me))
        for p in range(1, copies)
    ]

    def attend(pair, _):
        base = pl.multiple_of(pair * pair_width, pair_width)
        q = qkv_ref[:, pl.ds(base, pair_width)]
        k = qkv_ref[:, pl.ds(base + width, pair_width)]
        v_t = qkv_ref[:, pl.ds(base + 2 * width, pair_width)].T
        lanes = iota((rows, pair_width), 1)
        outs, stats = [], []
        for a in range(2):
            k_a = jnp.where((lanes >= HEAD_DIM) == (a == 1), k, jnp.zeros((), bf16))
            scores = dot(k_a, q, NT) + key_bias
            peak = jnp.max(scores, axis=0, keepdims=True)
            raised = jnp.exp2(scores * scale - peak * scale)
            total = jnp.sum(raised, axis=0, keepdims=True)
            out = dot(v_t[a * HEAD_DIM : (a + 1) * HEAD_DIM, :], raised.astype(bf16))
            outs.append(out / total)
            stats.append(peak * scale + jnp.log2(total))
        att_t_ref[pl.ds(base, pair_width), :] = jnp.concatenate(outs, axis=0).astype(bf16)
        lse_ref[pair] = jnp.concatenate(stats + [jnp.zeros((6, rows), f32)], axis=0)
        return 0

    lax.fori_loop(0, HEADS // 2, attend, 0)
    residual = inputs + dot(att_t_ref[...], out_w_ref[...], TN) + out_bias_ref[...]
    residual_ref[...] = residual
    second = (standardize(residual)[0] * gain2_ref[...] + bias2_ref[...]).astype(bf16)
    second_ref[...] = second
    for o in range(experts):
        x_slots_ref[pl.ds(o * most, most), :] = dot(taken(o), second).astype(bf16)
    logits = dot(second, router_ref[...])
    raised = jnp.exp(logits - jnp.max(logits, axis=-1, keepdims=True))
    probs = raised / jnp.sum(raised, axis=-1, keepdims=True)
    probs_ref[...] = probs
    prob0 = jnp.sum(jnp.where(expert_cols == id0_col, probs, 0.0), axis=1, keepdims=True)
    prob1 = jnp.sum(jnp.where(expert_cols == id1_col, probs, 0.0), axis=1, keepdims=True)
    both = prob0 + prob1
    gate0, gate1 = prob0 / both, prob1 / both
    for far_copy in far:
        far_copy.wait_recv()
    counts[...] = jnp.zeros_like(counts)
    rank_col = cols_ref[:, 0:1]

    def count(block, _):
        entry = table[block // experts, block % experts]
        real = entry[3:4, :] > 0
        hits = jnp.concatenate(
            [
                ones_where((expert_rows == entry[1:2, :]) & real),
                ones_where((expert_rows == entry[2:3, :]) & real),
            ],
            axis=0,
        )
        lower = ones_where(entry[0:1, :] < rank_col)
        counts[:rows, :] += dot(lower, hits, NT)
        counts[rows:, :] += dot(jnp.ones((8, rows), bf16), hits, NT)
        return 0

    lax.fori_loop(0, copies * experts, count, 0)
    both_cols = iota((rows, 2 * experts), 1)
    ahead = counts[:rows, :]
    loads = counts[rows : rows + 1, :]
    position0 = jnp.sum(jnp.where(both_cols == id0_col, ahead, 0.0), axis=1, keepdims=True)
    position1 = jnp.sum(
        jnp.where(both_cols == id1_col + experts, ahead, 0.0)
        + jnp.where(both_cols == id1_col, loads, 0.0),
        axis=1,
        keepdims=True,
    )
    real_col = cols_ref[:, 3:4] > 0
    kept0 = jnp.where(real_col & (position0 < capacity), 1.0, 0.0)
    kept1 = jnp.where(real_col & (position1 < capacity), 1.0, 0.0)
    gate0, gate1 = gate0 * kept0, gate1 * kept1
    for o in range(experts):
        slots = iota((rows, most), 1) + o * most
        gates = jnp.where(slots == slot0_col, gate0, 0.0) + jnp.where(slots == slot1_col, gate1, 0.0)
        gate_slots_ref[o] = jnp.broadcast_to(jnp.sum(gates, axis=0, keepdims=True), (8, most))
    lanes = iota((rows, 8), 1)
    columns = [slot0_col.astype(f32), slot1_col.astype(f32), gate0, gate1, kept0, kept1, both]
    packed = jnp.zeros((rows, 8), f32)
    for i, column in enumerate(columns):
        packed = jnp.where(lanes == i, column, packed)
    pairs_ref[...] = packed
    for copy in near + far:
        copy.wait_send()
    for copy in cots:
        copy.wait()


VMEM = pl.BlockSpec(memory_space=pltpu.VMEM)
HBM = pl.BlockSpec(memory_space=pl.ANY)
DMA = pltpu.SemaphoreType.DMA


def run_front(copies, experts, most, capacity, *operands):
    rows, width = operands[0].shape
    slots = experts * most
    shape = jax.ShapeDtypeStruct
    return pl.pallas_call(
        partial(front_kernel, copies, experts, most, capacity),
        out_shape=(
            shape((slots, width), bf16),
            shape((slots, width), bf16),
            shape((experts, 8, most), f32),
            shape((rows, 3 * width), bf16),
            shape((width, rows), bf16),
            shape((HEADS // 2, 8, rows), f32),
            shape((rows, width), f32),
            shape((rows, width), bf16),
            shape((rows, width), bf16),
            shape((rows, 8), f32),
            shape((rows, experts), f32),
        ),
        in_specs=[VMEM] * 13,
        out_specs=(VMEM,) * 11,
        scratch_shapes=[
            pltpu.VMEM((slots, width), bf16),
            pltpu.VMEM((copies, experts, 8, rows), i32),
            pltpu.VMEM((rows + 8, 2 * experts), f32),
            DMA((experts,)), DMA((experts,)),
            DMA((experts,)), DMA((experts,)),
            DMA((copies,)), DMA((copies,)),
        ],
        compiler_params=pltpu.CompilerParams(
            collective_id=0, has_side_effects=True, vmem_limit_bytes=VMEM_BYTES
        ),
        name="front",
    )(*operands)


def gelu_parts(values):
    bell = jnp.exp2(values * values * (-0.5 * LOG2E))
    t = 1.0 / (1.0 + (0.3275911 * 0.5**0.5) * jnp.abs(values))
    tail = t * (0.1274147959 + t * (-0.142248368 + t * (0.7107068705 + t * (-0.7265760135 + t * 0.5307027145))))
    tail = tail * bell
    share = jnp.where(values >= 0, 1.0 - tail, tail)
    return values * share, share + values * bell * 0.3989422804014327


def to_column(row):
    n = row.shape[1]
    return jnp.sum(jnp.where(iota((n, n), 0) == iota((n, n), 1), row, 0.0), axis=1, keepdims=True)


def to_row(column):
    n = column.shape[0]
    return jnp.sum(jnp.where(iota((n, n), 0) == iota((n, n), 1), column, 0.0), axis=0, keepdims=True)


def expert_kernel(
    copies, experts, most, chunks, tile,
    x_ref, gates_ref, cot_ref, in_w_ref, in_bias_ref, out_w_ref, out_bias_ref,
    d_rows_ref, d_gates_ref, produced_ref, grads_ref,
    recv_x, recv_g, send_d, send_g, hidden, d_pre, x_t, d_t, bias_sum, total_p, total_d, stage,
    x_ss, x_rs, g_ss, g_rs, d_ss, d_rs, dg_ss, dg_rs, own_sem, own_d_sem, stage_sem,
):
    me_dp = lax.axis_index("dp")
    me = lax.axis_index("expert")
    width, hidden_width = in_w_ref.shape
    rows = chunks * most
    block = hidden_width // copies

    def chunk(o):
        return pl.ds(pl.multiple_of(o * most, most), most)

    def move_x(o):
        return pltpu.make_async_remote_copy(
            x_ref.at[chunk(o)], recv_x.at[chunk(o)], x_ss.at[o], x_rs.at[o], (me_dp, me ^ o), MESH
        )

    def move_g(o):
        return pltpu.make_async_remote_copy(
            gates_ref.at[o], recv_g.at[o], g_ss.at[o], g_rs.at[o], (me_dp, me ^ o), MESH
        )

    def move_d(o):
        return pltpu.make_async_remote_copy(
            send_d.at[chunk(o)], d_rows_ref.at[chunk(o)], d_ss.at[o], d_rs.at[o], (me_dp, me ^ o), MESH
        )

    def move_dg(o):
        return pltpu.make_async_remote_copy(
            send_g.at[o], d_gates_ref.at[o], dg_ss.at[o], dg_rs.at[o], (me_dp, me ^ o), MESH
        )

    own = pltpu.make_async_copy(x_ref.at[chunk(0)], recv_x.at[chunk(0)], own_sem)
    own.start()
    greet([(me_dp, me ^ o) for o in range(1, experts)])
    for o in range(1, experts):
        move_g(o).start()
        move_x(o).start()
    recv_g[0] = gates_ref[0]
    bias_sum[...] = jnp.zeros_like(bias_sum)
    x_t[width:, :] = jnp.ones_like(x_t[width:, :])
    own.wait()
    own_d = pltpu.make_async_copy(send_d.at[chunk(0)], d_rows_ref.at[chunk(0)], own_d_sem)

    def work(g, _):
        for j in range(chunks):
            o = g * chunks + j

            @pl.when(o > 0)
            def _():
                move_g(o).wait_recv()
                move_x(o).wait_recv()

        at = pl.multiple_of(g * rows, rows)
        here = pl.ds(at, rows)
        gate = jnp.concatenate([to_column(recv_g[g * chunks + j][0:1, :]) for j in range(chunks)], axis=0)
        x = recv_x[here, :]
        cot = cot_ref[here, :].astype(f32)
        d_produced = (cot * gate).astype(bf16)
        bias_sum[0:1, :] += jnp.sum(d_produced.astype(f32), axis=0, keepdims=True)
        x_t[:width, here] = x.T
        d_t[:, here] = d_produced.T
        total_p[...] = jnp.zeros_like(total_p)
        total_d[...] = jnp.zeros_like(total_d)

        def step(n, _):
            cols = pl.ds(pl.multiple_of(n * tile, tile), tile)
            pre = dot(x, in_w_ref[:, cols]) + in_bias_ref[:, cols]
            value, slope = gelu_parts(pre)
            value = value.astype(bf16)
            hidden[here, cols] = value
            total_p[...] += dot(value, out_w_ref[cols, :])
            d_value = (dot(d_produced, out_w_ref[cols, :], NT) * slope).astype(bf16)
            d_pre[here, cols] = d_value
            total_d[...] += dot(d_value, in_w_ref[:, cols], NT)
            return 0

        lax.fori_loop(0, hidden_width // tile, step, 0)
        send_d[here, :] = total_d[...].astype(bf16)
        produced = (total_p[...] + out_bias_ref[...]).astype(bf16)
        produced_ref[here, :] = produced
        d_gate = jnp.sum(produced.astype(f32) * cot, axis=1, keepdims=True)
        for j in range(chunks):
            o = g * chunks + j
            d_gate_row = jnp.broadcast_to(to_row(d_gate[j * most : (j + 1) * most, :]), (8, most))
            send_g[o] = d_gate_row

            @pl.when(o > 0)
            def _():
                move_d(o).start()
                move_dg(o).start()

            @pl.when(o == 0)
            def _():
                own_d.start()
                d_gates_ref[0] = d_gate_row

        return 0

    lax.fori_loop(0, experts // chunks, work, 0)

    def store(w, p):
        return pltpu.make_async_copy(stage.at[w], grads_ref.at[w, p], stage_sem.at[w])

    def weigh(p, _):
        cols = pl.ds(pl.multiple_of((me_dp ^ p) * block, block), block)

        @pl.when(p > 0)
        def _():
            store(0, p - 1).wait()

        total = dot(x_t[...], d_pre[:, cols])
        stage[0, :width, :] = total[:width, :].astype(bf16)
        tail = total[width:, :]
        lines = iota((16, block), 0)
        for i in range(-(-width // block)):
            tail = jnp.where(lines == 8 + i, bias_sum[0:1, i * block : (i + 1) * block], tail)
        stage[0, width:, :] = tail.astype(bf16)
        store(0, p).start()

        @pl.when(p > 0)
        def _():
            store(1, p - 1).wait()

        stage[1, :width, :] = dot(d_t[...], hidden[:, cols]).astype(bf16)
        stage[1, width:, :] = jnp.zeros((16, block), bf16)
        store(1, p).start()
        return 0

    lax.fori_loop(0, copies, weigh, 0)
    store(0, copies - 1).wait()
    store(1, copies - 1).wait()
    own_d.wait()
    for o in range(1, experts):
        move_g(o).wait_send()
        move_x(o).wait_send()
        move_d(o).wait()
        move_dg(o).wait()


def run_experts(copies, experts, most, *operands):
    slots, width = operands[0].shape
    hidden_width = operands[3].shape[1]
    chunks = max(1, min(experts, 384 // most))
    rows = chunks * most
    block = hidden_width // copies
    shape = jax.ShapeDtypeStruct
    return pl.pallas_call(
        partial(expert_kernel, copies, experts, most, chunks, 512),
        out_shape=(
            shape((slots, width), bf16),
            shape((experts, 8, most), f32),
            shape((slots, width), bf16),
            shape((2, copies, width + 16, block), bf16),
        ),
        in_specs=[HBM] + [VMEM] * 6,
        out_specs=(HBM, VMEM, VMEM, HBM),
        scratch_shapes=[
            pltpu.VMEM((slots, width), bf16),
            pltpu.VMEM((experts, 8, most), f32),
            pltpu.VMEM((slots, width), bf16),
            pltpu.VMEM((experts, 8, most), f32),
            pltpu.VMEM((slots, hidden_width), bf16),
            pltpu.VMEM((slots, hidden_width), bf16),
            pltpu.VMEM((width + 16, slots), bf16),
            pltpu.VMEM((width, slots), bf16),
            pltpu.VMEM((8, width), f32),
            pltpu.VMEM((rows, width), f32),
            pltpu.VMEM((rows, width), f32),
            pltpu.VMEM((2, width + 16, block), bf16),
        ]
        + [DMA((experts,))] * 8
        + [DMA(()), DMA(()), DMA((2,))],
        compiler_params=pltpu.CompilerParams(
            collective_id=1, has_side_effects=True, vmem_limit_bytes=VMEM_BYTES
        ),
        name="experts",
    )(*operands)


def exact_gelu(values):
    return jax.nn.gelu(values, approximate=False)


def normalize(values, gain, shift):
    return standardize(values)[0] * gain + shift


def attend_backward(pieces):
    queries, key_rows, value_rows, key_valid, lse2, d_attended = pieces
    scores = jnp.einsum("qhd,khd->hqk", queries, key_rows, preferred_element_type=f32) * HEAD_DIM ** (-0.5)
    scores = jnp.where(key_valid[None, None, :], scores, -1000000000.0)
    probabilities = jnp.exp2(scores * LOG2E - lse2[:, :, None])
    weights = probabilities.astype(jnp.bfloat16)
    d_values = jnp.einsum("hqk,qhd->khd", weights, d_attended, preferred_element_type=jnp.float32)
    d_weights = jnp.einsum("qhd,khd->hqk", d_attended, value_rows, preferred_element_type=jnp.float32)
    centre = jnp.sum(probabilities * d_weights, axis=-1, keepdims=True)
    d_scores = (probabilities * (d_weights - centre)).astype(jnp.bfloat16)
    scaling = HEAD_DIM ** (-0.5)
    d_queries = jnp.einsum("hqk,khd->qhd", d_scores, key_rows, preferred_element_type=jnp.float32) * scaling
    d_keys = jnp.einsum("hqk,qhd->khd", d_scores, queries, preferred_element_type=jnp.float32) * scaling
    return (d_queries, d_keys, d_values)


def local(
    patches, padding, expert_ids, priority, norm1_gain, norm1_bias, qkv_weight, qv_bias, out_weight,
    out_bias, norm2_gain, norm2_bias, router, expert_in, expert_in_bias, expert_out, expert_out_bias,
    cotangent,
):
    row_count, width = patches.shape
    copies, experts = lax.axis_size("dp"), lax.axis_size("expert")
    total_rows = row_count * copies * experts
    capacity = (210 * total_rows + 100 * experts - 1) // (100 * experts)
    most = 8 * row_count // (3 * experts)
    me = lax.axis_index("expert")
    facts = [priority, expert_ids[:, 0], expert_ids[:, 1], padding]
    facts = facts + [jnp.zeros_like(padding)] * 4
    (recv_cot, x_slots, gate_slots, qkv, att_t, lse, residual, second, first, pairs, probs) = run_front(
        copies, experts, most, capacity,
        patches, cotangent, jnp.stack(facts), jnp.stack(facts, axis=1),
        norm1_gain[None, :], norm1_bias[None, :], qkv_weight, qv_bias[None, :],
        out_weight, out_bias[None, :], norm2_gain[None, :], norm2_bias[None, :], router,
    )
    order = jnp.arange(experts) ^ me

    def exchange(block):
        block = jnp.take(block.reshape(experts, -1, block.shape[-1]), order, axis=0)
        out = lax.all_to_all(block, "expert", split_axis=0, concat_axis=0, tiled=True)
        return jnp.take(out, order, axis=0)

    ret_rows, ret_gate, produced, grads = run_experts(
        copies, experts, most,
        x_slots, gate_slots, recv_cot, expert_in[0], expert_in_bias, expert_out[0], expert_out_bias,
    )
    me_dp = lax.axis_index("dp")
    grads = jnp.take(grads, jnp.arange(copies) ^ me_dp, axis=1)
    block = grads.shape[-1]
    g1 = grads[0].transpose(1, 0, 2).reshape(width + 16, -1)
    g2 = grads[1].transpose(1, 0, 2).reshape(width + 16, -1)
    g1 = lax.psum_scatter(g1, "dp", scatter_dimension=1, tiled=True).astype(f32)
    g2 = lax.psum_scatter(g2, "dp", scatter_dimension=1, tiled=True).astype(f32)
    grad_expert_in, grad_expert_in_bias = g1[:width][None], g1[width][None]
    grad_expert_out = g2[:width].T[None]
    gb2 = g1[width + 8 :].reshape(-1)[:width]
    grad_expert_out_bias = lax.dynamic_slice(gb2, (me_dp * (width // copies),), (width // copies,))[None]
    ret_produced = exchange(produced).reshape(-1, width)
    ret_gate = ret_gate[:, 0].reshape(-1, 1)
    slot = pairs[:, :2].astype(i32)
    gk, kept, both = pairs[:, 2:4], pairs[:, 4:6], pairs[:, 6:7]
    chosen = jnp.take(ret_produced, slot.reshape(-1), axis=0).reshape(row_count, 2, width).astype(f32)
    output = (residual + jnp.sum(gk[:, :, None] * chosen, axis=1)).astype(bf16)
    d_gate = jnp.take(ret_gate[:, 0], slot.reshape(-1), axis=0).reshape(row_count, 2) * kept
    matches = expert_ids[:, :, None] == jnp.arange(experts)[None, None, :]
    picked = jnp.sum(jnp.where(matches, probs[:, None, :], 0.0), axis=-1)
    gate = picked / both
    d_picked = (d_gate - jnp.sum(d_gate * gate, axis=1, keepdims=True)) / both
    d_probs = jnp.sum(jnp.where(matches, d_picked[:, :, None], 0.0), axis=1)
    d_logits = (probs * (d_probs - jnp.sum(probs * d_probs, axis=1, keepdims=True))).astype(bf16)
    grad_router = jnp.dot(second.T, d_logits, preferred_element_type=jnp.float32)
    d_pairs = jnp.take(ret_rows, slot.reshape(-1), axis=0).reshape(row_count, 2, width).astype(f32)
    d_second = jnp.sum(d_pairs * kept[:, :, None], axis=1) + jnp.dot(d_logits, router.T, preferred_element_type=f32)
    second_value, second_pull = jax.vjp(normalize, residual, norm2_gain, norm2_bias)
    d_residual_norm, grad_norm2_gain, grad_norm2_bias = second_pull(d_second)
    d_residual = cotangent.astype(f32) + d_residual_norm
    d_branch = d_residual.astype(jnp.bfloat16)
    grad_out_weight = jnp.dot(att_t, d_branch, preferred_element_type=jnp.float32)
    grad_out_bias = jnp.sum(d_branch.astype(jnp.float32), axis=0)
    d_att = jnp.dot(d_branch, out_weight.T, preferred_element_type=jnp.float32).astype(bf16)
    d_att = d_att.reshape(SEQ_LEN, HEADS, HEAD_DIM)
    heads = qkv.reshape(SEQ_LEN, 3, HEADS, HEAD_DIM)
    lse2 = lse[:, :2].reshape(HEADS, row_count)
    d_q, d_k, d_v = attend_backward((heads[:, 0], heads[:, 1], heads[:, 2], padding > 0, lse2, d_att))
    d_projected = jnp.stack([d_q, d_k, d_v], axis=1).reshape(row_count, 3 * width).astype(bf16)
    grad_qkv_weight = jnp.dot(first.T, d_projected, preferred_element_type=jnp.float32)
    column_sums = jnp.sum(d_projected.astype(jnp.float32), axis=0)
    grad_qv_bias = jnp.concatenate([column_sums[:width], column_sums[2 * width :]])
    d_first = jnp.dot(d_projected, qkv_weight.T, preferred_element_type=jnp.float32)
    first_value, first_pull = jax.vjp(normalize, patches.astype(f32), norm1_gain, norm1_bias)
    d_inputs, grad_norm1_gain, grad_norm1_bias = first_pull(d_first)
    grad_patches = (d_residual + d_inputs).astype(jnp.bfloat16)
    dense = [grad_norm1_gain, grad_norm1_bias, grad_qkv_weight, grad_qv_bias, grad_out_weight, grad_out_bias,
             grad_norm2_gain, grad_norm2_bias, grad_router]
    dense = [lax.psum_scatter(g.astype(bf16), "expert", scatter_dimension=0, tiled=True) for g in dense]
    dense = [lax.psum(g, "dp").astype(f32) for g in dense]
    return (output, grad_patches, *dense, grad_expert_in, grad_expert_in_bias, grad_expert_out, grad_expert_out_bias)


def solution(mesh):
    tokens = P(("dp", "expert"))
    wide = P(("dp", "expert"), None)
    return jax.shard_map(
        local,
        mesh=mesh,
        in_specs=(
            wide, tokens, wide, tokens, P(), P(), P(), P(), P(), P(), P(), P(), P(),
            P("expert", None, None), P("expert", None), P("expert", None, None), P("expert", None), wide,
        ),
        out_specs=(
            wide, wide, P("expert"), P("expert"), P("expert", None), P("expert"), P("expert", None),
            P("expert"), P("expert"), P("expert"), P("expert", None), P("expert", None, "dp"),
            P("expert", "dp"), P("expert", "dp", None), P("expert", "dp"),
        ),
        check_vma=False,
    )
```

```python
from functools import partial

import jax
import jax.numpy as jnp
from jax import lax
from jax.experimental import pallas as pl
from jax.experimental.pallas import tpu as pltpu
from jax.sharding import PartitionSpec as P

HEADS = 12
HEAD_DIM = 64
SEQ_LEN = 576
LOG2E = 1.4426950408889634
EPS = 1e-06
MESH = pl.DeviceIdType.MESH
NN = (((1,), (0,)), ((), ()))
NT = (((1,), (1,)), ((), ()))
TN = (((0,), (0,)), ((), ()))
VMEM_BYTES = 60 << 20
bf16 = jnp.bfloat16
f32 = jnp.float32
i32 = jnp.int32


def dot(a, b, dims=NN):
    return lax.dot_general(a, b, dims, preferred_element_type=f32)


def iota(shape, axis):
    return lax.broadcasted_iota(i32, shape, axis)


def ones_where(mask):
    return jnp.where(mask, 1.0, 0.0).astype(bf16)


def standardize(values):
    centred = values - jnp.mean(values, axis=-1, keepdims=True)
    inverse = lax.rsqrt(jnp.mean(centred * centred, axis=-1, keepdims=True) + EPS)
    return centred * inverse, inverse


def greet(peers):
    barrier = pltpu.get_barrier_semaphore()
    for peer in peers:
        pl.semaphore_signal(barrier, inc=1, device_id=peer, device_id_type=MESH)
    pl.semaphore_wait(barrier, len(peers))


def send(src, dst, send_sem, recv_sem, peer):
    copy = pltpu.make_async_remote_copy(
        src_ref=src, dst_ref=dst, send_sem=send_sem, recv_sem=recv_sem,
        device_id=peer, device_id_type=MESH,
    )
    copy.start()
    return copy


def front_kernel(
    copies, experts, most, capacity,
    patches_ref, cot_ref, rows_ref, cols_ref, gain1_ref, bias1_ref, qkv_w_ref, qv_bias_ref,
    out_w_ref, out_bias_ref, gain2_ref, bias2_ref, router_ref,
    recv_cot_ref, x_slots_ref, gate_slots_ref, qkv_ref, att_t_ref, lse_ref, residual_ref,
    second_ref, first_ref, pairs_ref, probs_ref,
    cot_send, table, counts, cot_ss, cot_rs, near_ss, near_rs, far_ss, far_rs,
):
    me_dp = lax.axis_index("dp")
    me = lax.axis_index("expert")
    rows, width = patches_ref.shape
    greet(
        [(me_dp, me ^ o) for o in range(1, experts)]
        + [(me_dp ^ p, me) for p in range(1, copies)]
    )
    near = [
        send(rows_ref, table.at[0, o], near_ss.at[o], near_rs.at[o], (me_dp, me ^ o))
        for o in range(1, experts)
    ]
    table[0, 0] = rows_ref[...]
    id0_row, id1_row = rows_ref[1:2, :] ^ me, rows_ref[2:3, :] ^ me
    expert_rows = iota((experts, rows), 0)
    named_t = ones_where((expert_rows == id0_row) | (expert_rows == id1_row))
    before_t = ones_where(iota((rows, rows), 0) < iota((rows, rows), 1))
    place_t = dot(named_t, before_t).astype(i32) + expert_rows * most
    slot0_row = jnp.sum(jnp.where(expert_rows == id0_row, place_t, 0), axis=0, keepdims=True)
    slot1_row = jnp.sum(jnp.where(expert_rows == id1_row, place_t, 0), axis=0, keepdims=True)
    id0_col, id1_col = cols_ref[:, 1:2], cols_ref[:, 2:3]
    rel0_col, rel1_col = id0_col ^ me, id1_col ^ me
    expert_cols = iota((rows, experts), 1)
    named = ones_where((expert_cols == rel0_col) | (expert_cols == rel1_col))
    before = ones_where(iota((rows, rows), 1) < iota((rows, rows), 0))
    place = dot(before, named).astype(i32) + expert_cols * most
    slot0_col = jnp.sum(jnp.where(expert_cols == rel0_col, place, 0), axis=1, keepdims=True)
    slot1_col = jnp.sum(jnp.where(expert_cols == rel1_col, place, 0), axis=1, keepdims=True)

    def taken(o):
        slots = iota((most, rows), 0) + o * most
        return ones_where((slots == slot0_row) | (slots == slot1_row))

    cot_value = cot_ref[...]
    cots = []
    for o in [*range(1, experts), 0]:
        picked = dot(taken(o), cot_value).astype(bf16)
        if o == 0:
            recv_cot_ref[0:most, :] = picked
            continue
        part = pl.ds(o * most, most)
        cot_send[part, :] = picked
        cots.append(
            send(cot_send.at[part], recv_cot_ref.at[part], cot_ss.at[o], cot_rs.at[o], (me_dp, me ^ o))
        )
    inputs = patches_ref[...].astype(f32)
    first = (standardize(inputs)[0] * gain1_ref[...] + bias1_ref[...]).astype(bf16)
    first_ref[...] = first
    qkv_ref[:, :width] = (dot(first, qkv_w_ref[:, :width]) + qv_bias_ref[:, :width]).astype(bf16)
    qkv_ref[:, width : 2 * width] = dot(first, qkv_w_ref[:, width : 2 * width]).astype(bf16)
    qkv_ref[:, 2 * width :] = (
        dot(first, qkv_w_ref[:, 2 * width :]) + qv_bias_ref[:, width:]
    ).astype(bf16)
    key_bias = jnp.where(cols_ref[:, 3:4] > 0, 0.0, -1e30)
    scale = LOG2E * HEAD_DIM ** (-0.5)
    pair_width = 2 * HEAD_DIM

    for near_copy in near:
        near_copy.wait_recv()
    far = [
        send(table.at[0], table.at[p], far_ss.at[p], far_rs.at[p], (me_dp ^ p, me))
        for p in range(1, copies)
    ]

    def attend(pair, _):
        base = pl.multiple_of(pair * pair_width, pair_width)
        q = qkv_ref[:, pl.ds(base, pair_width)]
        k = qkv_ref[:, pl.ds(base + width, pair_width)]
        v_t = qkv_ref[:, pl.ds(base + 2 * width, pair_width)].T
        lanes = iota((rows, pair_width), 1)
        outs, stats = [], []
        for a in range(2):
            k_a = jnp.where((lanes >= HEAD_DIM) == (a == 1), k, jnp.zeros((), bf16))
            scores = dot(k_a, q, NT) + key_bias
            peak = jnp.max(scores, axis=0, keepdims=True)
            raised = jnp.exp2(scores * scale - peak * scale)
            total = jnp.sum(raised, axis=0, keepdims=True)
            out = dot(v_t[a * HEAD_DIM : (a + 1) * HEAD_DIM, :], raised.astype(bf16))
            outs.append(out / total)
            stats.append(peak * scale + jnp.log2(total))
        att_t_ref[pl.ds(base, pair_width), :] = jnp.concatenate(outs, axis=0).astype(bf16)
        lse_ref[pair] = jnp.concatenate(stats + [jnp.zeros((6, rows), f32)], axis=0)
        return 0

    lax.fori_loop(0, HEADS // 2, attend, 0)
    residual = inputs + dot(att_t_ref[...], out_w_ref[...], TN) + out_bias_ref[...]
    residual_ref[...] = residual
    second = (standardize(residual)[0] * gain2_ref[...] + bias2_ref[...]).astype(bf16)
    second_ref[...] = second
    for o in range(experts):
        x_slots_ref[pl.ds(o * most, most), :] = dot(taken(o), second).astype(bf16)
    logits = dot(second, router_ref[...])
    raised = jnp.exp(logits - jnp.max(logits, axis=-1, keepdims=True))
    probs = raised / jnp.sum(raised, axis=-1, keepdims=True)
    probs_ref[...] = probs
    prob0 = jnp.sum(jnp.where(expert_cols == id0_col, probs, 0.0), axis=1, keepdims=True)
    prob1 = jnp.sum(jnp.where(expert_cols == id1_col, probs, 0.0), axis=1, keepdims=True)
    both = prob0 + prob1
    gate0, gate1 = prob0 / both, prob1 / both
    for far_copy in far:
        far_copy.wait_recv()
    counts[...] = jnp.zeros_like(counts)
    rank_col = cols_ref[:, 0:1]

    def count(block, _):
        entry = table[block // experts, block % experts]
        real = entry[3:4, :] > 0
        hits = jnp.concatenate(
            [
                ones_where((expert_rows == entry[1:2, :]) & real),
                ones_where((expert_rows == entry[2:3, :]) & real),
            ],
            axis=0,
        )
        lower = ones_where(entry[0:1, :] < rank_col)
        counts[:rows, :] += dot(lower, hits, NT)
        counts[rows:, :] += dot(jnp.ones((8, rows), bf16), hits, NT)
        return 0

    lax.fori_loop(0, copies * experts, count, 0)
    both_cols = iota((rows, 2 * experts), 1)
    ahead = counts[:rows, :]
    loads = counts[rows : rows + 1, :]
    position0 = jnp.sum(jnp.where(both_cols == id0_col, ahead, 0.0), axis=1, keepdims=True)
    position1 = jnp.sum(
        jnp.where(both_cols == id1_col + experts, ahead, 0.0)
        + jnp.where(both_cols == id1_col, loads, 0.0),
        axis=1,
        keepdims=True,
    )
    real_col = cols_ref[:, 3:4] > 0
    kept0 = jnp.where(real_col & (position0 < capacity), 1.0, 0.0)
    kept1 = jnp.where(real_col & (position1 < capacity), 1.0, 0.0)
    gate0, gate1 = gate0 * kept0, gate1 * kept1
    for o in range(experts):
        slots = iota((rows, most), 1) + o * most
        gates = jnp.where(slots == slot0_col, gate0, 0.0) + jnp.where(slots == slot1_col, gate1, 0.0)
        gate_slots_ref[o] = jnp.broadcast_to(jnp.sum(gates, axis=0, keepdims=True), (8, most))
    lanes = iota((rows, 8), 1)
    columns = [slot0_col.astype(f32), slot1_col.astype(f32), gate0, gate1, kept0, kept1, both]
    packed = jnp.zeros((rows, 8), f32)
    for i, column in enumerate(columns):
        packed = jnp.where(lanes == i, column, packed)
    pairs_ref[...] = packed
    for copy in near + far:
        copy.wait_send()
    for copy in cots:
        copy.wait()


VMEM = pl.BlockSpec(memory_space=pltpu.VMEM)
HBM = pl.BlockSpec(memory_space=pl.ANY)
DMA = pltpu.SemaphoreType.DMA


def run_front(copies, experts, most, capacity, *operands):
    rows, width = operands[0].shape
    slots = experts * most
    shape = jax.ShapeDtypeStruct
    return pl.pallas_call(
        partial(front_kernel, copies, experts, most, capacity),
        out_shape=(
            shape((slots, width), bf16),
            shape((slots, width), bf16),
            shape((experts, 8, most), f32),
            shape((rows, 3 * width), bf16),
            shape((width, rows), bf16),
            shape((HEADS // 2, 8, rows), f32),
            shape((rows, width), f32),
            shape((rows, width), bf16),
            shape((rows, width), bf16),
            shape((rows, 8), f32),
            shape((rows, experts), f32),
        ),
        in_specs=[VMEM] * 13,
        out_specs=(VMEM,) * 11,
        scratch_shapes=[
            pltpu.VMEM((slots, width), bf16),
            pltpu.VMEM((copies, experts, 8, rows), i32),
            pltpu.VMEM((rows + 8, 2 * experts), f32),
            DMA((experts,)), DMA((experts,)),
            DMA((experts,)), DMA((experts,)),
            DMA((copies,)), DMA((copies,)),
        ],
        compiler_params=pltpu.CompilerParams(
            collective_id=0, has_side_effects=True, vmem_limit_bytes=VMEM_BYTES
        ),
        name="front",
    )(*operands)


def gelu_parts(values):
    bell = jnp.exp2(values * values * (-0.5 * LOG2E))
    t = 1.0 / (1.0 + (0.3275911 * 0.5**0.5) * jnp.abs(values))
    tail = t * (0.1274147959 + t * (-0.142248368 + t * (0.7107068705 + t * (-0.7265760135 + t * 0.5307027145))))
    tail = tail * bell
    share = jnp.where(values >= 0, 1.0 - tail, tail)
    return values * share, share + values * bell * 0.3989422804014327


def to_column(row):
    n = row.shape[1]
    return jnp.sum(jnp.where(iota((n, n), 0) == iota((n, n), 1), row, 0.0), axis=1, keepdims=True)


def to_row(column):
    n = column.shape[0]
    return jnp.sum(jnp.where(iota((n, n), 0) == iota((n, n), 1), column, 0.0), axis=0, keepdims=True)


def expert_kernel(
    copies, experts, most, chunks, tile,
    x_ref, gates_ref, cot_ref, in_w_ref, in_bias_ref, out_w_ref, out_bias_ref,
    d_rows_ref, d_gates_ref, produced_ref, grads_ref,
    recv_x, recv_g, send_d, send_g, hidden, d_pre, x_t, d_t, bias_sum, total_p, total_d, stage,
    x_ss, x_rs, g_ss, g_rs, d_ss, d_rs, dg_ss, dg_rs, own_sem, own_d_sem, stage_sem,
):
    me_dp = lax.axis_index("dp")
    me = lax.axis_index("expert")
    width, hidden_width = in_w_ref.shape
    rows = chunks * most
    block = hidden_width // copies

    def chunk(o):
        return pl.ds(pl.multiple_of(o * most, most), most)

    def move_x(o):
        return pltpu.make_async_remote_copy(
            x_ref.at[chunk(o)], recv_x.at[chunk(o)], x_ss.at[o], x_rs.at[o], (me_dp, me ^ o), MESH
        )

    def move_g(o):
        return pltpu.make_async_remote_copy(
            gates_ref.at[o], recv_g.at[o], g_ss.at[o], g_rs.at[o], (me_dp, me ^ o), MESH
        )

    def move_d(o):
        return pltpu.make_async_remote_copy(
            send_d.at[chunk(o)], d_rows_ref.at[chunk(o)], d_ss.at[o], d_rs.at[o], (me_dp, me ^ o), MESH
        )

    def move_dg(o):
        return pltpu.make_async_remote_copy(
            send_g.at[o], d_gates_ref.at[o], dg_ss.at[o], dg_rs.at[o], (me_dp, me ^ o), MESH
        )

    own = pltpu.make_async_copy(x_ref.at[chunk(0)], recv_x.at[chunk(0)], own_sem)
    own.start()
    greet([(me_dp, me ^ o) for o in range(1, experts)])
    for o in range(1, experts):
        move_g(o).start()
        move_x(o).start()
    recv_g[0] = gates_ref[0]
    bias_sum[...] = jnp.zeros_like(bias_sum)
    x_t[width:, :] = jnp.ones_like(x_t[width:, :])
    own.wait()
    own_d = pltpu.make_async_copy(send_d.at[chunk(0)], d_rows_ref.at[chunk(0)], own_d_sem)

    def work(g, _):
        for j in range(chunks):
            o = g * chunks + j

            @pl.when(o > 0)
            def _():
                move_g(o).wait_recv()
                move_x(o).wait_recv()

        at = pl.multiple_of(g * rows, rows)
        here = pl.ds(at, rows)
        gate = jnp.concatenate([to_column(recv_g[g * chunks + j][0:1, :]) for j in range(chunks)], axis=0)
        x = recv_x[here, :]
        cot = cot_ref[here, :].astype(f32)
        d_produced = (cot * gate).astype(bf16)
        bias_sum[0:1, :] += jnp.sum(d_produced.astype(f32), axis=0, keepdims=True)
        x_t[:width, here] = x.T
        d_t[:, here] = d_produced.T
        total_p[...] = jnp.zeros_like(total_p)
        total_d[...] = jnp.zeros_like(total_d)

        def step(n, _):
            cols = pl.ds(pl.multiple_of(n * tile, tile), tile)
            pre = dot(x, in_w_ref[:, cols]) + in_bias_ref[:, cols]
            value, slope = gelu_parts(pre)
            value = value.astype(bf16)
            hidden[here, cols] = value
            total_p[...] += dot(value, out_w_ref[cols, :])
            d_value = (dot(d_produced, out_w_ref[cols, :], NT) * slope).astype(bf16)
            d_pre[here, cols] = d_value
            total_d[...] += dot(d_value, in_w_ref[:, cols], NT)
            return 0

        lax.fori_loop(0, hidden_width // tile, step, 0)
        send_d[here, :] = total_d[...].astype(bf16)
        produced = (total_p[...] + out_bias_ref[...]).astype(bf16)
        produced_ref[here, :] = produced
        d_gate = jnp.sum(produced.astype(f32) * cot, axis=1, keepdims=True)
        for j in range(chunks):
            o = g * chunks + j
            d_gate_row = jnp.broadcast_to(to_row(d_gate[j * most : (j + 1) * most, :]), (8, most))
            send_g[o] = d_gate_row

            @pl.when(o > 0)
            def _():
                move_d(o).start()
                move_dg(o).start()

            @pl.when(o == 0)
            def _():
                own_d.start()
                d_gates_ref[0] = d_gate_row

        return 0

    lax.fori_loop(0, experts // chunks, work, 0)

    def store(w, p):
        return pltpu.make_async_copy(stage.at[w], grads_ref.at[w, p], stage_sem.at[w])

    def weigh(p, _):
        cols = pl.ds(pl.multiple_of((me_dp ^ p) * block, block), block)

        @pl.when(p > 0)
        def _():
            store(0, p - 1).wait()

        total = dot(x_t[...], d_pre[:, cols])
        stage[0, :width, :] = total[:width, :].astype(bf16)
        tail = total[width:, :]
        lines = iota((16, block), 0)
        for i in range(-(-width // block)):
            tail = jnp.where(lines == 8 + i, bias_sum[0:1, i * block : (i + 1) * block], tail)
        stage[0, width:, :] = tail.astype(bf16)
        store(0, p).start()

        @pl.when(p > 0)
        def _():
            store(1, p - 1).wait()

        stage[1, :width, :] = dot(d_t[...], hidden[:, cols]).astype(bf16)
        stage[1, width:, :] = jnp.zeros((16, block), bf16)
        store(1, p).start()
        return 0

    lax.fori_loop(0, copies, weigh, 0)
    store(0, copies - 1).wait()
    store(1, copies - 1).wait()
    own_d.wait()
    for o in range(1, experts):
        move_g(o).wait_send()
        move_x(o).wait_send()
        move_d(o).wait()
        move_dg(o).wait()


def run_experts(copies, experts, most, *operands):
    slots, width = operands[0].shape
    hidden_width = operands[3].shape[1]
    chunks = max(1, min(experts, 384 // most))
    rows = chunks * most
    block = hidden_width // copies
    shape = jax.ShapeDtypeStruct
    return pl.pallas_call(
        partial(expert_kernel, copies, experts, most, chunks, 512),
        out_shape=(
            shape((slots, width), bf16),
            shape((experts, 8, most), f32),
            shape((slots, width), bf16),
            shape((2, copies, width + 16, block), bf16),
        ),
        in_specs=[HBM] + [VMEM] * 6,
        out_specs=(HBM, VMEM, VMEM, HBM),
        scratch_shapes=[
            pltpu.VMEM((slots, width), bf16),
            pltpu.VMEM((experts, 8, most), f32),
            pltpu.VMEM((slots, width), bf16),
            pltpu.VMEM((experts, 8, most), f32),
            pltpu.VMEM((slots, hidden_width), bf16),
            pltpu.VMEM((slots, hidden_width), bf16),
            pltpu.VMEM((width + 16, slots), bf16),
            pltpu.VMEM((width, slots), bf16),
            pltpu.VMEM((8, width), f32),
            pltpu.VMEM((rows, width), f32),
            pltpu.VMEM((rows, width), f32),
            pltpu.VMEM((2, width + 16, block), bf16),
        ]
        + [DMA((experts,))] * 8
        + [DMA(()), DMA(()), DMA((2,))],
        compiler_params=pltpu.CompilerParams(
            collective_id=1, has_side_effects=True, vmem_limit_bytes=VMEM_BYTES
        ),
        name="experts",
    )(*operands)


def back_kernel(
    copies, experts, most,
    d_rows_ref, d_gates_ref, produced_ref, grads_ref, pairs_ref, probs_ref, cols_ref,
    second_ref, residual_ref, patches_ref, cot_ref, qkv_ref, att_t_ref, lse_ref, first_ref,
    gain1_ref, gain2_ref, qkv_w_ref, out_w_ref, router_ref,
    output_ref, grad_patches_ref, dense_ref, small_ref, kept_grads_ref, far_grads_ref,
    recv_p, own_grads, near_grads, d_qkv, d_att, d_att_t, d_residual_ref,
    p_ss, p_rs, n_ss, n_rs, f_ss, f_rs, own_sem,
):
    me_dp = lax.axis_index("dp")
    me = lax.axis_index("expert")
    rows, width = patches_ref.shape
    slots = experts * most
    chips = copies // 2
    greet(
        [(me_dp, me ^ o) for o in range(1, experts)]
        + [(me_dp ^ 1, me)]
        + [(me_dp ^ (2 * q), me) for q in range(1, chips)]
    )
    near = [
        send(grads_ref.at[w, 2 * q + 1], near_grads.at[w, q], n_ss.at[w, q], n_rs.at[w, q], (me_dp ^ 1, me))
        for q in range(chips)
        for w in range(2)
    ]
    own = [
        pltpu.make_async_copy(grads_ref.at[w, 2 * q], own_grads.at[w, q], own_sem.at[w, q])
        for q in range(chips)
        for w in range(2)
    ]
    for copy in own:
        copy.start()
    returns = []
    for o in range(1, experts):
        part = pl.ds(o * most, most)
        returns.append(
            send(produced_ref.at[part], recv_p.at[part], p_ss.at[o], p_rs.at[o], (me_dp, me ^ o))
        )
    own_p = pltpu.make_async_copy(
        produced_ref.at[pl.ds(0, most)], recv_p.at[pl.ds(0, most)], p_rs.at[0]
    )
    own_p.start()
    slot0, slot1 = pairs_ref[:, 0:1].astype(i32), pairs_ref[:, 1:2].astype(i32)
    gate0, gate1 = pairs_ref[:, 2:3], pairs_ref[:, 3:4]
    kept0, kept1, both = pairs_ref[:, 4:5], pairs_ref[:, 5:6], pairs_ref[:, 6:7]
    places = iota((rows, slots), 1)
    d_second = dot(ones_where((places == slot0) | (places == slot1)), d_rows_ref[...])
    d_gate0 = jnp.zeros((rows, 1), f32)
    d_gate1 = jnp.zeros((rows, 1), f32)
    for o in range(experts):
        part = iota((rows, most), 1) + o * most
        line = d_gates_ref[o][0:1, :]
        d_gate0 += jnp.sum(jnp.where(part == slot0, line, 0.0), axis=1, keepdims=True)
        d_gate1 += jnp.sum(jnp.where(part == slot1, line, 0.0), axis=1, keepdims=True)
    d_gate0, d_gate1 = d_gate0 * kept0, d_gate1 * kept1
    probs = probs_ref[...]
    names = iota((rows, experts), 1)
    is0, is1 = names == cols_ref[:, 1:2], names == cols_ref[:, 2:3]
    share0 = jnp.sum(jnp.where(is0, probs, 0.0), axis=1, keepdims=True) / both
    share1 = jnp.sum(jnp.where(is1, probs, 0.0), axis=1, keepdims=True) / both
    centre = d_gate0 * share0 + d_gate1 * share1
    d_probs = jnp.where(is0, (d_gate0 - centre) / both, 0.0) + jnp.where(is1, (d_gate1 - centre) / both, 0.0)
    d_logits = (probs * (d_probs - jnp.sum(probs * d_probs, axis=1, keepdims=True))).astype(bf16)
    small_ref[8:, :] = jnp.zeros_like(small_ref[8:, :])
    small_ref[8 : 8 + experts, :] = dot(d_logits, second_ref[...], TN)
    d_second += dot(d_logits, router_ref[...], NT)
    n, inverse = standardize(residual_ref[...])
    small_ref[5:6, :] = jnp.sum(d_second * n, axis=0, keepdims=True)
    small_ref[6:7, :] = jnp.sum(d_second, axis=0, keepdims=True)
    m = d_second * gain2_ref[...]
    d_residual = cot_ref[...].astype(f32) + inverse * (
        m - jnp.mean(m, axis=-1, keepdims=True) - n * jnp.mean(m * n, axis=-1, keepdims=True)
    )
    d_residual_ref[...] = d_residual
    d_branch = d_residual.astype(bf16)
    small_ref[4:5, :] = jnp.sum(d_branch.astype(f32), axis=0, keepdims=True)
    small_ref[7:8, :] = jnp.zeros((1, width), f32)
    for copy in own:
        copy.wait()
    for copy in near:
        copy.wait_recv()
    far = []
    for q in range(chips):
        for w in range(2):
            total = own_grads[w, q].astype(f32) + near_grads[w, q].astype(f32)
            if q == 0:
                kept_grads_ref[w] = total.astype(bf16)
                continue
            own_grads[w, q] = total.astype(bf16)
            far.append(
                send(
                    own_grads.at[w, q], far_grads_ref.at[w, q - 1], f_ss.at[w, q], f_rs.at[w, q],
                    (me_dp ^ (2 * q), me),
                )
            )
    per = width // experts
    group = experts // chips
    half = width // 2

    def keep(matrix, value):
        for e in range(experts):
            at = (e // 2) % chips * group + e // (2 * chips) * 2 + e % 2
            for h in range(2):
                dense_ref[matrix, h, at] = value[e * per : (e + 1) * per, h * half : (h + 1) * half].astype(bf16)

    keep(3, dot(att_t_ref[...], d_branch))
    d_att[...] = dot(d_branch, out_w_ref[...], NT).astype(bf16)
    d_att_t[...] = dot(out_w_ref[...], d_branch, NT).astype(bf16)
    key_bias = jnp.where(cols_ref[:, 3:4] > 0, 0.0, -1e30)
    scale = LOG2E * HEAD_DIM ** (-0.5)
    pair_width = 2 * HEAD_DIM

    def attend(pair, _):
        base = pl.multiple_of(pair * pair_width, pair_width)
        here = pl.ds(base, pair_width)
        q = qkv_ref[:, here]
        k = qkv_ref[:, pl.ds(base + width, pair_width)]
        v = qkv_ref[:, pl.ds(base + 2 * width, pair_width)]
        k_t = k.T
        d_out = d_att[:, here]
        products = att_t_ref[here, :].astype(f32) * d_att_t[here, :].astype(f32)
        lanes = iota((rows, pair_width), 1)
        d_q, d_k, d_v = [], [], []
        for a in range(2):
            mine = (lanes >= HEAD_DIM) == (a == 1)
            k_a = jnp.where(mine, k, jnp.zeros((), bf16))
            v_a = jnp.where(mine, v, jnp.zeros((), bf16))
            part = slice(a * HEAD_DIM, (a + 1) * HEAD_DIM)
            delta = jnp.sum(products[part, :], axis=0, keepdims=True)
            weights = jnp.exp2((dot(k_a, q, NT) + key_bias) * scale - lse_ref[pair][a : a + 1, :])
            d_scores = (weights * (dot(v_a, d_out, NT) - delta)).astype(bf16)
            d_v.append(dot(weights.astype(bf16), d_out))
            d_k.append(dot(d_scores, q))
            d_q.append(dot(k_t[part, :], d_scores))
        low = lanes < HEAD_DIM
        down = HEAD_DIM ** (-0.5)
        d_qkv[:, here] = (jnp.concatenate(d_q, axis=0).T * down).astype(bf16)
        d_qkv[:, pl.ds(base + width, pair_width)] = (jnp.where(low, d_k[0], d_k[1]) * down).astype(bf16)
        d_qkv[:, pl.ds(base + 2 * width, pair_width)] = jnp.where(low, d_v[0], d_v[1]).astype(bf16)
        return 0

    lax.fori_loop(0, HEADS // 2, attend, 0)
    first_t = first_ref[...].T
    d_first = jnp.zeros((rows, width), f32)
    ones = jnp.ones((8, rows), bf16)
    for i in range(3):
        part = slice(i * width, (i + 1) * width)
        d_part = d_qkv[:, part]
        keep(i, dot(first_t, d_part))
        if i != 1:
            small_ref[2 + i // 2 : 3 + i // 2, :] = dot(ones, d_part)[0:1, :]
        d_first += dot(d_part, qkv_w_ref[:, part], NT)
    n, inverse = standardize(patches_ref[...].astype(f32))
    small_ref[0:1, :] = jnp.sum(d_first * n, axis=0, keepdims=True)
    small_ref[1:2, :] = jnp.sum(d_first, axis=0, keepdims=True)
    m = d_first * gain1_ref[...]
    grad_patches_ref[...] = (
        d_residual_ref[...]
        + inverse * (m - jnp.mean(m, axis=-1, keepdims=True) - n * jnp.mean(m * n, axis=-1, keepdims=True))
    ).astype(bf16)
    own_p.wait()
    for copy in returns:
        copy.wait()
    produced = recv_p[...]
    output_ref[...] = (
        residual_ref[...]
        + gate0 * dot(ones_where(places == slot0), produced)
        + gate1 * dot(ones_where(places == slot1), produced)
    ).astype(bf16)
    for copy in near:
        copy.wait_send()
    for copy in far:
        copy.wait()


def run_back(copies, experts, most, *operands):
    rows, width = operands[9].shape
    slots = experts * most
    chips = copies // 2
    block = operands[3].shape[-1]
    shape = jax.ShapeDtypeStruct
    smalls = -(-(8 + experts) // 16) * 16
    return pl.pallas_call(
        partial(back_kernel, copies, experts, most),
        out_shape=(
            shape((rows, width), bf16),
            shape((rows, width), bf16),
            shape((4, 2, experts, width // experts, width // 2), bf16),
            shape((smalls, width), f32),
            shape((2, width + 16, block), bf16),
            shape((2, chips - 1, width + 16, block), bf16),
        ),
        in_specs=[VMEM] * 2 + [HBM] * 2 + [VMEM] * 16,
        out_specs=(VMEM,) * 5 + (HBM,),
        scratch_shapes=[
            pltpu.VMEM((slots, width), bf16),
            pltpu.VMEM((2, chips, width + 16, block), bf16),
            pltpu.VMEM((2, chips, width + 16, block), bf16),
            pltpu.VMEM((rows, 3 * width), bf16),
            pltpu.VMEM((rows, width), bf16),
            pltpu.VMEM((width, rows), bf16),
            pltpu.VMEM((rows, width), f32),
            DMA((experts,)), DMA((experts,)),
            DMA((2, chips)), DMA((2, chips)),
            DMA((2, chips)), DMA((2, chips)),
            DMA((2, chips)),
        ],
        compiler_params=pltpu.CompilerParams(
            collective_id=2, has_side_effects=True, vmem_limit_bytes=VMEM_BYTES
        ),
        name="back",
    )(*operands)


def reduce_kernel(
    copies, experts,
    dense_ref, small_ref, out_ref, small_out_ref,
    near, summed, far, chip_sum, gathered, tiny,
    a_ss, a_rs, b_ss, b_rs, c_ss, c_rs, d_ss, d_rs, e_ss, e_rs, t_ss, t_rs,
):
    me_dp = lax.axis_index("dp")
    me = lax.axis_index("expert")
    core, chip = me_dp % 2, me_dp // 2
    chips = copies // 2
    group = experts // chips
    matrices = dense_ref.shape[0]
    inside = (me // 2) % chips == chip
    over_copies = [(me_dp ^ (1 << i), me) for i in range(copies.bit_length() - 1)]
    over_experts = [(me_dp, me ^ (1 << i)) for i in range(experts.bit_length() - 1)]
    steps = over_copies + over_experts
    greet(
        [(me_dp, me ^ o) for o in range(1, experts)]
        + [(me_dp ^ 1, me)]
        + [(me_dp ^ (2 * q), me) for q in range(1, chips)]
    )

    def place(k):
        return k // 2 * (2 * chips) + chip * 2 + k % 2

    def copy_a(m):
        return pltpu.make_async_remote_copy(
            dense_ref.at[m, 1 - core], near.at[m], a_ss.at[m], a_rs.at[m], (me_dp ^ 1, me), MESH
        )

    def copy_b(m, q):
        return pltpu.make_async_remote_copy(
            summed.at[m, chip ^ q], far.at[m, q - 1], b_ss.at[m, q], b_rs.at[m, q],
            (me_dp ^ (2 * q), me), MESH,
        )

    def copy_c(m, k, o, peer):
        return pltpu.make_async_remote_copy(
            chip_sum.at[m, k], gathered.at[m, o], c_ss.at[m, k], c_rs.at[m, o], (me_dp, peer), MESH
        )

    def copy_d(m, q):
        return pltpu.make_async_remote_copy(
            out_ref.at[m, core], out_ref.at[m, core], d_ss.at[m, q], d_rs.at[m],
            (me_dp ^ (2 * q), me), MESH,
        )

    def copy_e(m):
        return pltpu.make_async_remote_copy(
            out_ref.at[m, core], out_ref.at[m, core], e_ss.at[m], e_rs.at[m], (me_dp ^ 1, me), MESH
        )

    def copy_t(i):
        src = small_ref if i == 0 else tiny.at[0, i - 1]
        return pltpu.make_async_remote_copy(src, tiny.at[1, i], t_ss.at[i], t_rs.at[i], steps[i], MESH)

    def end_t(i):
        copy_t(i).wait_recv()
        mine = small_ref[...] if i == 0 else tiny[0, i - 1]
        tiny[0, i] = mine + tiny[1, i]
        if i + 1 < len(steps):
            copy_t(i + 1).start()

    todo = list(range(len(steps)))

    def advance():
        if todo:
            end_t(todo.pop(0))

    order = [3, 0, 1, 2][-matrices:] if matrices < 4 else [3, 0, 1, 2]
    for m in order:
        copy_a(m).start()
    copy_t(0).start()
    for m in order:
        copy_a(m).wait_recv()
        total = dense_ref[m, core].astype(f32) + near[m].astype(f32)
        summed[m] = total.astype(bf16).reshape(summed.shape[1:])
        for q in range(1, chips):
            copy_b(m, q).start()
    advance()
    for m in order:
        total = summed[m, chip].astype(f32)
        for q in range(1, chips):
            copy_b(m, q).wait_recv()
            total += far[m, q - 1].astype(f32)
        chip_sum[m] = total.astype(bf16)
        for k in range(group):
            peer = place(k)

            @pl.when(peer != me)
            def _():
                copy_c(m, k, me ^ peer, peer).start()

        advance()
    for m in order:

        @pl.when(inside)
        def _():
            total = chip_sum[m, me // (2 * chips) * 2 + me % 2].astype(f32)
            for o in range(1, experts):
                copy_c(m, 0, o, me ^ o).wait_recv()
                total += gathered[m, o].astype(f32)
            out_ref[m, core] = total.astype(bf16)
            for q in range(1, chips):
                copy_d(m, q).start()

        advance()
    for m in order:

        @pl.when(jnp.logical_not(inside))
        def _():
            copy_d(m, 1).wait_recv()

        copy_e(m).start()
        advance()
    while todo:
        advance()
    small_out_ref[...] = tiny[0, len(steps) - 1]
    for m in order:
        copy_a(m).wait_send()
        for q in range(1, chips):
            copy_b(m, q).wait_send()
        for k in range(group):

            @pl.when(place(k) != me)
            def _():
                copy_c(m, k, 1, place(k)).wait_send()

        @pl.when(inside)
        def _():
            for q in range(1, chips):
                copy_d(m, q).wait_send()

        pltpu.make_async_remote_copy(
            out_ref.at[m, core], out_ref.at[m, 1 - core], e_ss.at[m], e_rs.at[m], (me_dp ^ 1, me), MESH
        ).wait()
    for i in range(len(steps)):
        copy_t(i).wait_send()


def run_reduce(copies, experts, *operands):
    matrices, _, _, per, half = operands[0].shape
    smalls, width = operands[1].shape
    chips = copies // 2
    group = experts // chips
    steps = copies.bit_length() - 1 + experts.bit_length() - 1
    shape = jax.ShapeDtypeStruct
    return pl.pallas_call(
        partial(reduce_kernel, copies, experts),
        out_shape=(shape((matrices, 2, per, half), bf16), shape((smalls, width), f32)),
        in_specs=[VMEM] * 2,
        out_specs=(VMEM,) * 2,
        scratch_shapes=[
            pltpu.VMEM((matrices, experts, per, half), bf16),
            pltpu.VMEM((matrices, chips, group, per, half), bf16),
            pltpu.VMEM((matrices, chips - 1, group, per, half), bf16),
            pltpu.VMEM((matrices, group, per, half), bf16),
            pltpu.VMEM((matrices, experts, per, half), bf16),
            pltpu.VMEM((2, steps, smalls, width), f32),
            DMA((matrices,)), DMA((matrices,)),
            DMA((matrices, chips)), DMA((matrices, chips)),
            DMA((matrices, group)), DMA((matrices, experts)),
            DMA((matrices, chips)), DMA((matrices,)),
            DMA((matrices,)), DMA((matrices,)),
            DMA((steps,)), DMA((steps,)),
        ],
        compiler_params=pltpu.CompilerParams(
            collective_id=3, has_side_effects=True, vmem_limit_bytes=VMEM_BYTES
        ),
        name="reduce",
    )(*operands)


def local(
    patches, padding, expert_ids, priority, norm1_gain, norm1_bias, qkv_weight, qv_bias, out_weight,
    out_bias, norm2_gain, norm2_bias, router, expert_in, expert_in_bias, expert_out, expert_out_bias,
    cotangent,
):
    row_count, width = patches.shape
    copies, experts = lax.axis_size("dp"), lax.axis_size("expert")
    total_rows = row_count * copies * experts
    capacity = (210 * total_rows + 100 * experts - 1) // (100 * experts)
    most = 8 * row_count // (3 * experts)
    me_dp, me = lax.axis_index("dp"), lax.axis_index("expert")
    facts = [priority, expert_ids[:, 0], expert_ids[:, 1], padding]
    facts = facts + [jnp.zeros_like(padding)] * 4
    columns = jnp.stack(facts, axis=1)
    gain1, gain2 = norm1_gain[None, :], norm2_gain[None, :]
    (recv_cot, x_slots, gate_slots, qkv, att_t, lse, residual, second, first, pairs, probs) = run_front(
        copies, experts, most, capacity,
        patches, cotangent, jnp.stack(facts), columns,
        gain1, norm1_bias[None, :], qkv_weight, qv_bias[None, :],
        out_weight, out_bias[None, :], gain2, norm2_bias[None, :], router,
    )
    d_rows, d_gates, produced, grads = run_experts(
        copies, experts, most,
        x_slots, gate_slots, recv_cot, expert_in[0], expert_in_bias, expert_out[0], expert_out_bias,
    )
    output, grad_patches, dense, small, kept_grads, far_grads = run_back(
        copies, experts, most,
        d_rows, d_gates, produced, grads, pairs, probs, columns,
        second, residual, patches, cotangent, qkv, att_t, lse, first,
        gain1, gain2, qkv_weight, out_weight, router,
    )
    reduced, small = run_reduce(copies, experts, dense, small)
    expert_grads = kept_grads.astype(f32) + jnp.sum(far_grads.astype(f32), axis=1)
    grad_expert_in = expert_grads[0, :width][None]
    grad_expert_in_bias = expert_grads[0, width][None]
    grad_expert_out = expert_grads[1, :width].T[None]
    out_bias_grad = expert_grads[0, width + 8 :].reshape(-1)[:width]
    share = width // copies
    grad_expert_out_bias = lax.dynamic_slice(out_bias_grad, (me_dp * share,), (share,))[None]
    weights = reduced.astype(f32).transpose(2, 0, 1, 3).reshape(width // experts, 4 * width)
    per = width // experts
    mine = lax.dynamic_slice(small, (0, me * per), (small.shape[0], per))
    value_bias = lax.dynamic_slice(small[2:4].reshape(-1), (me * 2 * per,), (2 * per,))
    return (
        output, grad_patches, mine[0], mine[1], weights[:, : 3 * width], value_bias, weights[:, 3 * width :],
        mine[4], mine[5], mine[6], mine[8 : 8 + experts].T,
        grad_expert_in, grad_expert_in_bias, grad_expert_out, grad_expert_out_bias,
    )


def solution(mesh):
    tokens = P(("dp", "expert"))
    wide = P(("dp", "expert"), None)
    return jax.shard_map(
        local,
        mesh=mesh,
        in_specs=(
            wide, tokens, wide, tokens, P(), P(), P(), P(), P(), P(), P(), P(), P(),
            P("expert", None, None), P("expert", None), P("expert", None, None), P("expert", None), wide,
        ),
        out_specs=(
            wide, wide, P("expert"), P("expert"), P("expert", None), P("expert"), P("expert", None),
            P("expert"), P("expert"), P("expert"), P("expert", None), P("expert", None, "dp"),
            P("expert", "dp"), P("expert", "dp", None), P("expert", "dp"),
        ),
        check_vma=False,
    )
```

```python
from functools import partial

import jax
import jax.numpy as jnp
from jax import lax
from jax.experimental import pallas as pl
from jax.experimental.pallas import tpu as pltpu
from jax.sharding import PartitionSpec as P

HEADS = 12
HEAD_DIM = 64
SEQ_LEN = 576
LOG2E = 1.4426950408889634
EPS = 1e-06
MESH = pl.DeviceIdType.MESH
NN = (((1,), (0,)), ((), ()))
NT = (((1,), (1,)), ((), ()))
TN = (((0,), (0,)), ((), ()))
VMEM_BYTES = 63 << 20
bf16 = jnp.bfloat16
f32 = jnp.float32
i32 = jnp.int32


def dot(a, b, dims=NN):
    return lax.dot_general(a, b, dims, preferred_element_type=f32)


def iota(shape, axis):
    return lax.broadcasted_iota(i32, shape, axis)


def flat(ref):
    return ref[...].reshape(1, ref.shape[0])


def ones_where(mask):
    return jnp.where(mask, 1.0, 0.0).astype(bf16)


def standardize(values):
    centred = values - jnp.mean(values, axis=-1, keepdims=True)
    inverse = lax.rsqrt(jnp.mean(centred * centred, axis=-1, keepdims=True) + EPS)
    return centred * inverse, inverse


def greet(peers):
    barrier = pltpu.get_barrier_semaphore()
    for peer in peers:
        pl.semaphore_signal(barrier, inc=1, device_id=peer, device_id_type=MESH)
    pl.semaphore_wait(barrier, len(peers))


def send(src, dst, send_sem, recv_sem, peer):
    copy = pltpu.make_async_remote_copy(
        src_ref=src, dst_ref=dst, send_sem=send_sem, recv_sem=recv_sem,
        device_id=peer, device_id_type=MESH,
    )
    copy.start()
    return copy


def front_kernel(
    copies, experts, most, capacity,
    patches_ref, cot_ref, priority_ref, ids_ref, padding_ref, gain1_ref, bias1_ref, qkv_w_ref, qv_bias_ref,
    out_w_ref, out_bias_ref, gain2_ref, bias2_ref, router_ref,
    recv_cot_ref, x_slots_ref, gate_slots_ref, qkv_ref, att_t_ref, lse_ref, residual_ref,
    second_ref, first_ref, pairs_ref, probs_ref,
    cot_send, rows_ref, table, counts, cot_ss, cot_rs, near_ss, near_rs, far_ss, far_rs,
):
    me_dp = lax.axis_index("dp")
    me = lax.axis_index("expert")
    rows, width = patches_ref.shape
    rows_ref[0:1, :] = priority_ref[...].reshape(1, rows)
    rows_ref[1:3, :] = ids_ref[...]
    rows_ref[3:4, :] = padding_ref[...].reshape(1, rows)
    rows_ref[4:, :] = jnp.zeros((4, rows), i32)
    cols = rows_ref[...].T
    greet(
        [(me_dp, me ^ o) for o in range(1, experts)]
        + [(me_dp ^ p, me) for p in range(1, copies)]
    )
    near = [
        send(rows_ref, table.at[0, o], near_ss.at[o], near_rs.at[o], (me_dp, me ^ o))
        for o in range(1, experts)
    ]
    table[0, 0] = rows_ref[...]
    id0_row, id1_row = rows_ref[1:2, :] ^ me, rows_ref[2:3, :] ^ me
    expert_rows = iota((experts, rows), 0)
    named_t = ones_where((expert_rows == id0_row) | (expert_rows == id1_row))
    before_t = ones_where(iota((rows, rows), 0) < iota((rows, rows), 1))
    place_t = dot(named_t, before_t).astype(i32) + expert_rows * most
    slot0_row = jnp.sum(jnp.where(expert_rows == id0_row, place_t, 0), axis=0, keepdims=True)
    slot1_row = jnp.sum(jnp.where(expert_rows == id1_row, place_t, 0), axis=0, keepdims=True)
    id0_col, id1_col = cols[:, 1:2], cols[:, 2:3]
    rel0_col, rel1_col = id0_col ^ me, id1_col ^ me
    expert_cols = iota((rows, experts), 1)
    named = ones_where((expert_cols == rel0_col) | (expert_cols == rel1_col))
    before = ones_where(iota((rows, rows), 1) < iota((rows, rows), 0))
    place = dot(before, named).astype(i32) + expert_cols * most
    slot0_col = jnp.sum(jnp.where(expert_cols == rel0_col, place, 0), axis=1, keepdims=True)
    slot1_col = jnp.sum(jnp.where(expert_cols == rel1_col, place, 0), axis=1, keepdims=True)

    def taken(o):
        slots = iota((most, rows), 0) + o * most
        return ones_where((slots == slot0_row) | (slots == slot1_row))

    cot_value = cot_ref[...]
    cots = []
    for o in [*range(1, experts), 0]:
        picked = dot(taken(o), cot_value).astype(bf16)
        if o == 0:
            recv_cot_ref[0:most, :] = picked
            continue
        part = pl.ds(o * most, most)
        cot_send[part, :] = picked
        cots.append(
            send(cot_send.at[part], recv_cot_ref.at[part], cot_ss.at[o], cot_rs.at[o], (me_dp, me ^ o))
        )
    inputs = patches_ref[...].astype(f32)
    first = (standardize(inputs)[0] * flat(gain1_ref) + flat(bias1_ref)).astype(bf16)
    first_ref[...] = first
    qkv_ref[:, :width] = (dot(first, qkv_w_ref[:, :width]) + flat(qv_bias_ref)[:, :width]).astype(bf16)
    qkv_ref[:, width : 2 * width] = dot(first, qkv_w_ref[:, width : 2 * width]).astype(bf16)
    qkv_ref[:, 2 * width :] = (
        dot(first, qkv_w_ref[:, 2 * width :]) + flat(qv_bias_ref)[:, width:]
    ).astype(bf16)
    key_bias = jnp.where(cols[:, 3:4] > 0, 0.0, -1e30)
    scale = LOG2E * HEAD_DIM ** (-0.5)
    pair_width = 2 * HEAD_DIM

    for near_copy in near:
        near_copy.wait_recv()
    far = [
        send(table.at[0], table.at[p], far_ss.at[p], far_rs.at[p], (me_dp ^ p, me))
        for p in range(1, copies)
    ]

    def attend(pair, _):
        base = pl.multiple_of(pair * pair_width, pair_width)
        q = qkv_ref[:, pl.ds(base, pair_width)]
        k = qkv_ref[:, pl.ds(base + width, pair_width)]
        v_t = qkv_ref[:, pl.ds(base + 2 * width, pair_width)].T
        lanes = iota((rows, pair_width), 1)
        outs, stats = [], []
        for a in range(2):
            k_a = jnp.where((lanes >= HEAD_DIM) == (a == 1), k, jnp.zeros((), bf16))
            scores = dot(k_a, q, NT) + key_bias
            peak = jnp.max(scores, axis=0, keepdims=True)
            raised = jnp.exp2(scores * scale - peak * scale)
            total = jnp.sum(raised, axis=0, keepdims=True)
            out = dot(v_t[a * HEAD_DIM : (a + 1) * HEAD_DIM, :], raised.astype(bf16))
            outs.append(out / total)
            stats.append(peak * scale + jnp.log2(total))
        att_t_ref[pl.ds(base, pair_width), :] = jnp.concatenate(outs, axis=0).astype(bf16)
        lse_ref[pair] = jnp.concatenate(stats + [jnp.zeros((6, rows), f32)], axis=0)
        return 0

    lax.fori_loop(0, HEADS // 2, attend, 0)
    residual = inputs + dot(att_t_ref[...], out_w_ref[...], TN) + flat(out_bias_ref)
    residual_ref[...] = residual
    second = (standardize(residual)[0] * flat(gain2_ref) + flat(bias2_ref)).astype(bf16)
    second_ref[...] = second
    for o in range(experts):
        x_slots_ref[pl.ds(o * most, most), :] = dot(taken(o), second).astype(bf16)
    logits = dot(second, router_ref[...], NT)
    raised = jnp.exp(logits - jnp.max(logits, axis=-1, keepdims=True))
    probs = raised / jnp.sum(raised, axis=-1, keepdims=True)
    probs_ref[...] = probs
    prob0 = jnp.sum(jnp.where(expert_cols == id0_col, probs, 0.0), axis=1, keepdims=True)
    prob1 = jnp.sum(jnp.where(expert_cols == id1_col, probs, 0.0), axis=1, keepdims=True)
    both = prob0 + prob1
    gate0, gate1 = prob0 / both, prob1 / both
    for far_copy in far:
        far_copy.wait_recv()
    counts[...] = jnp.zeros_like(counts)
    rank_col = cols[:, 0:1]

    def count(block, _):
        entry = table[block // experts, block % experts]
        real = entry[3:4, :] > 0
        hits = jnp.concatenate(
            [
                ones_where((expert_rows == entry[1:2, :]) & real),
                ones_where((expert_rows == entry[2:3, :]) & real),
            ],
            axis=0,
        )
        lower = ones_where(entry[0:1, :] < rank_col)
        counts[:rows, :] += dot(lower, hits, NT)
        counts[rows:, :] += dot(jnp.ones((8, rows), bf16), hits, NT)
        return 0

    lax.fori_loop(0, copies * experts, count, 0)
    both_cols = iota((rows, 2 * experts), 1)
    ahead = counts[:rows, :]
    loads = counts[rows : rows + 1, :]
    position0 = jnp.sum(jnp.where(both_cols == id0_col, ahead, 0.0), axis=1, keepdims=True)
    position1 = jnp.sum(
        jnp.where(both_cols == id1_col + experts, ahead, 0.0)
        + jnp.where(both_cols == id1_col, loads, 0.0),
        axis=1,
        keepdims=True,
    )
    real_col = cols[:, 3:4] > 0
    kept0 = jnp.where(real_col & (position0 < capacity), 1.0, 0.0)
    kept1 = jnp.where(real_col & (position1 < capacity), 1.0, 0.0)
    gate0, gate1 = gate0 * kept0, gate1 * kept1
    for o in range(experts):
        slots = iota((rows, most), 1) + o * most
        gates = jnp.where(slots == slot0_col, gate0, 0.0) + jnp.where(slots == slot1_col, gate1, 0.0)
        gate_slots_ref[o] = jnp.broadcast_to(jnp.sum(gates, axis=0, keepdims=True), (8, most))
    lanes = iota((rows, 16), 1)
    columns = [slot0_col, slot1_col, gate0, gate1, kept0, kept1, both, cols[:, 3:4], id0_col, id1_col]
    columns = [column.astype(f32) for column in columns]
    packed = jnp.zeros((rows, 16), f32)
    for i, column in enumerate(columns):
        packed = jnp.where(lanes == i, column, packed)
    pairs_ref[...] = packed
    for copy in near + far:
        copy.wait_send()
    for copy in cots:
        copy.wait()


VMEM = pl.BlockSpec(memory_space=pltpu.VMEM)
HBM = pl.BlockSpec(memory_space=pl.ANY)
DMA = pltpu.SemaphoreType.DMA


def run_front(copies, experts, most, capacity, *operands):
    rows, width = operands[0].shape
    slots = experts * most
    shape = jax.ShapeDtypeStruct
    return pl.pallas_call(
        partial(front_kernel, copies, experts, most, capacity),
        out_shape=(
            shape((slots, width), bf16),
            shape((slots, width), bf16),
            shape((experts, 8, most), f32),
            shape((rows, 3 * width), bf16),
            shape((width, rows), bf16),
            shape((HEADS // 2, 8, rows), f32),
            shape((rows, width), f32),
            shape((rows, width), bf16),
            shape((rows, width), bf16),
            shape((rows, 16), f32),
            shape((rows, experts), f32),
        ),
        in_specs=[VMEM] * 14,
        out_specs=(VMEM,) * 11,
        scratch_shapes=[
            pltpu.VMEM((slots, width), bf16),
            pltpu.VMEM((8, rows), i32),
            pltpu.VMEM((copies, experts, 8, rows), i32),
            pltpu.VMEM((rows + 8, 2 * experts), f32),
            DMA((experts,)), DMA((experts,)),
            DMA((experts,)), DMA((experts,)),
            DMA((copies,)), DMA((copies,)),
        ],
        compiler_params=pltpu.CompilerParams(
            collective_id=0, has_side_effects=True, vmem_limit_bytes=VMEM_BYTES
        ),
        name="front",
    )(*operands)


def gelu_parts(values):
    bell = jnp.exp2(values * values * (-0.5 * LOG2E))
    t = 1.0 / (1.0 + (0.3275911 * 0.5**0.5) * jnp.abs(values))
    tail = t * (0.1274147959 + t * (-0.142248368 + t * (0.7107068705 + t * (-0.7265760135 + t * 0.5307027145))))
    tail = tail * bell
    share = jnp.where(values >= 0, 1.0 - tail, tail)
    return values * share, share + values * bell * 0.3989422804014327


def to_column(row):
    n = row.shape[1]
    return jnp.sum(jnp.where(iota((n, n), 0) == iota((n, n), 1), row, 0.0), axis=1, keepdims=True)


def to_row(column):
    n = column.shape[0]
    return jnp.sum(jnp.where(iota((n, n), 0) == iota((n, n), 1), column, 0.0), axis=0, keepdims=True)


def expert_kernel(
    copies, experts, most, chunks, tile,
    x_ref, gates_ref, cot_ref, in_w_ref, in_bias_ref, out_w_ref, out_bias_ref,
    d_rows_ref, d_gates_ref, produced_ref, grads_ref,
    recv_x, recv_g, send_d, send_g, hidden, d_pre, x_t, d_t, bias_sum, total_p, total_d, stage,
    x_ss, x_rs, g_ss, g_rs, d_ss, d_rs, dg_ss, dg_rs, own_sem, own_d_sem, stage_sem,
):
    me_dp = lax.axis_index("dp")
    me = lax.axis_index("expert")
    width, hidden_width = in_w_ref.shape
    rows = chunks * most
    block = hidden_width // copies

    def chunk(o):
        return pl.ds(pl.multiple_of(o * most, most), most)

    def move_x(o):
        return pltpu.make_async_remote_copy(
            x_ref.at[chunk(o)], recv_x.at[chunk(o)], x_ss.at[o], x_rs.at[o], (me_dp, me ^ o), MESH
        )

    def move_g(o):
        return pltpu.make_async_remote_copy(
            gates_ref.at[o], recv_g.at[o], g_ss.at[o], g_rs.at[o], (me_dp, me ^ o), MESH
        )

    def move_d(o):
        return pltpu.make_async_remote_copy(
            send_d.at[chunk(o)], d_rows_ref.at[chunk(o)], d_ss.at[o], d_rs.at[o], (me_dp, me ^ o), MESH
        )

    def move_dg(o):
        return pltpu.make_async_remote_copy(
            send_g.at[o], d_gates_ref.at[o], dg_ss.at[o], dg_rs.at[o], (me_dp, me ^ o), MESH
        )

    own = pltpu.make_async_copy(x_ref.at[chunk(0)], recv_x.at[chunk(0)], own_sem)
    own.start()
    greet([(me_dp, me ^ o) for o in range(1, experts)])

    def begin(g):
        for o in range(max(1, g * chunks), (g + 1) * chunks):
            move_g(o).start()
            move_x(o).start()

    groups = experts // chunks
    order = [0, *range(groups // 2, groups), *range(1, groups // 2)]
    begin(order[0])
    begin(order[1])
    recv_g[0] = gates_ref[0]
    bias_sum[...] = jnp.zeros_like(bias_sum)
    x_t[width:, :] = jnp.ones_like(x_t[width:, :])
    own.wait()
    own_d = pltpu.make_async_copy(send_d.at[chunk(0)], d_rows_ref.at[chunk(0)], own_d_sem)

    def work(n, _):
        g = n % 2 * (groups // 2) + n // 2
        for j in range(chunks):
            o = g * chunks + j

            @pl.when(o > 0)
            def _():
                move_g(o).wait_recv()
                move_x(o).wait_recv()

        at = pl.multiple_of(g * rows, rows)
        here = pl.ds(at, rows)
        gate = jnp.concatenate([to_column(recv_g[g * chunks + j][0:1, :]) for j in range(chunks)], axis=0)
        x = recv_x[here, :]
        cot = cot_ref[here, :].astype(f32)
        d_produced = (cot * gate).astype(bf16)
        bias_sum[0:1, :] += jnp.sum(d_produced.astype(f32), axis=0, keepdims=True)
        x_t[:width, here] = x.T
        d_t[:, here] = d_produced.T
        total_p[...] = jnp.zeros_like(total_p)
        total_d[...] = jnp.zeros_like(total_d)

        def step(n, _):
            cols = pl.ds(pl.multiple_of(n * tile, tile), tile)
            pre = dot(x, in_w_ref[:, cols]) + in_bias_ref[:, cols]
            value, slope = gelu_parts(pre)
            value = value.astype(bf16)
            hidden[here, cols] = value
            total_p[...] += dot(value, out_w_ref[cols, :])
            d_value = (dot(d_produced, out_w_ref[cols, :], NT) * slope).astype(bf16)
            d_pre[here, cols] = d_value
            total_d[...] += dot(d_value, in_w_ref[:, cols], NT)
            return 0

        lax.fori_loop(0, hidden_width // tile, step, 0)

        @pl.when(n == 0)
        def _():
            for later in order[2:]:
                begin(later)

        send_d[here, :] = total_d[...].astype(bf16)
        produced = (total_p[...] + out_bias_ref[...]).astype(bf16)
        produced_ref[here, :] = produced
        d_gate = jnp.sum(produced.astype(f32) * cot, axis=1, keepdims=True)
        for j in range(chunks):
            o = g * chunks + j
            d_gate_row = jnp.broadcast_to(to_row(d_gate[j * most : (j + 1) * most, :]), (8, most))
            send_g[o] = d_gate_row

            @pl.when(o > 0)
            def _():
                move_d(o).start()
                move_dg(o).start()

            @pl.when(o == 0)
            def _():
                own_d.start()
                d_gates_ref[0] = d_gate_row

        return 0

    lax.fori_loop(0, groups, work, 0)

    def store(w, p):
        return pltpu.make_async_copy(stage.at[w], grads_ref.at[w, p], stage_sem.at[w])

    def weigh(p, _):
        cols = pl.ds(pl.multiple_of((me_dp ^ p) * block, block), block)

        @pl.when(p > 0)
        def _():
            store(0, p - 1).wait()

        total = dot(x_t[...], d_pre[:, cols])
        stage[0, :width, :] = total[:width, :].astype(bf16)
        tail = total[width:, :]
        lines = iota((16, block), 0)
        for i in range(-(-width // block)):
            tail = jnp.where(lines == 8 + i, bias_sum[0:1, i * block : (i + 1) * block], tail)
        stage[0, width:, :] = tail.astype(bf16)
        store(0, p).start()

        @pl.when(p > 0)
        def _():
            store(1, p - 1).wait()

        stage[1, :width, :] = dot(d_t[...], hidden[:, cols]).astype(bf16)
        stage[1, width:, :] = jnp.zeros((16, block), bf16)
        store(1, p).start()
        return 0

    lax.fori_loop(0, copies, weigh, 0)
    store(0, copies - 1).wait()
    store(1, copies - 1).wait()
    own_d.wait()
    for o in range(1, experts):
        move_g(o).wait_send()
        move_x(o).wait_send()
        move_d(o).wait()
        move_dg(o).wait()


def run_experts(copies, experts, most, *operands):
    slots, width = operands[0].shape
    hidden_width = operands[3].shape[1]
    chunks = max(1, min(experts, 384 // most))
    rows = chunks * most
    block = hidden_width // copies
    shape = jax.ShapeDtypeStruct
    return pl.pallas_call(
        partial(expert_kernel, copies, experts, most, chunks, 512),
        out_shape=(
            shape((slots, width), bf16),
            shape((experts, 8, most), f32),
            shape((slots, width), bf16),
            shape((2, copies, width + 16, block), bf16),
        ),
        in_specs=[HBM] + [VMEM] * 6,
        out_specs=(HBM, VMEM, VMEM, HBM),
        scratch_shapes=[
            pltpu.VMEM((slots, width), bf16),
            pltpu.VMEM((experts, 8, most), f32),
            pltpu.VMEM((slots, width), bf16),
            pltpu.VMEM((experts, 8, most), f32),
            pltpu.VMEM((slots, hidden_width), bf16),
            pltpu.VMEM((slots, hidden_width), bf16),
            pltpu.VMEM((width + 16, slots), bf16),
            pltpu.VMEM((width, slots), bf16),
            pltpu.VMEM((8, width), f32),
            pltpu.VMEM((rows, width), f32),
            pltpu.VMEM((rows, width), f32),
            pltpu.VMEM((2, width + 16, block), bf16),
        ]
        + [DMA((experts,))] * 8
        + [DMA(()), DMA(()), DMA((2,))],
        compiler_params=pltpu.CompilerParams(
            collective_id=1, has_side_effects=True, vmem_limit_bytes=VMEM_BYTES
        ),
        name="experts",
    )(*operands)


def back_kernel(
    copies, experts, most,
    d_rows_ref, d_gates_ref, produced_ref, grads_ref, pairs_ref, probs_ref,
    second_ref, residual_ref, patches_ref, cot_ref, qkv_ref, att_t_ref, lse_ref, first_ref,
    gain1_ref, gain2_ref, qkv_w_ref, out_w_ref, router_ref,
    output_ref, grad_patches_ref, sums_ref, small_sums_ref, kept_grads_ref, far_grads_ref,
    recv_p, own_grads, near_grads, d_qkv, d_att, d_att_t, d_residual_ref,
    dense, small, halves, landed, crossed, tiny,
    p_ss, p_rs, n_ss, n_rs, f_ss, f_rs, own_sem, kept_sem,
    a_ss, a_rs, b_ss, b_rs, c_ss, c_rs, e_ss, e_rs, t_ss, t_rs,
):
    me_dp = lax.axis_index("dp")
    me = lax.axis_index("expert")
    rows, width = patches_ref.shape
    slots = experts * most
    chips = copies // 2
    core = me_dp % 2
    per = width // experts
    half = width // 2
    partner = (me_dp ^ 1, me)
    bits = [1, 0, *range(2, experts.bit_length() - 1)]
    steps = [(me_dp ^ (1 << i), me) for i in range(copies.bit_length() - 1)]
    steps += [(me_dp, me ^ (1 << i)) for i in range(experts.bit_length() - 1)]

    def copy_a(m):
        return pltpu.make_async_remote_copy(
            dense.at[m, 1 - core], halves.at[m], a_ss.at[m], a_rs.at[m], partner, MESH
        )

    def copy_b(m, i):
        part = pl.ds(experts >> (i + 1), experts >> (i + 1))
        return pltpu.make_async_remote_copy(
            dense.at[m, core, part], landed.at[m, part], b_ss.at[m, i], b_rs.at[m, i],
            (me_dp, me ^ (1 << bits[i])), MESH,
        )

    def copy_c(m, q):
        return pltpu.make_async_remote_copy(
            dense.at[m, core, 0], crossed.at[m, q - 1], c_ss.at[m, q], c_rs.at[m, q],
            (me_dp ^ (2 * q), me), MESH,
        )

    def copy_e(m):
        return pltpu.make_async_remote_copy(
            sums_ref.at[m, core], sums_ref.at[m, core], e_ss.at[m], e_rs.at[m], partner, MESH
        )

    def begin(m, k):
        if k == 0:
            copy_a(m).start()
        elif k <= len(bits):
            copy_b(m, k - 1).start()
        elif k == len(bits) + 1:
            for q in range(1, chips):
                copy_c(m, q).start()
        else:
            copy_e(m).start()

    def end(m, k):
        if k == 0:
            copy_a(m).wait_recv()
            dense[m, core] = (dense[m, core].astype(f32) + halves[m].astype(f32)).astype(bf16)
        elif k <= len(bits):
            copy_b(m, k - 1).wait_recv()
            n = experts >> k
            total = dense[m, core, 0:n].astype(f32) + landed[m, n : 2 * n].astype(f32)
            dense[m, core, 0:n] = total.astype(bf16)
        elif k == len(bits) + 1:
            total = dense[m, core, 0].astype(f32)
            for q in range(1, chips):
                copy_c(m, q).wait_recv()
                total += crossed[m, q - 1].astype(f32)
            sums_ref[m, core] = total.astype(bf16)

    stages = [0] * 4

    def advance(m):
        if stages[m] < len(bits) + 2:
            end(m, stages[m])
            stages[m] += 1
            begin(m, stages[m])

    def copy_t(i):
        src = small if i == 0 else tiny.at[0, i - 1]
        return pltpu.make_async_remote_copy(src, tiny.at[1, i], t_ss.at[i], t_rs.at[i], steps[i], MESH)

    todo = list(range(len(steps)))

    def advance_small():
        if todo:
            i = todo.pop(0)
            copy_t(i).wait_recv()
            mine = small[...] if i == 0 else tiny[0, i - 1]
            tiny[0, i] = mine + tiny[1, i]
            if i + 1 < len(steps):
                copy_t(i + 1).start()

    def copy_f(w, q):
        return pltpu.make_async_remote_copy(
            near_grads.at[w, q], far_grads_ref.at[w, q - 1], f_ss.at[w, q], f_rs.at[w, q],
            (me_dp ^ (2 * q), me), MESH,
        )

    greet(
        [(me_dp, me ^ o) for o in range(1, experts)]
        + [partner]
        + [(me_dp ^ (2 * q), me) for q in range(1, chips)]
    )
    near = [
        send(grads_ref.at[w, 2 * q + 1], near_grads.at[w, q], n_ss.at[w, q], n_rs.at[w, q], partner)
        for q in range(chips)
        for w in range(2)
    ]
    turns = [(w, q) for q in [*range(1, chips), 0] for w in range(2)]
    own = [
        pltpu.make_async_copy(grads_ref.at[w, 2 * q], own_grads.at[i % 2], own_sem.at[i % 2])
        for i, (w, q) in enumerate(turns)
    ]
    for copy in own[:2]:
        copy.start()
    returns = []
    for o in range(1, experts):
        part = pl.ds(o * most, most)
        returns.append(
            send(produced_ref.at[part], recv_p.at[part], p_ss.at[o], p_rs.at[o], (me_dp, me ^ o))
        )
    own_p = pltpu.make_async_copy(
        produced_ref.at[pl.ds(0, most)], recv_p.at[pl.ds(0, most)], p_rs.at[0]
    )
    own_p.start()
    slot0, slot1 = pairs_ref[:, 0:1].astype(i32), pairs_ref[:, 1:2].astype(i32)
    kept0, kept1, both = pairs_ref[:, 4:5], pairs_ref[:, 5:6], pairs_ref[:, 6:7]
    places = iota((rows, slots), 1)
    d_second = dot(ones_where((places == slot0) | (places == slot1)), d_rows_ref[...])
    d_gate0 = jnp.zeros((rows, 1), f32)
    d_gate1 = jnp.zeros((rows, 1), f32)
    for o in range(experts):
        part = iota((rows, most), 1) + o * most
        line = d_gates_ref[o][0:1, :]
        d_gate0 += jnp.sum(jnp.where(part == slot0, line, 0.0), axis=1, keepdims=True)
        d_gate1 += jnp.sum(jnp.where(part == slot1, line, 0.0), axis=1, keepdims=True)
    d_gate0, d_gate1 = d_gate0 * kept0, d_gate1 * kept1
    probs = probs_ref[...]
    names = iota((rows, experts), 1)
    is0, is1 = names == pairs_ref[:, 8:9].astype(i32), names == pairs_ref[:, 9:10].astype(i32)
    share0 = jnp.sum(jnp.where(is0, probs, 0.0), axis=1, keepdims=True) / both
    share1 = jnp.sum(jnp.where(is1, probs, 0.0), axis=1, keepdims=True) / both
    centre = d_gate0 * share0 + d_gate1 * share1
    d_probs = jnp.where(is0, (d_gate0 - centre) / both, 0.0) + jnp.where(is1, (d_gate1 - centre) / both, 0.0)
    d_logits = (probs * (d_probs - jnp.sum(probs * d_probs, axis=1, keepdims=True))).astype(bf16)
    small[8:, :] = jnp.zeros_like(small[8:, :])
    small[8 : 8 + experts, :] = dot(d_logits, second_ref[...], TN)
    d_second += dot(d_logits, router_ref[...])
    n, inverse = standardize(residual_ref[...])
    small[5:6, :] = jnp.sum(d_second * n, axis=0, keepdims=True)
    small[6:7, :] = jnp.sum(d_second, axis=0, keepdims=True)
    m = d_second * flat(gain2_ref)
    d_residual = cot_ref[...].astype(f32) + inverse * (
        m - jnp.mean(m, axis=-1, keepdims=True) - n * jnp.mean(m * n, axis=-1, keepdims=True)
    )
    d_residual_ref[...] = d_residual
    d_branch = d_residual.astype(bf16)
    small[4:5, :] = jnp.sum(d_branch.astype(f32), axis=0, keepdims=True)
    small[7:8, :] = jnp.zeros((1, width), f32)

    def keep(matrix, value):
        for e in range(experts):
            r = e ^ me
            at = 0
            for bit in bits:
                at = at * 2 + (r // (1 << bit)) % 2
            for h in range(2):
                dense[matrix, h, at] = value[e * per : (e + 1) * per, h * half : (h + 1) * half].astype(bf16)
        begin(matrix, 0)

    keep(3, dot(att_t_ref[...], d_branch))
    for copy in near:
        copy.wait_recv()
    for i, (w, q) in enumerate(turns):
        own[i].wait()
        near_grads[w, q] = (own_grads[i % 2].astype(f32) + near_grads[w, q].astype(f32)).astype(bf16)
        if i + 2 < len(turns):
            own[i + 2].start()
        if q > 0:
            copy_f(w, q).start()
    kept = pltpu.make_async_copy(near_grads.at[:, 0], kept_grads_ref, kept_sem)
    kept.start()
    advance(3)
    d_att[...] = dot(d_branch, out_w_ref[...], NT).astype(bf16)
    d_att_t[...] = dot(out_w_ref[...], d_branch, NT).astype(bf16)
    key_bias = jnp.where(pairs_ref[:, 7:8] > 0, 0.0, -1e30)
    scale = LOG2E * HEAD_DIM ** (-0.5)
    pair_width = 2 * HEAD_DIM

    def attend(pair, _):
        base = pl.multiple_of(pair * pair_width, pair_width)
        here = pl.ds(base, pair_width)
        q = qkv_ref[:, here]
        k = qkv_ref[:, pl.ds(base + width, pair_width)]
        v = qkv_ref[:, pl.ds(base + 2 * width, pair_width)]
        k_t = k.T
        d_out = d_att[:, here]
        products = att_t_ref[here, :].astype(f32) * d_att_t[here, :].astype(f32)
        lanes = iota((rows, pair_width), 1)
        d_q, d_k, d_v = [], [], []
        for a in range(2):
            mine = (lanes >= HEAD_DIM) == (a == 1)
            k_a = jnp.where(mine, k, jnp.zeros((), bf16))
            v_a = jnp.where(mine, v, jnp.zeros((), bf16))
            part = slice(a * HEAD_DIM, (a + 1) * HEAD_DIM)
            delta = jnp.sum(products[part, :], axis=0, keepdims=True)
            weights = jnp.exp2((dot(k_a, q, NT) + key_bias) * scale - lse_ref[pair][a : a + 1, :])
            d_scores = (weights * (dot(v_a, d_out, NT) - delta)).astype(bf16)
            d_v.append(dot(weights.astype(bf16), d_out))
            d_k.append(dot(d_scores, q))
            d_q.append(dot(k_t[part, :], d_scores))
        low = lanes < HEAD_DIM
        down = HEAD_DIM ** (-0.5)
        d_qkv[:, here] = (jnp.concatenate(d_q, axis=0).T * down).astype(bf16)
        d_qkv[:, pl.ds(base + width, pair_width)] = (jnp.where(low, d_k[0], d_k[1]) * down).astype(bf16)
        d_qkv[:, pl.ds(base + 2 * width, pair_width)] = jnp.where(low, d_v[0], d_v[1]).astype(bf16)
        return 0

    lax.fori_loop(0, HEADS // 2, attend, 0)
    first_t = first_ref[...].T
    ones = jnp.ones((8, rows), bf16)
    for i in range(3):
        part = slice(i * width, (i + 1) * width)
        keep(i, dot(first_t, d_qkv[:, part]))
        if i != 1:
            small[2 + i // 2 : 3 + i // 2, :] = dot(ones, d_qkv[:, part])[0:1, :]
        if i > 0:
            advance(i - 1)
    d_first = dot(d_qkv[...], qkv_w_ref[...], NT)
    advance(2)
    n, inverse = standardize(patches_ref[...].astype(f32))
    small[0:1, :] = jnp.sum(d_first * n, axis=0, keepdims=True)
    small[1:2, :] = jnp.sum(d_first, axis=0, keepdims=True)
    copy_t(0).start()
    m = d_first * flat(gain1_ref)
    grad_patches_ref[...] = (
        d_residual_ref[...]
        + inverse * (m - jnp.mean(m, axis=-1, keepdims=True) - n * jnp.mean(m * n, axis=-1, keepdims=True))
    ).astype(bf16)
    own_p.wait()
    for copy in returns:
        copy.wait()
    blocks = 3
    lines = rows // blocks

    def combine(i, _):
        part = pl.ds(pl.multiple_of(i * lines, lines), lines)
        facts = pairs_ref[part, :]
        spots = iota((lines, slots), 1)
        output_ref[part, :] = (
            residual_ref[part, :]
            + facts[:, 2:3] * dot(ones_where(spots == facts[:, 0:1].astype(i32)), recv_p[...])
            + facts[:, 3:4] * dot(ones_where(spots == facts[:, 1:2].astype(i32)), recv_p[...])
        ).astype(bf16)
        return 0

    lax.fori_loop(0, blocks, combine, 0)
    for _ in range(len(bits) + 2):
        for m in [3, 0, 1, 2]:
            advance(m)
        advance_small()
    while todo:
        advance_small()
    small_sums_ref[...] = tiny[0, len(steps) - 1]
    for copy in near:
        copy.wait_send()
    kept.wait()
    for q in range(1, chips):
        for w in range(2):
            copy_f(w, q).wait()
    for m in range(4):
        copy_a(m).wait_send()
        for i in range(len(bits)):
            copy_b(m, i).wait_send()
        for q in range(1, chips):
            copy_c(m, q).wait_send()
        pltpu.make_async_remote_copy(
            sums_ref.at[m, core], sums_ref.at[m, 1 - core], e_ss.at[m], e_rs.at[m], partner, MESH
        ).wait()
    for i in range(len(steps)):
        copy_t(i).wait_send()


def run_back(copies, experts, most, *operands):
    rows, width = operands[8].shape
    slots = experts * most
    chips = copies // 2
    block = operands[3].shape[-1]
    shape = jax.ShapeDtypeStruct
    smalls = -(-(8 + experts) // 16) * 16
    per, half = width // experts, width // 2
    bits = experts.bit_length() - 1
    steps = copies.bit_length() - 1 + bits
    return pl.pallas_call(
        partial(back_kernel, copies, experts, most),
        out_shape=(
            shape((rows, width), bf16),
            shape((rows, width), bf16),
            shape((4, 2, per, half), bf16),
            shape((smalls, width), f32),
            shape((2, width + 16, block), bf16),
            shape((2, chips - 1, width + 16, block), bf16),
        ),
        in_specs=[VMEM] * 2 + [HBM] * 2 + [VMEM] * 15,
        out_specs=(VMEM,) * 4 + (HBM,) * 2,
        scratch_shapes=[
            pltpu.VMEM((slots, width), bf16),
            pltpu.VMEM((2, width + 16, block), bf16),
            pltpu.VMEM((2, chips, width + 16, block), bf16),
            pltpu.VMEM((rows, 3 * width), bf16),
            pltpu.VMEM((rows, width), bf16),
            pltpu.VMEM((width, rows), bf16),
            pltpu.VMEM((rows, width), f32),
            pltpu.VMEM((4, 2, experts, per, half), bf16),
            pltpu.VMEM((smalls, width), f32),
            pltpu.VMEM((4, experts, per, half), bf16),
            pltpu.VMEM((4, experts, per, half), bf16),
            pltpu.VMEM((4, chips - 1, per, half), bf16),
            pltpu.VMEM((2, steps, smalls, width), f32),
            DMA((experts,)), DMA((experts,)),
            DMA((2, chips)), DMA((2, chips)),
            DMA((2, chips)), DMA((2, chips)),
            DMA((2,)), DMA(()),
            DMA((4,)), DMA((4,)),
            DMA((4, bits)), DMA((4, bits)),
            DMA((4, chips)), DMA((4, chips)),
            DMA((4,)), DMA((4,)),
            DMA((steps,)), DMA((steps,)),
        ],
        compiler_params=pltpu.CompilerParams(
            collective_id=2, has_side_effects=True, vmem_limit_bytes=VMEM_BYTES
        ),
        name="back",
    )(*operands)


def finish_kernel(
    copies, experts,
    kept_ref, far_ref, sums_ref, small_ref,
    gain1_ref, bias1_ref, qkv_w_ref, qv_bias_ref, out_w_ref, out_bias_ref, gain2_ref, bias2_ref, router_ref,
    in_w_ref, in_bias_ref, expert_out_ref, expert_out_bias_ref,
    turned, turned_bias,
):
    width = small_ref.shape[1]
    per, half = width // experts, width // 2
    me = lax.axis_index("expert")
    me_dp = lax.axis_index("dp")

    def total(w, part):
        value = kept_ref[w, part, :].astype(f32)
        for q in range(copies // 2 - 1):
            value += far_ref[w, q, part, :].astype(f32)
        return value

    body = slice(0, width)
    in_w_ref[0] = total(0, body)
    expert_out_ref[0] = total(1, body).T
    tail = total(0, slice(width, width + 16))
    in_bias_ref[...] = tail[0:1, :]
    block = tail.shape[1]
    lines = [tail[8 + i : 9 + i, :] for i in range(-(-width // block))]
    bias_row = jnp.concatenate(lines, axis=1)[:, :width]
    turned_bias[...] = jnp.concatenate([bias_row, jnp.zeros((127, width), f32)], axis=0).T
    share = width // copies
    mine = turned_bias[pl.ds(pl.multiple_of(me_dp * share, share), share), :]
    pad = -share % 128
    mine = jnp.concatenate([mine, jnp.zeros((pad, 128), f32)], axis=0) if pad else mine
    expert_out_bias_ref[...] = mine.T[0:1, :share]
    count = small_ref.shape[0]
    turned[...] = jnp.concatenate([small_ref[...], jnp.zeros((128 - count, width), f32)], axis=0).T

    def share_of(start, n):
        value = turned[pl.ds(pl.multiple_of(start, 8), n), :]
        pad = -n % 128
        return (jnp.concatenate([value, jnp.zeros((pad, 128), f32)], axis=0) if pad else value).T

    vectors = share_of(me * per, per)
    for ref, i in [(gain1_ref, 0), (bias1_ref, 1), (out_bias_ref, 4), (gain2_ref, 5), (bias2_ref, 6)]:
        ref[...] = vectors[i : i + 1, :per].reshape(per)
    router_ref[...] = vectors[8 : 8 + experts, :per]
    values = share_of(me % (experts // 2) * 2 * per, 2 * per)
    picked = jnp.where(me < experts // 2, values[2:3, :], values[3:4, :])
    qv_bias_ref[...] = picked[:, : 2 * per].reshape(2 * per)
    for i in range(3):
        for h in range(2):
            qkv_w_ref[:, i * width + h * half : i * width + (h + 1) * half] = sums_ref[i, h].astype(f32)
    for h in range(2):
        out_w_ref[:, h * half : (h + 1) * half] = sums_ref[3, h].astype(f32)


def run_finish(copies, experts, *operands):
    smalls, width = operands[3].shape
    block = operands[0].shape[-1]
    per = width // experts
    shape = jax.ShapeDtypeStruct
    return pl.pallas_call(
        partial(finish_kernel, copies, experts),
        out_shape=(
            shape((per,), f32), shape((per,), f32), shape((per, 3 * width), f32), shape((2 * per,), f32),
            shape((per, width), f32), shape((per,), f32), shape((per,), f32), shape((per,), f32),
            shape((experts, per), f32),
            shape((1, width, block), f32), shape((1, block), f32),
            shape((1, block, width), f32), shape((1, width // copies), f32),
        ),
        in_specs=[VMEM] * 4,
        out_specs=(VMEM,) * 13,
        scratch_shapes=[pltpu.VMEM((width, 128), f32), pltpu.VMEM((width, 128), f32)],
        compiler_params=pltpu.CompilerParams(vmem_limit_bytes=VMEM_BYTES),
        name="finish",
    )(*operands)


def local(
    patches, padding, expert_ids, priority, norm1_gain, norm1_bias, qkv_weight, qv_bias, out_weight,
    out_bias, norm2_gain, norm2_bias, router, expert_in, expert_in_bias, expert_out, expert_out_bias,
    cotangent,
):
    row_count, width = patches.shape
    copies, experts = lax.axis_size("dp"), lax.axis_size("expert")
    total_rows = row_count * copies * experts
    capacity = (210 * total_rows + 100 * experts - 1) // (100 * experts)
    most = 8 * row_count // (3 * experts)
    (recv_cot, x_slots, gate_slots, qkv, att_t, lse, residual, second, first, pairs, probs) = run_front(
        copies, experts, most, capacity,
        patches, cotangent, priority, expert_ids.T, padding, norm1_gain, norm1_bias, qkv_weight, qv_bias,
        out_weight, out_bias, norm2_gain, norm2_bias, router.T,
    )
    d_rows, d_gates, produced, grads = run_experts(
        copies, experts, most,
        x_slots, gate_slots, recv_cot, expert_in[0], expert_in_bias, expert_out[0], expert_out_bias,
    )
    output, grad_patches, sums, small, kept_grads, far_grads = run_back(
        copies, experts, most,
        d_rows, d_gates, produced, grads, pairs, probs,
        second, residual, patches, cotangent, qkv, att_t, lse, first,
        norm1_gain, norm2_gain, qkv_weight, out_weight, router.T,
    )
    (n1_gain, n1_bias, qkv_w, qv, out_w, out_b, n2_gain, n2_bias, router_t, *rest) = run_finish(
        copies, experts, kept_grads, far_grads, sums, small
    )
    return (output, grad_patches, n1_gain, n1_bias, qkv_w, qv, out_w, out_b, n2_gain, n2_bias, router_t.T, *rest)


def solution(mesh):
    tokens = P(("dp", "expert"))
    wide = P(("dp", "expert"), None)
    return jax.shard_map(
        local,
        mesh=mesh,
        in_specs=(
            wide, tokens, wide, tokens, P(), P(), P(), P(), P(), P(), P(), P(), P(),
            P("expert", None, None), P("expert", None), P("expert", None, None), P("expert", None), wide,
        ),
        out_specs=(
            wide, wide, P("expert"), P("expert"), P("expert", None), P("expert"), P("expert", None),
            P("expert"), P("expert"), P("expert"), P("expert", None), P("expert", None, "dp"),
            P("expert", "dp"), P("expert", "dp", None), P("expert", "dp"),
        ),
        check_vma=False,
    )
```

```python
from functools import partial

import jax
import jax.numpy as jnp
from jax import lax
from jax.experimental import pallas as pl
from jax.experimental.pallas import tpu as pltpu
from jax.sharding import PartitionSpec as P

HEADS = 12
HEAD_DIM = 64
SEQ_LEN = 576
LOG2E = 1.4426950408889634
EPS = 1e-06
lane_count = 256
MESH = pl.DeviceIdType.MESH
NN = (((1,), (0,)), ((), ()))
NT = (((1,), (1,)), ((), ()))
TN = (((0,), (0,)), ((), ()))
VMEM_BYTES = 63 << 20
bf16 = jnp.bfloat16
f32 = jnp.float32
i32 = jnp.int32


def dot(a, b, dims=NN):
    return lax.dot_general(a, b, dims, preferred_element_type=f32)


def iota(shape, axis):
    return lax.broadcasted_iota(i32, shape, axis)


def flat(ref):
    return ref[...].reshape(1, ref.shape[0])


def ones_where(mask):
    return jnp.where(mask, 1.0, 0.0).astype(bf16)


def standardize(values):
    centred = values - jnp.mean(values, axis=-1, keepdims=True)
    inverse = lax.rsqrt(jnp.mean(centred * centred, axis=-1, keepdims=True) + EPS)
    return centred * inverse, inverse


def greet(peers):
    barrier = pltpu.get_barrier_semaphore()
    for peer in peers:
        pl.semaphore_signal(barrier, inc=1, device_id=peer, device_id_type=MESH)
    pl.semaphore_wait(barrier, len(peers))


def send(src, dst, send_sem, recv_sem, peer):
    copy = pltpu.make_async_remote_copy(
        src_ref=src, dst_ref=dst, send_sem=send_sem, recv_sem=recv_sem,
        device_id=peer, device_id_type=MESH,
    )
    copy.start()
    return copy


def front_kernel(
    copies, experts, most, capacity,
    patches_hbm, cot_hbm, priority_ref, ids_ref, padding_ref, gain1_ref, bias1_ref, qkv_w_hbm, qv_bias_ref,
    out_w_hbm, out_bias_ref, gain2_ref, bias2_ref, router_ref,
    recv_cot_hbm, raw_hbm, far_slots_ref, x_slots_hbm, gate_slots_ref, qkv_hbm, att_t_hbm, lse_ref,
    residual_hbm, second_hbm, first_t_hbm, pairs_ref, probs_ref,
    patches_ref, cot_ref, qkv_w_ref, out_w_ref, x_slots_ref, qkv_ref, att_t_ref, residual_ref, second_ref,
    first_t_ref, fetch_sem, store_sem, cot_send, rows_ref, line_ref, table, counts, cot_ss, cot_rs, near_ss, near_rs, far_ss, far_rs, raw_sem,
):
    me_dp = lax.axis_index("dp")
    me = lax.axis_index("expert")
    rows, width = patches_ref.shape
    ends = [(cot_hbm, cot_ref), (patches_hbm, patches_ref), (qkv_w_hbm, qkv_w_ref), (out_w_hbm, out_w_ref)]
    fetches = [pltpu.make_async_copy(a, b, fetch_sem.at[i]) for i, (a, b) in enumerate(ends)]
    for fetch in fetches:
        fetch.start()
    ends = [
        (qkv_ref, qkv_hbm), (first_t_ref, first_t_hbm), (att_t_ref, att_t_hbm), (residual_ref, residual_hbm),
        (second_ref, second_hbm), (x_slots_ref, x_slots_hbm),
        (cot_send.at[pl.ds(0, most)], recv_cot_hbm.at[pl.ds(0, most)]),
    ]
    stores = [pltpu.make_async_copy(a, b, store_sem.at[i]) for i, (a, b) in enumerate(ends)]
    rows_ref[0:1, :] = priority_ref[...].reshape(1, rows)
    rows_ref[1:3, :] = ids_ref[...]
    rows_ref[3:4, :] = padding_ref[...].reshape(1, rows)
    rows_ref[4:6, :] = jnp.where(rows_ref[3:4, :] > 0, rows_ref[1:3, :], experts)
    rows_ref[6:, :] = jnp.zeros((2, rows), i32)
    cols = rows_ref[...].T
    starts = range(0, rows, lane_count)
    parts = [(start, min(lane_count, rows - start)) for start in starts]

    def spot(fact, i):
        line = fact * len(parts) + i
        return (line, 0) if line < line_ref.shape[0] else (len(parts) - 1, lane_count // 2)

    line_ref[...] = jnp.zeros_like(line_ref)
    for fact, row in enumerate([0, 4, 5]):
        for i, (start, size) in enumerate(parts):
            line, at = spot(fact, i)
            line_ref[line : line + 1, at : at + size] = rows_ref[row : row + 1, start : start + size]
    greet(
        [(me_dp, me ^ o) for o in range(1, experts)]
        + [(me_dp ^ p, me) for p in range(1, copies)]
    )
    near = [
        send(line_ref, table.at[0, o], near_ss.at[o], near_rs.at[o], (me_dp, me ^ o))
        for o in range(1, experts)
    ]
    table[0, 0] = line_ref[...]
    far_half = experts // 2
    raw = send(cot_hbm, raw_hbm, raw_sem.at[0], raw_sem.at[1], (me_dp, me ^ far_half))
    expert_rows = iota((experts, rows), 0)
    before_t = ones_where(iota((rows, rows), 0) < iota((rows, rows), 1))

    def slot_rows(ids, device):
        ids = ids ^ device
        hits = [expert_rows == ids[k : k + 1, :] for k in range(2)]
        place = dot(ones_where(hits[0] | hits[1]), before_t).astype(i32) + expert_rows * most
        none = ids[0:1, :] >= experts
        return [
            jnp.where(none, -1, jnp.sum(jnp.where(hit, place, 0), axis=0, keepdims=True)) for hit in hits
        ]

    slot0_row, slot1_row = slot_rows(rows_ref[4:6, :], me)
    id0_col, id1_col = cols[:, 1:2], cols[:, 2:3]
    def taken(o):
        slots = iota((most, rows), 0) + o * most
        return ones_where((slots == slot0_row) | (slots == slot1_row))

    fetches[0].wait()
    cot_value = cot_ref[...]
    cots = []
    for o in range(far_half):
        picked = dot(taken(o), cot_value).astype(bf16)
        part = pl.ds(o * most, most)
        cot_send[part, :] = picked
        if o == 0:
            stores[6].start()
            continue
        cots.append(
            send(cot_send.at[part], recv_cot_hbm.at[part], cot_ss.at[o], cot_rs.at[o], (me_dp, me ^ o))
        )
    fetches[1].wait()
    inputs = patches_ref[...].astype(f32)
    first = (standardize(inputs)[0] * flat(gain1_ref) + flat(bias1_ref)).astype(bf16)
    first_t_ref[...] = first.T
    stores[1].start()
    fetches[2].wait()
    qkv_ref[:, :width] = (dot(first, qkv_w_ref[:, :width]) + flat(qv_bias_ref)[:, :width]).astype(bf16)
    qkv_ref[:, width : 2 * width] = dot(first, qkv_w_ref[:, width : 2 * width]).astype(bf16)
    qkv_ref[:, 2 * width :] = (
        dot(first, qkv_w_ref[:, 2 * width :]) + flat(qv_bias_ref)[:, width:]
    ).astype(bf16)
    stores[0].start()
    key_bias = jnp.where(cols[:, 3:4] > 0, 0.0, -1e30)
    scale = LOG2E * HEAD_DIM ** (-0.5)
    pair_width = 2 * HEAD_DIM

    far = [
        pltpu.make_async_remote_copy(
            table.at[0], table.at[p], far_ss.at[p], far_rs.at[p], (me_dp ^ p, me), MESH
        )
        for p in range(1, copies)
    ]

    def attend(pair, _):
        @pl.when(pair == 5)
        def _():
            for near_copy in near:
                near_copy.wait_recv()
            for far_copy in far:
                far_copy.start()

        base = pl.multiple_of(pair * pair_width, pair_width)
        q = qkv_ref[:, pl.ds(base, pair_width)]
        k = qkv_ref[:, pl.ds(base + width, pair_width)]
        v_t = qkv_ref[:, pl.ds(base + 2 * width, pair_width)].T
        lanes = iota((rows, pair_width), 1)
        outs, stats = [], []
        for a in range(2):
            k_a = jnp.where((lanes >= HEAD_DIM) == (a == 1), k, jnp.zeros((), bf16))
            scores = dot(k_a, q, NT) + key_bias
            peak = jnp.max(scores, axis=0, keepdims=True)
            raised = jnp.exp2(scores * scale - peak * scale)
            total = jnp.sum(raised, axis=0, keepdims=True)
            out = dot(v_t[a * HEAD_DIM : (a + 1) * HEAD_DIM, :], raised.astype(bf16))
            outs.append(out / total)
            stats.append(peak * scale + jnp.log2(total))
        att_t_ref[pl.ds(base, pair_width), :] = jnp.concatenate(outs, axis=0).astype(bf16)
        lse_ref[pair] = jnp.concatenate(stats + [jnp.zeros((6, rows), f32)], axis=0)
        return 0

    lax.fori_loop(0, HEADS // 2, attend, 0)
    rel0_col, rel1_col = cols[:, 4:5] ^ me, cols[:, 5:6] ^ me
    expert_cols = iota((rows, experts), 1)
    named = ones_where((expert_cols == rel0_col) | (expert_cols == rel1_col))
    before = ones_where(iota((rows, rows), 1) < iota((rows, rows), 0))
    place = dot(before, named).astype(i32) + expert_cols * most
    slot0_col = jnp.sum(jnp.where(expert_cols == rel0_col, place, 0), axis=1, keepdims=True)
    slot1_col = jnp.sum(jnp.where(expert_cols == rel1_col, place, 0), axis=1, keepdims=True)
    none_col = cols[:, 4:5] >= experts
    slot0_col, slot1_col = jnp.where(none_col, -1, slot0_col), jnp.where(none_col, -1, slot1_col)

    far_line = table[0, far_half]
    far_codes = []
    for fact in (1, 2):
        spots = [(spot(fact, i), size) for i, (start, size) in enumerate(parts)]
        pieces = [far_line[line : line + 1, at : at + size] for (line, at), size in spots]
        far_codes.append(jnp.concatenate(pieces, axis=1))
    far0_row, far1_row = slot_rows(jnp.concatenate(far_codes, axis=0), me ^ far_half)
    far_slots_ref[...] = jnp.concatenate([far0_row, far1_row, jnp.zeros((6, rows), i32)], axis=0)
    stores[2].start()
    fetches[3].wait()
    residual = inputs + dot(att_t_ref[...], out_w_ref[...], TN) + flat(out_bias_ref)
    residual_ref[...] = residual
    stores[3].start()
    second = (standardize(residual)[0] * flat(gain2_ref) + flat(bias2_ref)).astype(bf16)
    second_ref[...] = second
    stores[4].start()
    for o in range(experts):
        x_slots_ref[pl.ds(o * most, most), :] = dot(taken(o), second).astype(bf16)
    stores[5].start()
    logits = dot(second, router_ref[...], NT)
    raised = jnp.exp(logits - jnp.max(logits, axis=-1, keepdims=True))
    probs = raised / jnp.sum(raised, axis=-1, keepdims=True)
    probs_ref[...] = probs
    prob0 = jnp.sum(jnp.where(expert_cols == id0_col, probs, 0.0), axis=1, keepdims=True)
    prob1 = jnp.sum(jnp.where(expert_cols == id1_col, probs, 0.0), axis=1, keepdims=True)
    both = prob0 + prob1
    gate0, gate1 = prob0 / both, prob1 / both
    for far_copy in far:
        far_copy.wait_recv()
    counts[...] = jnp.zeros_like(counts)
    rank_col = cols[:, 0:1]

    def count(block, _):
        entry = table[block // experts, block % experts]
        ahead = jnp.zeros((rows, 2 * experts), f32)
        loads = jnp.zeros((8, 2 * experts), f32)
        for i, (start, size) in enumerate(parts):

            def fact(k):
                line, at = spot(k, i)
                return entry[line : line + 1, at : at + size]

            names = iota((experts, size), 0)
            hits = jnp.concatenate([ones_where(names == fact(1)), ones_where(names == fact(2))], axis=0)
            ahead += dot(ones_where(fact(0) < rank_col), hits, NT)
            loads += dot(jnp.ones((8, size), bf16), hits, NT)
        counts[:rows, :] += ahead
        counts[rows:, :] += loads
        return 0

    lax.fori_loop(0, copies * experts, count, 0)
    both_cols = iota((rows, 2 * experts), 1)
    ahead = counts[:rows, :]
    loads = counts[rows : rows + 1, :]
    position0 = jnp.sum(jnp.where(both_cols == id0_col, ahead, 0.0), axis=1, keepdims=True)
    position1 = jnp.sum(
        jnp.where(both_cols == id1_col + experts, ahead, 0.0)
        + jnp.where(both_cols == id1_col, loads, 0.0),
        axis=1,
        keepdims=True,
    )
    real_col = cols[:, 3:4] > 0
    kept0 = jnp.where(real_col & (position0 < capacity), 1.0, 0.0)
    kept1 = jnp.where(real_col & (position1 < capacity), 1.0, 0.0)
    gate0, gate1 = gate0 * kept0, gate1 * kept1
    for o in range(experts):
        slots = iota((rows, most), 1) + o * most
        gates = jnp.where(slots == slot0_col, gate0, 0.0) + jnp.where(slots == slot1_col, gate1, 0.0)
        gate_slots_ref[o] = jnp.sum(gates, axis=0, keepdims=True)
    lanes = iota((rows, 16), 1)
    columns = [slot0_col, slot1_col, gate0, gate1, kept0, kept1, both, cols[:, 3:4], id0_col, id1_col]
    columns = [column.astype(f32) for column in columns]
    packed = jnp.zeros((rows, 16), f32)
    for i, column in enumerate(columns):
        packed = jnp.where(lanes == i, column, packed)
    pairs_ref[...] = packed
    for copy in near + far:
        copy.wait_send()
    for copy in [*cots, raw, *stores]:
        copy.wait()


VMEM = pl.BlockSpec(memory_space=pltpu.VMEM)
HBM = pl.BlockSpec(memory_space=pl.ANY)
DMA = pltpu.SemaphoreType.DMA


def run_front(copies, experts, most, capacity, *operands):
    rows, width = operands[0].shape
    slots = experts * most
    shape = jax.ShapeDtypeStruct
    return pl.pallas_call(
        partial(front_kernel, copies, experts, most, capacity),
        out_shape=(
            shape((slots // 2, width), bf16),
            shape((rows, width), bf16),
            shape((8, rows), i32),
            shape((slots, width), bf16),
            shape((experts, 1, most), f32),
            shape((rows, 3 * width), bf16),
            shape((width, rows), bf16),
            shape((HEADS // 2, 8, rows), f32),
            shape((rows, width), f32),
            shape((rows, width), bf16),
            shape((width, rows), bf16),
            shape((rows, 16), f32),
            shape((rows, experts), f32),
        ),
        in_specs=[HBM] * 2 + [VMEM] * 5 + [HBM, VMEM, HBM] + [VMEM] * 4,
        out_specs=(HBM, HBM, VMEM, HBM, VMEM, HBM, HBM, VMEM, HBM, HBM, HBM, VMEM, VMEM),
        scratch_shapes=[
            pltpu.VMEM((rows, width), bf16),
            pltpu.VMEM((rows, width), bf16),
            pltpu.VMEM((width, 3 * width), bf16),
            pltpu.VMEM((width, width), bf16),
            pltpu.VMEM((slots, width), bf16),
            pltpu.VMEM((rows, 3 * width), bf16),
            pltpu.VMEM((width, rows), bf16),
            pltpu.VMEM((rows, width), f32),
            pltpu.VMEM((rows, width), bf16),
            pltpu.VMEM((width, rows), bf16),
            DMA((4,)), DMA((7,)),
            pltpu.VMEM((slots // 2, width), bf16),
            pltpu.VMEM((8, rows), i32),
            pltpu.VMEM((8, lane_count), i32),
            pltpu.VMEM((copies, experts, 8, lane_count), i32),
            pltpu.VMEM((rows + 8, 2 * experts), f32),
            DMA((experts,)), DMA((experts,)),
            DMA((experts,)), DMA((experts,)),
            DMA((copies,)), DMA((copies,)), DMA((2,)),
        ],
        compiler_params=pltpu.CompilerParams(
            collective_id=0, has_side_effects=True, vmem_limit_bytes=VMEM_BYTES
        ),
        name="front",
    )(*operands)


def gelu_parts(values):
    bell = jnp.exp2(values * values * (-0.5 * LOG2E))
    t = 1.0 / (1.0 + (0.3275911 * 0.5**0.5) * jnp.abs(values))
    tail = t * (0.1274147959 + t * (-0.142248368 + t * (0.7107068705 + t * (-0.7265760135 + t * 0.5307027145))))
    tail = tail * bell
    share = jnp.where(values >= 0, 1.0 - tail, tail)
    return values * share, share + values * bell * 0.3989422804014327


def to_column(row):
    n = row.shape[1]
    return jnp.sum(jnp.where(iota((n, n), 0) == iota((n, n), 1), row, 0.0), axis=1, keepdims=True)


def to_row(column):
    n = column.shape[0]
    return jnp.sum(jnp.where(iota((n, n), 0) == iota((n, n), 1), column, 0.0), axis=0, keepdims=True)


def expert_kernel(
    copies, experts, most, chunks, tile,
    x_ref, gates_ref, near_cot_ref, raw_ref, far_slots_ref, in_w_hbm, in_bias_ref, out_w_hbm, out_bias_ref,
    d_rows_ref, d_gates_ref, produced_ref, grads_ref,
    in_w_ref, out_w_ref, cot_ref, send_cot, recv_x, recv_g, send_d, send_g, hidden, d_pre, x_t, d_t, bias_sum, total_p, total_d, stage,
    x_ss, x_rs, g_ss, g_rs, d_ss, d_rs, dg_ss, dg_rs, own_sem, own_d_sem, stage_sem,
    cot_ss, cot_rs, near_sem, fetch_sem,
):
    me_dp = lax.axis_index("dp")
    me = lax.axis_index("expert")
    width, hidden_width = in_w_ref.shape
    rows = chunks * most
    block = hidden_width // copies

    def chunk(o):
        return pl.ds(pl.multiple_of(o * most, most), most)

    def move_x(o):
        return pltpu.make_async_remote_copy(
            x_ref.at[chunk(o)], recv_x.at[chunk(o)], x_ss.at[o], x_rs.at[o], (me_dp, me ^ o), MESH
        )

    def move_g(o):
        return pltpu.make_async_remote_copy(
            gates_ref.at[o], recv_g.at[o], g_ss.at[o], g_rs.at[o], (me_dp, me ^ o), MESH
        )

    def move_d(o):
        return pltpu.make_async_remote_copy(
            send_d.at[chunk(o)], d_rows_ref.at[chunk(o)], d_ss.at[o], d_rs.at[o], (me_dp, me ^ o), MESH
        )

    def move_dg(o):
        return pltpu.make_async_remote_copy(
            send_g.at[o], d_gates_ref.at[o], dg_ss.at[o], dg_rs.at[o], (me_dp, me ^ o), MESH
        )

    far_half = experts // 2

    def move_cot(j):
        return pltpu.make_async_remote_copy(
            send_cot.at[chunk(j)], cot_ref.at[chunk(far_half + j)], cot_ss.at[j], cot_rs.at[j],
            (me_dp, me ^ j), MESH,
        )

    fetches = [
        pltpu.make_async_copy(in_w_hbm, in_w_ref, fetch_sem.at[0]),
        pltpu.make_async_copy(out_w_hbm, out_w_ref, fetch_sem.at[1]),
    ]
    for fetch in fetches:
        fetch.start()
    own = pltpu.make_async_copy(x_ref.at[chunk(0)], recv_x.at[chunk(0)], own_sem)
    own.start()
    half_slots = near_cot_ref.shape[0]
    near_cot = pltpu.make_async_copy(near_cot_ref, cot_ref.at[pl.ds(0, half_slots)], near_sem)
    near_cot.start()
    greet([(me_dp, me ^ o) for o in range(1, experts)])

    def begin(g):
        for o in range(max(1, g * chunks), (g + 1) * chunks):
            move_g(o).start()
            move_x(o).start()

    groups = experts // chunks
    order = [0, *range(groups // 2, groups), *range(1, groups // 2)]
    begin(order[0])
    begin(order[1])
    for j in [*range(1, far_half), 0]:
        places = iota((most, raw_ref.shape[0]), 0) + (far_half + j) * most
        taken = ones_where((places == far_slots_ref[0:1, :]) | (places == far_slots_ref[1:2, :]))
        picked = dot(taken, raw_ref[...]).astype(bf16)
        if j == 0:
            cot_ref[chunk(far_half), :] = picked
        else:
            send_cot[chunk(j), :] = picked
            move_cot(j).start()
    near_cot.wait()
    for fetch in fetches:
        fetch.wait()
    recv_g[0] = gates_ref[0]
    bias_sum[...] = jnp.zeros_like(bias_sum)
    x_t[width:, :] = jnp.ones_like(x_t[width:, :])
    own.wait()
    own_d = pltpu.make_async_copy(send_d.at[chunk(0)], d_rows_ref.at[chunk(0)], own_d_sem)

    def work(n, _):
        g = n % 2 * (groups // 2) + n // 2
        for j in range(chunks):
            o = g * chunks + j

            @pl.when(o > 0)
            def _():
                move_g(o).wait_recv()
                move_x(o).wait_recv()

            @pl.when(o > far_half)
            def _():
                move_cot(o - far_half).wait_recv()

        at = pl.multiple_of(g * rows, rows)
        here = pl.ds(at, rows)
        gate = jnp.concatenate([to_column(recv_g[g * chunks + j]) for j in range(chunks)], axis=0)
        x = recv_x[here, :]
        cot = cot_ref[here, :].astype(f32)
        d_produced = (cot * gate).astype(bf16)
        bias_sum[0:1, :] += jnp.sum(d_produced.astype(f32), axis=0, keepdims=True)
        x_t[:width, here] = x.T
        d_t[:, here] = d_produced.T
        total_p[...] = jnp.zeros_like(total_p)
        total_d[...] = jnp.zeros_like(total_d)

        def step(n, _):
            cols = pl.ds(pl.multiple_of(n * tile, tile), tile)
            pre = dot(x, in_w_ref[:, cols]) + in_bias_ref[:, cols]
            value, slope = gelu_parts(pre)
            value = value.astype(bf16)
            hidden[here, cols] = value
            total_p[...] += dot(value, out_w_ref[cols, :])
            d_value = (dot(d_produced, out_w_ref[cols, :], NT) * slope).astype(bf16)
            d_pre[here, cols] = d_value
            total_d[...] += dot(d_value, in_w_ref[:, cols], NT)
            return 0

        lax.fori_loop(0, hidden_width // tile, step, 0)

        @pl.when(n == 0)
        def _():
            for later in order[2:]:
                begin(later)

        send_d[here, :] = total_d[...].astype(bf16)
        produced = (total_p[...] + out_bias_ref[...]).astype(bf16)
        produced_ref[here, :] = produced
        d_gate = jnp.sum(produced.astype(f32) * cot, axis=1, keepdims=True)
        for j in range(chunks):
            o = g * chunks + j
            d_gate_row = to_row(d_gate[j * most : (j + 1) * most, :])
            send_g[o] = d_gate_row

            @pl.when(o > 0)
            def _():
                move_d(o).start()
                move_dg(o).start()

            @pl.when(o == 0)
            def _():
                own_d.start()
                d_gates_ref[0] = d_gate_row

        return 0

    lax.fori_loop(0, groups, work, 0)

    def store(w, p):
        return pltpu.make_async_copy(stage.at[w], grads_ref.at[w, p], stage_sem.at[w])

    def weigh(p, _):
        cols = pl.ds(pl.multiple_of((me_dp ^ p) * block, block), block)

        @pl.when(p > 0)
        def _():
            store(0, p - 1).wait()

        total = dot(x_t[...], d_pre[:, cols])
        stage[0, :width, :] = total[:width, :].astype(bf16)
        tail = total[width:, :]
        lines = iota((16, block), 0)
        for i in range(-(-width // block)):
            tail = jnp.where(lines == 8 + i, bias_sum[0:1, i * block : (i + 1) * block], tail)
        stage[0, width:, :] = tail.astype(bf16)
        store(0, p).start()

        @pl.when(p > 0)
        def _():
            store(1, p - 1).wait()

        stage[1, :width, :] = dot(d_t[...], hidden[:, cols]).astype(bf16)
        stage[1, width:, :] = jnp.zeros((16, block), bf16)
        store(1, p).start()
        return 0

    lax.fori_loop(0, copies, weigh, 0)
    store(0, copies - 1).wait()
    store(1, copies - 1).wait()
    own_d.wait()
    for j in range(1, far_half):
        move_cot(j).wait_send()
    for o in range(1, experts):
        move_g(o).wait_send()
        move_x(o).wait_send()
        move_d(o).wait()
        move_dg(o).wait()


def run_experts(copies, experts, most, *operands):
    slots, width = operands[0].shape
    hidden_width = operands[5].shape[1]
    chunks = max(1, min(experts, 384 // most))
    rows = chunks * most
    block = hidden_width // copies
    shape = jax.ShapeDtypeStruct
    return pl.pallas_call(
        partial(expert_kernel, copies, experts, most, chunks, 512),
        out_shape=(
            shape((slots, width), bf16),
            shape((experts, 1, most), f32),
            shape((slots, width), bf16),
            shape((2, copies, width + 16, block), bf16),
        ),
        in_specs=[HBM, VMEM, HBM] + [VMEM] * 2 + [HBM, VMEM] * 2,
        out_specs=(HBM, VMEM, VMEM, HBM),
        scratch_shapes=[
            pltpu.VMEM((width, hidden_width), bf16),
            pltpu.VMEM((hidden_width, width), bf16),
            pltpu.VMEM((slots, width), bf16),
            pltpu.VMEM((slots // 2, width), bf16),
            pltpu.VMEM((slots, width), bf16),
            pltpu.VMEM((experts, 1, most), f32),
            pltpu.VMEM((slots, width), bf16),
            pltpu.VMEM((experts, 1, most), f32),
            pltpu.VMEM((slots, hidden_width), bf16),
            pltpu.VMEM((slots, hidden_width), bf16),
            pltpu.VMEM((width + 16, slots), bf16),
            pltpu.VMEM((width, slots), bf16),
            pltpu.VMEM((8, width), f32),
            pltpu.VMEM((rows, width), f32),
            pltpu.VMEM((rows, width), f32),
            pltpu.VMEM((2, width + 16, block), bf16),
        ]
        + [DMA((experts,))] * 8
        + [DMA(()), DMA(()), DMA((2,)), DMA((experts // 2,)), DMA((experts // 2,)), DMA(()), DMA((2,))],
        compiler_params=pltpu.CompilerParams(
            collective_id=1, has_side_effects=True, vmem_limit_bytes=VMEM_BYTES
        ),
        name="experts",
    )(*operands)


def back_kernel(
    copies, experts, most,
    d_rows_hbm, d_gates_ref, produced_ref, grads_ref, pairs_ref, probs_ref,
    second_hbm, residual_hbm, patches_hbm, cot_hbm, qkv_hbm, att_t_hbm, lse_ref, first_t_hbm,
    gain1_ref, gain2_ref, qkv_w_hbm, out_w_hbm, router_ref,
    output_ref, grad_patches_ref, sums_ref, small_sums_ref, kept_grads_ref, far_grads_ref,
    d_rows_ref, second_ref, residual_ref, cot_ref, att_t_ref, out_w_ref, qkv_ref, first_t_ref, qkv_w_ref,
    patches_ref, fetch_sem,
    recv_p, own_grads, near_grads, d_qkv, d_att, d_att_t, d_residual_ref,
    dense, small, halves, landed, crossed, tiny,
    p_ss, p_rs, n_ss, n_rs, f_ss, f_rs, own_sem, kept_sem,
    a_ss, a_rs, b_ss, b_rs, c_ss, c_rs, e_ss, e_rs, t_ss, t_rs,
):
    me_dp = lax.axis_index("dp")
    me = lax.axis_index("expert")
    rows, width = patches_ref.shape
    ends = [
        (d_rows_hbm, d_rows_ref), (second_hbm, second_ref), (residual_hbm, residual_ref), (cot_hbm, cot_ref),
        (att_t_hbm, att_t_ref), (out_w_hbm, out_w_ref), (qkv_hbm, qkv_ref), (first_t_hbm, first_t_ref),
        (qkv_w_hbm, qkv_w_ref), (patches_hbm, patches_ref),
    ]
    fetches = [pltpu.make_async_copy(a, b, fetch_sem.at[i]) for i, (a, b) in enumerate(ends)]
    for fetch in fetches:
        fetch.start()
    slots = experts * most
    chips = copies // 2
    core = me_dp % 2
    per = width // experts
    half = width // 2
    partner = (me_dp ^ 1, me)
    bits = [1, 0, *range(2, experts.bit_length() - 1)]
    turns_of = [bits, [0, 1, *bits[2:]], bits, bits]
    steps = [(me_dp ^ (1 << i), me) for i in range(copies.bit_length() - 1)]
    steps += [(me_dp, me ^ (1 << i)) for i in range(experts.bit_length() - 1)]

    def copy_a(m):
        return pltpu.make_async_remote_copy(
            dense.at[m, 1 - core], halves.at[m], a_ss.at[m], a_rs.at[m], partner, MESH
        )

    def copy_b(m, i):
        part = pl.ds(experts >> (i + 1), experts >> (i + 1))
        return pltpu.make_async_remote_copy(
            dense.at[m, core, part], landed.at[m, part], b_ss.at[m, i], b_rs.at[m, i],
            (me_dp, me ^ (1 << turns_of[m][i])), MESH,
        )

    def copy_c(m, q):
        return pltpu.make_async_remote_copy(
            dense.at[m, core, 0], crossed.at[m, q - 1], c_ss.at[m, q], c_rs.at[m, q],
            (me_dp ^ (2 * q), me), MESH,
        )

    def copy_e(m):
        return pltpu.make_async_remote_copy(
            sums_ref.at[m, core], sums_ref.at[m, core], e_ss.at[m], e_rs.at[m], partner, MESH
        )

    def begin(m, k):
        if k == 0:
            copy_a(m).start()
        elif k <= len(bits):
            copy_b(m, k - 1).start()
        elif k == len(bits) + 1:
            for q in range(1, chips):
                copy_c(m, q).start()
        else:
            copy_e(m).start()

    def end(m, k):
        if k == 0:
            copy_a(m).wait_recv()
            dense[m, core] = (dense[m, core].astype(f32) + halves[m].astype(f32)).astype(bf16)
        elif k <= len(bits):
            copy_b(m, k - 1).wait_recv()
            n = experts >> k
            total = dense[m, core, 0:n].astype(f32) + landed[m, n : 2 * n].astype(f32)
            dense[m, core, 0:n] = total.astype(bf16)
        elif k == len(bits) + 1:
            total = dense[m, core, 0].astype(f32)
            for q in range(1, chips):
                copy_c(m, q).wait_recv()
                total += crossed[m, q - 1].astype(f32)
            sums_ref[m, core] = total.astype(bf16)

    stages = [0] * 4

    def advance(m):
        if stages[m] < len(bits) + 2:
            end(m, stages[m])
            stages[m] += 1
            begin(m, stages[m])

    def copy_t(i):
        src = small if i == 0 else tiny.at[0, i - 1]
        return pltpu.make_async_remote_copy(src, tiny.at[1, i], t_ss.at[i], t_rs.at[i], steps[i], MESH)

    todo = list(range(len(steps)))

    def advance_small():
        if todo:
            i = todo.pop(0)
            copy_t(i).wait_recv()
            mine = small[...] if i == 0 else tiny[0, i - 1]
            tiny[0, i] = mine + tiny[1, i]
            if i + 1 < len(steps):
                copy_t(i + 1).start()

    def copy_f(w, q):
        return pltpu.make_async_remote_copy(
            near_grads.at[w, q], far_grads_ref.at[w, q - 1], f_ss.at[w, q], f_rs.at[w, q],
            (me_dp ^ (2 * q), me), MESH,
        )

    greet(
        [(me_dp, me ^ o) for o in range(1, experts)]
        + [partner]
        + [(me_dp ^ (2 * q), me) for q in range(1, chips)]
    )
    near = [
        send(grads_ref.at[w, 2 * q + 1], near_grads.at[w, q], n_ss.at[w, q], n_rs.at[w, q], partner)
        for q in range(chips)
        for w in range(2)
    ]
    turns = [(w, q) for q in [*range(1, chips), 0] for w in range(2)]
    own = [
        pltpu.make_async_copy(grads_ref.at[w, 2 * q], own_grads.at[i % 2], own_sem.at[i % 2])
        for i, (w, q) in enumerate(turns)
    ]
    for copy in own[:2]:
        copy.start()
    returns = []
    for o in range(1, experts):
        part = pl.ds(o * most, most)
        returns.append(
            send(produced_ref.at[part], recv_p.at[part], p_ss.at[o], p_rs.at[o], (me_dp, me ^ o))
        )
    own_p = pltpu.make_async_copy(
        produced_ref.at[pl.ds(0, most)], recv_p.at[pl.ds(0, most)], p_rs.at[0]
    )
    own_p.start()
    slot0, slot1 = pairs_ref[:, 0:1].astype(i32), pairs_ref[:, 1:2].astype(i32)
    kept0, kept1, both = pairs_ref[:, 4:5], pairs_ref[:, 5:6], pairs_ref[:, 6:7]
    places = iota((rows, slots), 1)
    fetches[0].wait()
    d_second = dot(ones_where((places == slot0) | (places == slot1)), d_rows_ref[...])
    d_gate0 = jnp.zeros((rows, 1), f32)
    d_gate1 = jnp.zeros((rows, 1), f32)
    for o in range(experts):
        part = iota((rows, most), 1) + o * most
        line = d_gates_ref[o]
        d_gate0 += jnp.sum(jnp.where(part == slot0, line, 0.0), axis=1, keepdims=True)
        d_gate1 += jnp.sum(jnp.where(part == slot1, line, 0.0), axis=1, keepdims=True)
    d_gate0, d_gate1 = d_gate0 * kept0, d_gate1 * kept1
    probs = probs_ref[...]
    names = iota((rows, experts), 1)
    is0, is1 = names == pairs_ref[:, 8:9].astype(i32), names == pairs_ref[:, 9:10].astype(i32)
    share0 = jnp.sum(jnp.where(is0, probs, 0.0), axis=1, keepdims=True) / both
    share1 = jnp.sum(jnp.where(is1, probs, 0.0), axis=1, keepdims=True) / both
    centre = d_gate0 * share0 + d_gate1 * share1
    d_probs = jnp.where(is0, (d_gate0 - centre) / both, 0.0) + jnp.where(is1, (d_gate1 - centre) / both, 0.0)
    d_logits = (probs * (d_probs - jnp.sum(probs * d_probs, axis=1, keepdims=True))).astype(bf16)
    small[8:, :] = jnp.zeros_like(small[8:, :])
    fetches[1].wait()
    small[8 : 8 + experts, :] = dot(d_logits, second_ref[...], TN)
    d_second += dot(d_logits, router_ref[...])
    fetches[2].wait()
    fetches[3].wait()
    n, inverse = standardize(residual_ref[...])
    small[5:6, :] = jnp.sum(d_second * n, axis=0, keepdims=True)
    small[6:7, :] = jnp.sum(d_second, axis=0, keepdims=True)
    m = d_second * flat(gain2_ref)
    d_residual = cot_ref[...].astype(f32) + inverse * (
        m - jnp.mean(m, axis=-1, keepdims=True) - n * jnp.mean(m * n, axis=-1, keepdims=True)
    )
    d_residual_ref[...] = d_residual
    d_branch = d_residual.astype(bf16)
    small[4:5, :] = jnp.sum(d_branch.astype(f32), axis=0, keepdims=True)
    small[7:8, :] = jnp.zeros((1, width), f32)

    def keep(matrix, h, value):
        for e in range(experts):
            r = e ^ me
            at = 0
            for bit in turns_of[matrix]:
                at = at * 2 + (r // (1 << bit)) % 2
            dense[matrix, h, at] = value[e * per : (e + 1) * per, :].astype(bf16)

    fetches[4].wait()
    for h in range(2):
        keep(3, h, dot(att_t_ref[...], d_branch[:, h * half : (h + 1) * half]))
    begin(3, 0)
    for copy in near:
        copy.wait_recv()
    for i, (w, q) in enumerate(turns):
        own[i].wait()
        near_grads[w, q] = (own_grads[i % 2].astype(f32) + near_grads[w, q].astype(f32)).astype(bf16)
        if i + 2 < len(turns):
            own[i + 2].start()
        if q > 0:
            copy_f(w, q).start()
    kept = pltpu.make_async_copy(near_grads.at[:, 0], kept_grads_ref, kept_sem)
    kept.start()
    advance(3)
    fetches[5].wait()
    d_att[...] = dot(d_branch, out_w_ref[...], NT).astype(bf16)
    d_att_t[...] = dot(out_w_ref[...], d_branch, NT).astype(bf16)
    key_bias = jnp.where(pairs_ref[:, 7:8] > 0, 0.0, -1e30)
    scale = LOG2E * HEAD_DIM ** (-0.5)
    pair_width = 2 * HEAD_DIM

    def columns(i, h):
        return slice(i * width + h * half, i * width + (h + 1) * half)

    def attend(pair, _):
        @pl.when(pair == 3)
        def _():
            for i in range(3):
                keep(i, 0, dot(first_t_ref[...], d_qkv[:, columns(i, 0)]))

                @pl.when(core == 1)
                def _():
                    begin(i, 0)

        @pl.when((pair == 5) & (core == 0))
        def _():
            for i in range(3):
                end(i, 0)
                begin(i, 1)

        base = pl.multiple_of(pair * pair_width, pair_width)
        here = pl.ds(base, pair_width)
        q = qkv_ref[:, here]
        k = qkv_ref[:, pl.ds(base + width, pair_width)]
        v = qkv_ref[:, pl.ds(base + 2 * width, pair_width)]
        k_t = k.T
        d_out = d_att[:, here]
        products = att_t_ref[here, :].astype(f32) * d_att_t[here, :].astype(f32)
        lanes = iota((rows, pair_width), 1)
        d_q, d_k, d_v = [], [], []
        for a in range(2):
            mine = (lanes >= HEAD_DIM) == (a == 1)
            k_a = jnp.where(mine, k, jnp.zeros((), bf16))
            v_a = jnp.where(mine, v, jnp.zeros((), bf16))
            part = slice(a * HEAD_DIM, (a + 1) * HEAD_DIM)
            delta = jnp.sum(products[part, :], axis=0, keepdims=True)
            weights = jnp.exp2((dot(k_a, q, NT) + key_bias) * scale - lse_ref[pair][a : a + 1, :])
            d_scores = (weights * (dot(v_a, d_out, NT) - delta)).astype(bf16)
            d_v.append(dot(weights.astype(bf16), d_out))
            d_k.append(dot(d_scores, q))
            d_q.append(dot(k_t[part, :], d_scores))
        low = lanes < HEAD_DIM
        down = HEAD_DIM ** (-0.5)
        d_qkv[:, here] = (jnp.concatenate(d_q, axis=0).T * down).astype(bf16)
        d_qkv[:, pl.ds(base + width, pair_width)] = (jnp.where(low, d_k[0], d_k[1]) * down).astype(bf16)
        d_qkv[:, pl.ds(base + 2 * width, pair_width)] = jnp.where(low, d_v[0], d_v[1]).astype(bf16)
        return 0

    fetches[6].wait()
    fetches[7].wait()
    lax.fori_loop(0, HEADS // 2, attend, 0)
    for fetch in fetches[8:]:
        fetch.wait()
    def combine_results():
        own_p.wait()
        for copy in returns:
            copy.wait()
        blocks = 3
        lines = rows // blocks

        def combine(i, _):
            part = pl.ds(pl.multiple_of(i * lines, lines), lines)
            facts = pairs_ref[part, :]
            spots = iota((lines, slots), 1)
            output_ref[part, :] = (
                residual_ref[part, :]
                + facts[:, 2:3] * dot(ones_where(spots == facts[:, 0:1].astype(i32)), recv_p[...])
                + facts[:, 3:4] * dot(ones_where(spots == facts[:, 1:2].astype(i32)), recv_p[...])
            ).astype(bf16)
            return 0

        lax.fori_loop(0, blocks, combine, 0)

    ones = jnp.ones((8, rows), bf16)
    for i in range(3):
        keep(i, 1, dot(first_t_ref[...], d_qkv[:, columns(i, 1)]))

        @pl.when(core == 0)
        def _():
            begin(i, 0)

        if i > 0:

            @pl.when(core == 1)
            def _():
                end(i - 1, 0)
                begin(i - 1, 1)

    for i in (0, 2):
        part = slice(i * width, (i + 1) * width)
        small[2 + i // 2 : 3 + i // 2, :] = dot(ones, d_qkv[:, part])[0:1, :]

    @pl.when(core == 1)
    def _():
        end(2, 0)
        begin(2, 1)

    stages[0:3] = [1, 1, 1]
    d_first = dot(d_qkv[...], qkv_w_ref[...], NT)
    n, inverse = standardize(patches_ref[...].astype(f32))
    small[0:1, :] = jnp.sum(d_first * n, axis=0, keepdims=True)
    small[1:2, :] = jnp.sum(d_first, axis=0, keepdims=True)
    copy_t(0).start()
    m = d_first * flat(gain1_ref)
    grad_patches_ref[...] = (
        d_residual_ref[...]
        + inverse * (m - jnp.mean(m, axis=-1, keepdims=True) - n * jnp.mean(m * n, axis=-1, keepdims=True))
    ).astype(bf16)
    for turn in range(len(bits) + 2):
        for m in [3, 0, 1, 2]:
            advance(m)
        advance_small()
        if turn == 0:
            combine_results()
    while todo:
        advance_small()
    small_sums_ref[...] = tiny[0, len(steps) - 1]
    for copy in near:
        copy.wait_send()
    kept.wait()
    for q in range(1, chips):
        for w in range(2):
            copy_f(w, q).wait()
    for m in range(4):
        copy_a(m).wait_send()
        for i in range(len(bits)):
            copy_b(m, i).wait_send()
        for q in range(1, chips):
            copy_c(m, q).wait_send()
        pltpu.make_async_remote_copy(
            sums_ref.at[m, core], sums_ref.at[m, 1 - core], e_ss.at[m], e_rs.at[m], partner, MESH
        ).wait()
    for i in range(len(steps)):
        copy_t(i).wait_send()


def run_back(copies, experts, most, *operands):
    rows, width = operands[8].shape
    slots = experts * most
    chips = copies // 2
    block = operands[3].shape[-1]
    shape = jax.ShapeDtypeStruct
    smalls = -(-(8 + experts) // 16) * 16
    per, half = width // experts, width // 2
    bits = experts.bit_length() - 1
    steps = copies.bit_length() - 1 + bits
    return pl.pallas_call(
        partial(back_kernel, copies, experts, most),
        out_shape=(
            shape((rows, width), bf16),
            shape((rows, width), bf16),
            shape((4, 2, per, half), bf16),
            shape((smalls, width), f32),
            shape((2, width + 16, block), bf16),
            shape((2, chips - 1, width + 16, block), bf16),
        ),
        in_specs=[HBM, VMEM, HBM, HBM, VMEM, VMEM] + [HBM] * 6 + [VMEM, HBM, VMEM, VMEM, HBM, HBM, VMEM],
        out_specs=(VMEM,) * 4 + (HBM,) * 2,
        scratch_shapes=[
            pltpu.VMEM((slots, width), bf16),
            pltpu.VMEM((rows, width), bf16),
            pltpu.VMEM((rows, width), f32),
            pltpu.VMEM((rows, width), bf16),
            pltpu.VMEM((width, rows), bf16),
            pltpu.VMEM((width, width), bf16),
            pltpu.VMEM((rows, 3 * width), bf16),
            pltpu.VMEM((width, rows), bf16),
            pltpu.VMEM((width, 3 * width), bf16),
            pltpu.VMEM((rows, width), bf16),
            DMA((10,)),
            pltpu.VMEM((slots, width), bf16),
            pltpu.VMEM((2, width + 16, block), bf16),
            pltpu.VMEM((2, chips, width + 16, block), bf16),
            pltpu.VMEM((rows, 3 * width), bf16),
            pltpu.VMEM((rows, width), bf16),
            pltpu.VMEM((width, rows), bf16),
            pltpu.VMEM((rows, width), f32),
            pltpu.VMEM((4, 2, experts, per, half), bf16),
            pltpu.VMEM((smalls, width), f32),
            pltpu.VMEM((4, experts, per, half), bf16),
            pltpu.VMEM((4, experts, per, half), bf16),
            pltpu.VMEM((4, chips - 1, per, half), bf16),
            pltpu.VMEM((2, steps, smalls, width), f32),
            DMA((experts,)), DMA((experts,)),
            DMA((2, chips)), DMA((2, chips)),
            DMA((2, chips)), DMA((2, chips)),
            DMA((2,)), DMA(()),
            DMA((4,)), DMA((4,)),
            DMA((4, bits)), DMA((4, bits)),
            DMA((4, chips)), DMA((4, chips)),
            DMA((4,)), DMA((4,)),
            DMA((steps,)), DMA((steps,)),
        ],
        compiler_params=pltpu.CompilerParams(
            collective_id=2, has_side_effects=True, vmem_limit_bytes=VMEM_BYTES
        ),
        name="back",
    )(*operands)


def finish_kernel(
    copies, experts,
    kept_ref, far_ref, sums_ref, small_ref, made_ref, grad_ref,
    output_ref, grad_patches_ref, gain1_ref, bias1_ref, qkv_w_ref, qv_bias_ref, out_w_ref, out_bias_ref, gain2_ref, bias2_ref, router_ref,
    in_w_ref, in_bias_ref, expert_out_ref, expert_out_bias_ref,
    turned, turned_bias,
):
    output_ref[...] = made_ref[...]
    grad_patches_ref[...] = grad_ref[...]
    width = small_ref.shape[1]
    per, half = width // experts, width // 2
    me = lax.axis_index("expert")
    me_dp = lax.axis_index("dp")

    def total(w, part):
        value = kept_ref[w, part, :].astype(f32)
        for q in range(copies // 2 - 1):
            value += far_ref[w, q, part, :].astype(f32)
        return value

    body = slice(0, width)
    in_w_ref[0] = total(0, body)
    expert_out_ref[0] = total(1, body).T
    tail = total(0, slice(width, width + 16))
    in_bias_ref[...] = tail[0:1, :]
    block = tail.shape[1]
    lines = [tail[8 + i : 9 + i, :] for i in range(-(-width // block))]
    bias_row = jnp.concatenate(lines, axis=1)[:, :width]
    turned_bias[...] = jnp.concatenate([bias_row, jnp.zeros((127, width), f32)], axis=0).T
    share = width // copies
    mine = turned_bias[pl.ds(pl.multiple_of(me_dp * share, share), share), :]
    pad = -share % 128
    mine = jnp.concatenate([mine, jnp.zeros((pad, 128), f32)], axis=0) if pad else mine
    expert_out_bias_ref[...] = mine.T[0:1, :share]
    count = small_ref.shape[0]
    turned[...] = jnp.concatenate([small_ref[...], jnp.zeros((128 - count, width), f32)], axis=0).T

    def share_of(start, n):
        value = turned[pl.ds(pl.multiple_of(start, 8), n), :]
        pad = -n % 128
        return (jnp.concatenate([value, jnp.zeros((pad, 128), f32)], axis=0) if pad else value).T

    vectors = share_of(me * per, per)
    for ref, i in [(gain1_ref, 0), (bias1_ref, 1), (out_bias_ref, 4), (gain2_ref, 5), (bias2_ref, 6)]:
        ref[...] = vectors[i : i + 1, :per].reshape(per)
    router_ref[...] = vectors[8 : 8 + experts, :per]
    values = share_of(me % (experts // 2) * 2 * per, 2 * per)
    picked = jnp.where(me < experts // 2, values[2:3, :], values[3:4, :])
    qv_bias_ref[...] = picked[:, : 2 * per].reshape(2 * per)
    for i in range(3):
        for h in range(2):
            qkv_w_ref[:, i * width + h * half : i * width + (h + 1) * half] = sums_ref[i, h].astype(f32)
    for h in range(2):
        out_w_ref[:, h * half : (h + 1) * half] = sums_ref[3, h].astype(f32)


def run_finish(copies, experts, *operands):
    smalls, width = operands[3].shape
    block = operands[0].shape[-1]
    per = width // experts
    shape = jax.ShapeDtypeStruct
    return pl.pallas_call(
        partial(finish_kernel, copies, experts),
        out_shape=(
            shape(operands[4].shape, bf16), shape(operands[5].shape, bf16),
            shape((per,), f32), shape((per,), f32), shape((per, 3 * width), f32), shape((2 * per,), f32),
            shape((per, width), f32), shape((per,), f32), shape((per,), f32), shape((per,), f32),
            shape((experts, per), f32),
            shape((1, width, block), f32), shape((1, block), f32),
            shape((1, block, width), f32), shape((1, width // copies), f32),
        ),
        in_specs=[VMEM] * 6,
        out_specs=(VMEM,) * 15,
        scratch_shapes=[pltpu.VMEM((width, 128), f32), pltpu.VMEM((width, 128), f32)],
        compiler_params=pltpu.CompilerParams(vmem_limit_bytes=VMEM_BYTES),
        name="finish",
    )(*operands)


def local(
    patches, padding, expert_ids, priority, norm1_gain, norm1_bias, qkv_weight, qv_bias, out_weight,
    out_bias, norm2_gain, norm2_bias, router, expert_in, expert_in_bias, expert_out, expert_out_bias,
    cotangent,
):
    row_count, width = patches.shape
    copies, experts = lax.axis_size("dp"), lax.axis_size("expert")
    total_rows = row_count * copies * experts
    capacity = (210 * total_rows + 100 * experts - 1) // (100 * experts)
    most = 8 * row_count // (3 * experts)
    (near_cot, raw_cot, far_slots, x_slots, gate_slots, qkv, att_t, lse, residual, second, first, pairs, probs) = run_front(
        copies, experts, most, capacity,
        patches, cotangent, priority, expert_ids.T, padding, norm1_gain, norm1_bias, qkv_weight, qv_bias,
        out_weight, out_bias, norm2_gain, norm2_bias, router.T,
    )
    d_rows, d_gates, produced, grads = run_experts(
        copies, experts, most,
        x_slots, gate_slots, near_cot, raw_cot, far_slots, expert_in[0], expert_in_bias, expert_out[0], expert_out_bias,
    )
    output, grad_patches, sums, small, kept_grads, far_grads = run_back(
        copies, experts, most,
        d_rows, d_gates, produced, grads, pairs, probs,
        second, residual, patches, cotangent, qkv, att_t, lse, first,
        norm1_gain, norm2_gain, qkv_weight, out_weight, router.T,
    )
    (output, grad_patches, n1_gain, n1_bias, qkv_w, qv, out_w, out_b, n2_gain, n2_bias, router_t, *rest) = run_finish(
        copies, experts, kept_grads, far_grads, sums, small, output, grad_patches
    )
    return (output, grad_patches, n1_gain, n1_bias, qkv_w, qv, out_w, out_b, n2_gain, n2_bias, router_t.T, *rest)


def solution(mesh):
    tokens = P(("dp", "expert"))
    wide = P(("dp", "expert"), None)
    return jax.shard_map(
        local,
        mesh=mesh,
        in_specs=(
            wide, tokens, wide, tokens, P(), P(), P(), P(), P(), P(), P(), P(), P(),
            P("expert", None, None), P("expert", None), P("expert", None, None), P("expert", None), wide,
        ),
        out_specs=(
            wide, wide, P("expert"), P("expert"), P("expert", None), P("expert"), P("expert", None),
            P("expert"), P("expert"), P("expert"), P("expert", None), P("expert", None, "dp"),
            P("expert", "dp"), P("expert", "dp", None), P("expert", "dp"),
        ),
        check_vma=False,
    )
```

```python
from functools import partial

import jax
import jax.numpy as jnp
from jax import lax
from jax.experimental import pallas as pl
from jax.experimental.pallas import tpu as pltpu
from jax.sharding import PartitionSpec as P

HEADS = 12
HEAD_DIM = 64
SEQ_LEN = 576
LOG2E = 1.4426950408889634
EPS = 1e-06
lane_count = 256
MESH = pl.DeviceIdType.MESH
NN = (((1,), (0,)), ((), ()))
NT = (((1,), (1,)), ((), ()))
TN = (((0,), (0,)), ((), ()))
VMEM_BYTES = 63 << 20
bf16 = jnp.bfloat16
f32 = jnp.float32
i32 = jnp.int32


def dot(a, b, dims=NN):
    return lax.dot_general(a, b, dims, preferred_element_type=f32)


def iota(shape, axis):
    return lax.broadcasted_iota(i32, shape, axis)


def flat(ref):
    return ref[...].reshape(1, ref.shape[0])


def ones_where(mask):
    return jnp.where(mask, 1.0, 0.0).astype(bf16)


def standardize(values):
    centred = values - jnp.mean(values, axis=-1, keepdims=True)
    inverse = lax.rsqrt(jnp.mean(centred * centred, axis=-1, keepdims=True) + EPS)
    return centred * inverse, inverse


def greet(peers):
    barrier = pltpu.get_barrier_semaphore()
    for peer in peers:
        pl.semaphore_signal(barrier, inc=1, device_id=peer, device_id_type=MESH)
    pl.semaphore_wait(barrier, len(peers))


def send(src, dst, send_sem, recv_sem, peer):
    copy = pltpu.make_async_remote_copy(
        src_ref=src, dst_ref=dst, send_sem=send_sem, recv_sem=recv_sem,
        device_id=peer, device_id_type=MESH,
    )
    copy.start()
    return copy


def front_kernel(
    copies, experts, most, capacity,
    patches_hbm, cot_hbm, priority_ref, ids_ref, padding_ref, gain1_ref, bias1_ref, qkv_w_hbm, qv_bias_ref,
    out_w_hbm, out_bias_ref, gain2_ref, bias2_ref, router_ref,
    recv_cot_hbm, raw_hbm, far_slots_ref, x_slots_hbm, gate_slots_ref, qkv_hbm, att_t_hbm, lse_ref,
    residual_hbm, second_hbm, first_t_hbm, pairs_ref, probs_ref,
    patches_ref, cot_ref, qkv_w_ref, out_w_ref, x_slots_ref, qkv_ref, att_t_ref, residual_ref, second_ref,
    first_t_ref, fetch_sem, store_sem, cot_send, rows_ref, line_ref, table, counts, cot_ss, cot_rs, near_ss, near_rs, far_ss, far_rs, raw_sem,
):
    me_dp = lax.axis_index("dp")
    me = lax.axis_index("expert")
    rows, width = patches_ref.shape
    ends = [(cot_hbm, cot_ref), (patches_hbm, patches_ref), (qkv_w_hbm, qkv_w_ref), (out_w_hbm, out_w_ref)]
    fetches = [pltpu.make_async_copy(a, b, fetch_sem.at[i]) for i, (a, b) in enumerate(ends)]
    for fetch in fetches:
        fetch.start()
    ends = [
        (qkv_ref, qkv_hbm), (first_t_ref, first_t_hbm), (att_t_ref, att_t_hbm), (residual_ref, residual_hbm),
        (second_ref, second_hbm), (x_slots_ref, x_slots_hbm),
        (cot_send.at[pl.ds(0, most)], recv_cot_hbm.at[pl.ds(0, most)]),
    ]
    stores = [pltpu.make_async_copy(a, b, store_sem.at[i]) for i, (a, b) in enumerate(ends)]
    rows_ref[0:1, :] = priority_ref[...].reshape(1, rows)
    rows_ref[1:3, :] = ids_ref[...]
    rows_ref[3:4, :] = padding_ref[...].reshape(1, rows)
    rows_ref[4:6, :] = jnp.where(rows_ref[3:4, :] > 0, rows_ref[1:3, :], experts)
    rows_ref[6:, :] = jnp.zeros((2, rows), i32)
    cols = rows_ref[...].T
    starts = range(0, rows, lane_count)
    parts = [(start, min(lane_count, rows - start)) for start in starts]

    def spot(fact, i):
        line = fact * len(parts) + i
        return (line, 0) if line < line_ref.shape[0] else (len(parts) - 1, lane_count // 2)

    line_ref[...] = jnp.zeros_like(line_ref)
    for fact, row in enumerate([0, 4, 5]):
        for i, (start, size) in enumerate(parts):
            line, at = spot(fact, i)
            line_ref[line : line + 1, at : at + size] = rows_ref[row : row + 1, start : start + size]
    greet(
        [(me_dp, me ^ o) for o in range(1, experts)]
        + [(me_dp ^ p, me) for p in range(1, copies)]
    )
    near = [
        send(line_ref, table.at[0, o], near_ss.at[o], near_rs.at[o], (me_dp, me ^ o))
        for o in range(1, experts)
    ]
    table[0, 0] = line_ref[...]
    far_half = experts // 2
    raw = send(cot_hbm, raw_hbm, raw_sem.at[0], raw_sem.at[1], (me_dp, me ^ far_half))
    expert_rows = iota((experts, rows), 0)
    before_t = ones_where(iota((rows, rows), 0) < iota((rows, rows), 1))

    def slot_rows(ids, device):
        ids = ids ^ device
        hits = [expert_rows == ids[k : k + 1, :] for k in range(2)]
        place = dot(ones_where(hits[0] | hits[1]), before_t).astype(i32) + expert_rows * most
        none = ids[0:1, :] >= experts
        return [
            jnp.where(none, -1, jnp.sum(jnp.where(hit, place, 0), axis=0, keepdims=True)) for hit in hits
        ]

    slot0_row, slot1_row = slot_rows(rows_ref[4:6, :], me)
    id0_col, id1_col = cols[:, 1:2], cols[:, 2:3]
    def taken(o):
        slots = iota((most, rows), 0) + o * most
        return ones_where((slots == slot0_row) | (slots == slot1_row))

    fetches[0].wait()
    cot_value = cot_ref[...]
    cots = []
    for o in range(far_half):
        picked = dot(taken(o), cot_value).astype(bf16)
        part = pl.ds(o * most, most)
        cot_send[part, :] = picked
        if o == 0:
            stores[6].start()
            continue
        cots.append(
            send(cot_send.at[part], recv_cot_hbm.at[part], cot_ss.at[o], cot_rs.at[o], (me_dp, me ^ o))
        )
    fetches[1].wait()
    inputs = patches_ref[...].astype(f32)
    first = (standardize(inputs)[0] * flat(gain1_ref) + flat(bias1_ref)).astype(bf16)
    first_t_ref[...] = first.T
    stores[1].start()
    fetches[2].wait()
    qkv_ref[:, :width] = (dot(first, qkv_w_ref[:, :width]) + flat(qv_bias_ref)[:, :width]).astype(bf16)
    qkv_ref[:, width : 2 * width] = dot(first, qkv_w_ref[:, width : 2 * width]).astype(bf16)
    qkv_ref[:, 2 * width :] = (
        dot(first, qkv_w_ref[:, 2 * width :]) + flat(qv_bias_ref)[:, width:]
    ).astype(bf16)
    stores[0].start()
    key_bias = jnp.where(cols[:, 3:4] > 0, 0.0, -1e30)
    scale = LOG2E * HEAD_DIM ** (-0.5)
    pair_width = 2 * HEAD_DIM

    far = [
        pltpu.make_async_remote_copy(
            table.at[0], table.at[p], far_ss.at[p], far_rs.at[p], (me_dp ^ p, me), MESH
        )
        for p in range(1, copies)
    ]

    def attend(pair, _):
        @pl.when(pair == 5)
        def _():
            for near_copy in near:
                near_copy.wait_recv()
            for far_copy in far:
                far_copy.start()

        base = pl.multiple_of(pair * pair_width, pair_width)
        q = qkv_ref[:, pl.ds(base, pair_width)]
        k = qkv_ref[:, pl.ds(base + width, pair_width)]
        v_t = qkv_ref[:, pl.ds(base + 2 * width, pair_width)].T
        lanes = iota((rows, pair_width), 1)
        outs, stats = [], []
        for a in range(2):
            k_a = jnp.where((lanes >= HEAD_DIM) == (a == 1), k, jnp.zeros((), bf16))
            scores = dot(k_a, q, NT) + key_bias
            peak = jnp.max(scores, axis=0, keepdims=True)
            raised = jnp.exp2(scores * scale - peak * scale)
            total = jnp.sum(raised, axis=0, keepdims=True)
            out = dot(v_t[a * HEAD_DIM : (a + 1) * HEAD_DIM, :], raised.astype(bf16))
            outs.append(out / total)
            stats.append(peak * scale + jnp.log2(total))
        att_t_ref[pl.ds(base, pair_width), :] = jnp.concatenate(outs, axis=0).astype(bf16)
        lse_ref[pair] = jnp.concatenate(stats + [jnp.zeros((6, rows), f32)], axis=0)
        return 0

    lax.fori_loop(0, HEADS // 2, attend, 0)
    rel0_col, rel1_col = cols[:, 4:5] ^ me, cols[:, 5:6] ^ me
    expert_cols = iota((rows, experts), 1)
    named = ones_where((expert_cols == rel0_col) | (expert_cols == rel1_col))
    before = ones_where(iota((rows, rows), 1) < iota((rows, rows), 0))
    place = dot(before, named).astype(i32) + expert_cols * most
    slot0_col = jnp.sum(jnp.where(expert_cols == rel0_col, place, 0), axis=1, keepdims=True)
    slot1_col = jnp.sum(jnp.where(expert_cols == rel1_col, place, 0), axis=1, keepdims=True)
    none_col = cols[:, 4:5] >= experts
    slot0_col, slot1_col = jnp.where(none_col, -1, slot0_col), jnp.where(none_col, -1, slot1_col)

    far_line = table[0, far_half]
    far_codes = []
    for fact in (1, 2):
        spots = [(spot(fact, i), size) for i, (start, size) in enumerate(parts)]
        pieces = [far_line[line : line + 1, at : at + size] for (line, at), size in spots]
        far_codes.append(jnp.concatenate(pieces, axis=1))
    far0_row, far1_row = slot_rows(jnp.concatenate(far_codes, axis=0), me ^ far_half)
    far_slots_ref[...] = jnp.concatenate([far0_row, far1_row, jnp.zeros((6, rows), i32)], axis=0)
    stores[2].start()
    fetches[3].wait()
    residual = inputs + dot(att_t_ref[...], out_w_ref[...], TN) + flat(out_bias_ref)
    residual_ref[...] = residual
    stores[3].start()
    second = (standardize(residual)[0] * flat(gain2_ref) + flat(bias2_ref)).astype(bf16)
    second_ref[...] = second
    stores[4].start()
    for o in range(experts):
        x_slots_ref[pl.ds(o * most, most), :] = dot(taken(o), second).astype(bf16)
    stores[5].start()
    logits = dot(second, router_ref[...], NT)
    raised = jnp.exp(logits - jnp.max(logits, axis=-1, keepdims=True))
    probs = raised / jnp.sum(raised, axis=-1, keepdims=True)
    probs_ref[...] = probs
    prob0 = jnp.sum(jnp.where(expert_cols == id0_col, probs, 0.0), axis=1, keepdims=True)
    prob1 = jnp.sum(jnp.where(expert_cols == id1_col, probs, 0.0), axis=1, keepdims=True)
    both = prob0 + prob1
    gate0, gate1 = prob0 / both, prob1 / both
    for far_copy in far:
        far_copy.wait_recv()
    counts[...] = jnp.zeros_like(counts)
    rank_col = cols[:, 0:1]

    def count(block, _):
        entry = table[block // experts, block % experts]
        ahead = jnp.zeros((rows, 2 * experts), f32)
        loads = jnp.zeros((8, 2 * experts), f32)
        for i, (start, size) in enumerate(parts):

            def fact(k):
                line, at = spot(k, i)
                return entry[line : line + 1, at : at + size]

            names = iota((experts, size), 0)
            hits = jnp.concatenate([ones_where(names == fact(1)), ones_where(names == fact(2))], axis=0)
            ahead += dot(ones_where(fact(0) < rank_col), hits, NT)
            loads += dot(jnp.ones((8, size), bf16), hits, NT)
        counts[:rows, :] += ahead
        counts[rows:, :] += loads
        return 0

    lax.fori_loop(0, copies * experts, count, 0)
    both_cols = iota((rows, 2 * experts), 1)
    ahead = counts[:rows, :]
    loads = counts[rows : rows + 1, :]
    position0 = jnp.sum(jnp.where(both_cols == id0_col, ahead, 0.0), axis=1, keepdims=True)
    position1 = jnp.sum(
        jnp.where(both_cols == id1_col + experts, ahead, 0.0)
        + jnp.where(both_cols == id1_col, loads, 0.0),
        axis=1,
        keepdims=True,
    )
    real_col = cols[:, 3:4] > 0
    kept0 = jnp.where(real_col & (position0 < capacity), 1.0, 0.0)
    kept1 = jnp.where(real_col & (position1 < capacity), 1.0, 0.0)
    gate0, gate1 = gate0 * kept0, gate1 * kept1
    for o in range(experts):
        slots = iota((rows, most), 1) + o * most
        gates = jnp.where(slots == slot0_col, gate0, 0.0) + jnp.where(slots == slot1_col, gate1, 0.0)
        gate_slots_ref[o] = jnp.sum(gates, axis=0, keepdims=True)
    lanes = iota((rows, 16), 1)
    columns = [slot0_col, slot1_col, gate0, gate1, kept0, kept1, both, cols[:, 3:4], id0_col, id1_col]
    columns = [column.astype(f32) for column in columns]
    packed = jnp.zeros((rows, 16), f32)
    for i, column in enumerate(columns):
        packed = jnp.where(lanes == i, column, packed)
    pairs_ref[...] = packed
    for copy in near + far:
        copy.wait_send()
    for copy in [*cots, raw, *stores]:
        copy.wait()


VMEM = pl.BlockSpec(memory_space=pltpu.VMEM)
HBM = pl.BlockSpec(memory_space=pl.ANY)
DMA = pltpu.SemaphoreType.DMA


def run_front(copies, experts, most, capacity, *operands):
    rows, width = operands[0].shape
    slots = experts * most
    shape = jax.ShapeDtypeStruct
    return pl.pallas_call(
        partial(front_kernel, copies, experts, most, capacity),
        out_shape=(
            shape((slots // 2, width), bf16),
            shape((rows, width), bf16),
            shape((8, rows), i32),
            shape((slots, width), bf16),
            shape((experts, 1, most), f32),
            shape((rows, 3 * width), bf16),
            shape((width, rows), bf16),
            shape((HEADS // 2, 8, rows), f32),
            shape((rows, width), f32),
            shape((rows, width), bf16),
            shape((width, rows), bf16),
            shape((rows, 16), f32),
            shape((rows, experts), f32),
        ),
        in_specs=[HBM] * 2 + [VMEM] * 5 + [HBM, VMEM, HBM] + [VMEM] * 4,
        out_specs=(HBM, HBM, VMEM, HBM, VMEM, HBM, HBM, VMEM, HBM, HBM, HBM, VMEM, VMEM),
        scratch_shapes=[
            pltpu.VMEM((rows, width), bf16),
            pltpu.VMEM((rows, width), bf16),
            pltpu.VMEM((width, 3 * width), bf16),
            pltpu.VMEM((width, width), bf16),
            pltpu.VMEM((slots, width), bf16),
            pltpu.VMEM((rows, 3 * width), bf16),
            pltpu.VMEM((width, rows), bf16),
            pltpu.VMEM((rows, width), f32),
            pltpu.VMEM((rows, width), bf16),
            pltpu.VMEM((width, rows), bf16),
            DMA((4,)), DMA((7,)),
            pltpu.VMEM((slots // 2, width), bf16),
            pltpu.VMEM((8, rows), i32),
            pltpu.VMEM((8, lane_count), i32),
            pltpu.VMEM((copies, experts, 8, lane_count), i32),
            pltpu.VMEM((rows + 8, 2 * experts), f32),
            DMA((experts,)), DMA((experts,)),
            DMA((experts,)), DMA((experts,)),
            DMA((copies,)), DMA((copies,)), DMA((2,)),
        ],
        compiler_params=pltpu.CompilerParams(
            collective_id=0, has_side_effects=True, vmem_limit_bytes=VMEM_BYTES
        ),
        name="front",
    )(*operands)


def gelu_parts(values):
    bell = jnp.exp2(values * values * (-0.5 * LOG2E))
    t = 1.0 / (1.0 + (0.3275911 * 0.5**0.5) * jnp.abs(values))
    tail = t * (0.1274147959 + t * (-0.142248368 + t * (0.7107068705 + t * (-0.7265760135 + t * 0.5307027145))))
    tail = tail * bell
    share = jnp.where(values >= 0, 1.0 - tail, tail)
    return values * share, share + values * bell * 0.3989422804014327


def to_column(row):
    n = row.shape[1]
    return jnp.sum(jnp.where(iota((n, n), 0) == iota((n, n), 1), row, 0.0), axis=1, keepdims=True)


def to_row(column):
    n = column.shape[0]
    return jnp.sum(jnp.where(iota((n, n), 0) == iota((n, n), 1), column, 0.0), axis=0, keepdims=True)


def expert_kernel(
    copies, experts, most, chunks, tile,
    x_ref, gates_ref, near_cot_ref, raw_ref, far_slots_ref, in_w_hbm, in_bias_ref, out_w_hbm, out_bias_ref,
    d_rows_ref, d_gates_ref, produced_ref, grads_ref,
    in_w_ref, out_w_ref, cot_ref, send_cot, recv_x, recv_g, send_d, send_g, hidden, d_pre, x_t, d_t, bias_sum, total_p, total_d, stage,
    x_ss, x_rs, g_ss, g_rs, d_ss, d_rs, dg_ss, dg_rs, own_sem, own_d_sem, stage_sem,
    cot_ss, cot_rs, near_sem, fetch_sem,
):
    me_dp = lax.axis_index("dp")
    me = lax.axis_index("expert")
    width, hidden_width = in_w_ref.shape
    rows = chunks * most
    block = hidden_width // copies

    def chunk(o):
        return pl.ds(pl.multiple_of(o * most, most), most)

    def move_x(o):
        return pltpu.make_async_remote_copy(
            x_ref.at[chunk(o)], recv_x.at[chunk(o)], x_ss.at[o], x_rs.at[o], (me_dp, me ^ o), MESH
        )

    def move_g(o):
        return pltpu.make_async_remote_copy(
            gates_ref.at[o], recv_g.at[o], g_ss.at[o], g_rs.at[o], (me_dp, me ^ o), MESH
        )

    def move_d(o):
        return pltpu.make_async_remote_copy(
            send_d.at[chunk(o)], d_rows_ref.at[chunk(o)], d_ss.at[o], d_rs.at[o], (me_dp, me ^ o), MESH
        )

    def move_dg(o):
        return pltpu.make_async_remote_copy(
            send_g.at[o], d_gates_ref.at[o], dg_ss.at[o], dg_rs.at[o], (me_dp, me ^ o), MESH
        )

    far_half = experts // 2

    def move_cot(j):
        return pltpu.make_async_remote_copy(
            send_cot.at[chunk(j)], cot_ref.at[chunk(far_half + j)], cot_ss.at[j], cot_rs.at[j],
            (me_dp, me ^ j), MESH,
        )

    fetches = [
        pltpu.make_async_copy(in_w_hbm, in_w_ref, fetch_sem.at[0]),
        pltpu.make_async_copy(out_w_hbm, out_w_ref, fetch_sem.at[1]),
    ]
    for fetch in fetches:
        fetch.start()
    own = pltpu.make_async_copy(x_ref.at[chunk(0)], recv_x.at[chunk(0)], own_sem)
    own.start()
    half_slots = near_cot_ref.shape[0]
    near_cot = pltpu.make_async_copy(near_cot_ref, cot_ref.at[pl.ds(0, half_slots)], near_sem)
    near_cot.start()
    greet([(me_dp, me ^ o) for o in range(1, experts)])

    def begin(g):
        for o in range(max(1, g * chunks), (g + 1) * chunks):
            move_g(o).start()
            move_x(o).start()

    groups = experts // chunks
    order = [0, *range(groups // 2, groups), *range(1, groups // 2)]
    begin(order[0])
    begin(order[1])
    for j in [*range(1, far_half), 0]:
        places = iota((most, raw_ref.shape[0]), 0) + (far_half + j) * most
        taken = ones_where((places == far_slots_ref[0:1, :]) | (places == far_slots_ref[1:2, :]))
        picked = dot(taken, raw_ref[...]).astype(bf16)
        if j == 0:
            cot_ref[chunk(far_half), :] = picked
        else:
            send_cot[chunk(j), :] = picked
            move_cot(j).start()
    near_cot.wait()
    for fetch in fetches:
        fetch.wait()
    recv_g[0] = gates_ref[0]
    bias_sum[...] = jnp.zeros_like(bias_sum)
    x_t[width:, :] = jnp.ones_like(x_t[width:, :])
    own.wait()
    own_d = pltpu.make_async_copy(send_d.at[chunk(0)], d_rows_ref.at[chunk(0)], own_d_sem)

    def work(n, _):
        g = n % 2 * (groups // 2) + n // 2
        for j in range(chunks):
            o = g * chunks + j

            @pl.when(o > 0)
            def _():
                move_g(o).wait_recv()
                move_x(o).wait_recv()

            @pl.when(o > far_half)
            def _():
                move_cot(o - far_half).wait_recv()

        at = pl.multiple_of(g * rows, rows)
        here = pl.ds(at, rows)
        gate = jnp.concatenate([to_column(recv_g[g * chunks + j]) for j in range(chunks)], axis=0)
        x = recv_x[here, :]
        cot = cot_ref[here, :].astype(f32)
        d_produced = (cot * gate).astype(bf16)
        bias_sum[0:1, :] += jnp.sum(d_produced.astype(f32), axis=0, keepdims=True)
        x_t[:width, here] = x.T
        d_t[:, here] = d_produced.T
        total_p[...] = jnp.zeros_like(total_p)
        total_d[...] = jnp.zeros_like(total_d)

        def step(n, _):
            cols = pl.ds(pl.multiple_of(n * tile, tile), tile)
            pre = dot(x, in_w_ref[:, cols]) + in_bias_ref[:, cols]
            value, slope = gelu_parts(pre)
            value = value.astype(bf16)
            hidden[here, cols] = value
            total_p[...] += dot(value, out_w_ref[cols, :])
            d_value = (dot(d_produced, out_w_ref[cols, :], NT) * slope).astype(bf16)
            d_pre[here, cols] = d_value
            total_d[...] += dot(d_value, in_w_ref[:, cols], NT)
            return 0

        lax.fori_loop(0, hidden_width // tile, step, 0)

        @pl.when(n == 0)
        def _():
            for later in order[2:]:
                begin(later)

        send_d[here, :] = total_d[...].astype(bf16)
        produced = (total_p[...] + out_bias_ref[...]).astype(bf16)
        produced_ref[here, :] = produced
        d_gate = jnp.sum(produced.astype(f32) * cot, axis=1, keepdims=True)
        for j in range(chunks):
            o = g * chunks + j
            d_gate_row = to_row(d_gate[j * most : (j + 1) * most, :])
            send_g[o] = d_gate_row

            @pl.when(o > 0)
            def _():
                move_d(o).start()
                move_dg(o).start()

            @pl.when(o == 0)
            def _():
                own_d.start()
                d_gates_ref[0] = d_gate_row

        return 0

    lax.fori_loop(0, groups, work, 0)

    def store(w, p):
        return pltpu.make_async_copy(stage.at[w], grads_ref.at[w, p], stage_sem.at[w])

    def weigh(p, _):
        cols = pl.ds(pl.multiple_of((me_dp ^ p) * block, block), block)

        @pl.when(p > 0)
        def _():
            store(0, p - 1).wait()

        total = dot(x_t[...], d_pre[:, cols])
        stage[0, :width, :] = total[:width, :].astype(bf16)
        tail = total[width:, :]
        lines = iota((16, block), 0)
        for i in range(-(-width // block)):
            tail = jnp.where(lines == 8 + i, bias_sum[0:1, i * block : (i + 1) * block], tail)
        stage[0, width:, :] = tail.astype(bf16)
        store(0, p).start()

        @pl.when(p > 0)
        def _():
            store(1, p - 1).wait()

        stage[1, :width, :] = dot(d_t[...], hidden[:, cols]).astype(bf16)
        stage[1, width:, :] = jnp.zeros((16, block), bf16)
        store(1, p).start()
        return 0

    lax.fori_loop(0, copies, weigh, 0)
    store(0, copies - 1).wait()
    store(1, copies - 1).wait()
    own_d.wait()
    for j in range(1, far_half):
        move_cot(j).wait_send()
    for o in range(1, experts):
        move_g(o).wait_send()
        move_x(o).wait_send()
        move_d(o).wait()
        move_dg(o).wait()


def run_experts(copies, experts, most, *operands):
    slots, width = operands[0].shape
    hidden_width = operands[5].shape[1]
    chunks = max(1, min(experts, 384 // most))
    rows = chunks * most
    block = hidden_width // copies
    shape = jax.ShapeDtypeStruct
    return pl.pallas_call(
        partial(expert_kernel, copies, experts, most, chunks, 512),
        out_shape=(
            shape((slots, width), bf16),
            shape((experts, 1, most), f32),
            shape((slots, width), bf16),
            shape((2, copies, width + 16, block), bf16),
        ),
        in_specs=[HBM, VMEM, HBM] + [VMEM] * 2 + [HBM, VMEM] * 2,
        out_specs=(HBM, VMEM, VMEM, HBM),
        scratch_shapes=[
            pltpu.VMEM((width, hidden_width), bf16),
            pltpu.VMEM((hidden_width, width), bf16),
            pltpu.VMEM((slots, width), bf16),
            pltpu.VMEM((slots // 2, width), bf16),
            pltpu.VMEM((slots, width), bf16),
            pltpu.VMEM((experts, 1, most), f32),
            pltpu.VMEM((slots, width), bf16),
            pltpu.VMEM((experts, 1, most), f32),
            pltpu.VMEM((slots, hidden_width), bf16),
            pltpu.VMEM((slots, hidden_width), bf16),
            pltpu.VMEM((width + 16, slots), bf16),
            pltpu.VMEM((width, slots), bf16),
            pltpu.VMEM((8, width), f32),
            pltpu.VMEM((rows, width), f32),
            pltpu.VMEM((rows, width), f32),
            pltpu.VMEM((2, width + 16, block), bf16),
        ]
        + [DMA((experts,))] * 8
        + [DMA(()), DMA(()), DMA((2,)), DMA((experts // 2,)), DMA((experts // 2,)), DMA(()), DMA((2,))],
        compiler_params=pltpu.CompilerParams(
            collective_id=1, has_side_effects=True, vmem_limit_bytes=VMEM_BYTES
        ),
        name="experts",
    )(*operands)


def back_kernel(
    copies, experts, most,
    d_rows_hbm, d_gates_ref, produced_ref, grads_ref, pairs_ref, probs_ref,
    second_hbm, residual_hbm, patches_hbm, cot_hbm, qkv_hbm, att_t_hbm, lse_ref, first_t_hbm,
    gain1_ref, gain2_ref, qkv_w_hbm, out_w_hbm, router_ref,
    output_ref, grad_patches_ref, sums_ref, small_sums_ref, kept_grads_ref, far_grads_ref,
    d_rows_ref, second_ref, residual_ref, cot_ref, att_t_ref, out_w_ref, qkv_ref, first_t_ref, qkv_w_ref,
    patches_ref, fetch_sem,
    recv_p, own_grads, near_grads, d_qkv, d_att, d_att_t, d_residual_ref,
    dense, small, halves, landed, crossed, tiny,
    p_ss, p_rs, n_ss, n_rs, f_ss, f_rs, own_sem, kept_sem,
    a_ss, a_rs, b_ss, b_rs, c_ss, c_rs, e_ss, e_rs, t_ss, t_rs,
):
    me_dp = lax.axis_index("dp")
    me = lax.axis_index("expert")
    rows, width = patches_ref.shape
    ends = [
        (d_rows_hbm, d_rows_ref), (second_hbm, second_ref), (residual_hbm, residual_ref), (cot_hbm, cot_ref),
        (att_t_hbm, att_t_ref), (out_w_hbm, out_w_ref), (qkv_hbm, qkv_ref), (first_t_hbm, first_t_ref),
        (qkv_w_hbm, qkv_w_ref), (patches_hbm, patches_ref),
    ]
    fetches = [pltpu.make_async_copy(a, b, fetch_sem.at[i]) for i, (a, b) in enumerate(ends)]
    for fetch in fetches:
        fetch.start()
    slots = experts * most
    chips = copies // 2
    core = me_dp % 2
    per = width // experts
    half = width // 2
    partner = (me_dp ^ 1, me)
    bits = list(range(experts.bit_length() - 1))
    steps = [(me_dp ^ (1 << i), me) for i in range(copies.bit_length() - 1)]
    steps += [(me_dp, me ^ (1 << i)) for i in range(experts.bit_length() - 1)]

    def copy_a(m):
        return pltpu.make_async_remote_copy(
            dense.at[m, 1 - core], halves.at[m], a_ss.at[m], a_rs.at[m], partner, MESH
        )

    def copy_b(m, i):
        part = pl.ds(experts >> (i + 1), experts >> (i + 1))
        return pltpu.make_async_remote_copy(
            dense.at[m, core, part], landed.at[m, part], b_ss.at[m, i], b_rs.at[m, i],
            (me_dp, me ^ (1 << bits[i])), MESH,
        )

    def copy_c(m, q):
        return pltpu.make_async_remote_copy(
            dense.at[m, core, 0], crossed.at[m, q - 1], c_ss.at[m, q], c_rs.at[m, q],
            (me_dp ^ (2 * q), me), MESH,
        )

    def copy_e(m):
        return pltpu.make_async_remote_copy(
            sums_ref.at[m, core], sums_ref.at[m, core], e_ss.at[m], e_rs.at[m], partner, MESH
        )

    def begin(m, k):
        if k == 0:
            copy_a(m).start()
        elif k <= len(bits):
            copy_b(m, k - 1).start()
        elif k == len(bits) + 1:
            for q in range(1, chips):
                copy_c(m, q).start()
        else:
            copy_e(m).start()

    def end(m, k):
        if k == 0:
            copy_a(m).wait_recv()
            dense[m, core] = (dense[m, core].astype(f32) + halves[m].astype(f32)).astype(bf16)
        elif k <= len(bits):
            copy_b(m, k - 1).wait_recv()
            n = experts >> k
            total = dense[m, core, 0:n].astype(f32) + landed[m, n : 2 * n].astype(f32)
            dense[m, core, 0:n] = total.astype(bf16)
        elif k == len(bits) + 1:
            total = dense[m, core, 0].astype(f32)
            for q in range(1, chips):
                copy_c(m, q).wait_recv()
                total += crossed[m, q - 1].astype(f32)
            sums_ref[m, core] = total.astype(bf16)

    stages = [0] * 4

    def advance(m):
        if stages[m] < len(bits) + 2:
            end(m, stages[m])
            stages[m] += 1
            begin(m, stages[m])

    def copy_t(i):
        return pltpu.make_async_remote_copy(tiny.at[0, i], tiny.at[1, i], t_ss.at[i], t_rs.at[i], steps[i], MESH)

    def begin_small(i):
        tiny[0, i] = small[...].astype(bf16)
        copy_t(i).start()

    todo = list(range(len(steps)))

    def advance_small():
        if todo:
            i = todo.pop(0)
            copy_t(i).wait_recv()
            small[...] += tiny[1, i].astype(f32)
            if i + 1 < len(steps):
                begin_small(i + 1)

    def copy_f(w, q):
        return pltpu.make_async_remote_copy(
            near_grads.at[w, q], far_grads_ref.at[w, q - 1], f_ss.at[w, q], f_rs.at[w, q],
            (me_dp ^ (2 * q), me), MESH,
        )

    greet(
        [(me_dp, me ^ o) for o in range(1, experts)]
        + [partner]
        + [(me_dp ^ (2 * q), me) for q in range(1, chips)]
    )
    near = [
        send(grads_ref.at[w, 2 * q + 1], near_grads.at[w, q], n_ss.at[w, q], n_rs.at[w, q], partner)
        for q in range(chips)
        for w in range(2)
    ]
    turns = [(w, q) for q in [*range(1, chips), 0] for w in range(2)]
    own = [
        pltpu.make_async_copy(grads_ref.at[w, 2 * q], own_grads.at[i % 2], own_sem.at[i % 2])
        for i, (w, q) in enumerate(turns)
    ]
    for copy in own[:2]:
        copy.start()
    returns = []
    for o in range(1, experts):
        part = pl.ds(o * most, most)
        returns.append(
            send(produced_ref.at[part], recv_p.at[part], p_ss.at[o], p_rs.at[o], (me_dp, me ^ o))
        )
    own_p = pltpu.make_async_copy(
        produced_ref.at[pl.ds(0, most)], recv_p.at[pl.ds(0, most)], p_rs.at[0]
    )
    own_p.start()
    slot0, slot1 = pairs_ref[:, 0:1].astype(i32), pairs_ref[:, 1:2].astype(i32)
    kept0, kept1, both = pairs_ref[:, 4:5], pairs_ref[:, 5:6], pairs_ref[:, 6:7]
    places = iota((rows, slots), 1)
    fetches[0].wait()
    d_second = dot(ones_where((places == slot0) | (places == slot1)), d_rows_ref[...])
    d_gate0 = jnp.zeros((rows, 1), f32)
    d_gate1 = jnp.zeros((rows, 1), f32)
    for o in range(experts):
        part = iota((rows, most), 1) + o * most
        line = d_gates_ref[o]
        d_gate0 += jnp.sum(jnp.where(part == slot0, line, 0.0), axis=1, keepdims=True)
        d_gate1 += jnp.sum(jnp.where(part == slot1, line, 0.0), axis=1, keepdims=True)
    d_gate0, d_gate1 = d_gate0 * kept0, d_gate1 * kept1
    probs = probs_ref[...]
    names = iota((rows, experts), 1)
    is0, is1 = names == pairs_ref[:, 8:9].astype(i32), names == pairs_ref[:, 9:10].astype(i32)
    share0 = jnp.sum(jnp.where(is0, probs, 0.0), axis=1, keepdims=True) / both
    share1 = jnp.sum(jnp.where(is1, probs, 0.0), axis=1, keepdims=True) / both
    centre = d_gate0 * share0 + d_gate1 * share1
    d_probs = jnp.where(is0, (d_gate0 - centre) / both, 0.0) + jnp.where(is1, (d_gate1 - centre) / both, 0.0)
    d_logits = (probs * (d_probs - jnp.sum(probs * d_probs, axis=1, keepdims=True))).astype(bf16)
    small[8:, :] = jnp.zeros_like(small[8:, :])
    fetches[1].wait()
    small[8 : 8 + experts, :] = dot(d_logits, second_ref[...], TN)
    d_second += dot(d_logits, router_ref[...])
    fetches[2].wait()
    fetches[3].wait()
    n, inverse = standardize(residual_ref[...])
    small[5:6, :] = jnp.sum(d_second * n, axis=0, keepdims=True)
    small[6:7, :] = jnp.sum(d_second, axis=0, keepdims=True)
    m = d_second * flat(gain2_ref)
    d_residual = cot_ref[...].astype(f32) + inverse * (
        m - jnp.mean(m, axis=-1, keepdims=True) - n * jnp.mean(m * n, axis=-1, keepdims=True)
    )
    d_residual_ref[...] = d_residual
    d_branch = d_residual.astype(bf16)
    small[4:5, :] = jnp.sum(d_branch.astype(f32), axis=0, keepdims=True)
    small[7:8, :] = jnp.zeros((1, width), f32)

    def keep(matrix, h, value):
        for e in range(experts):
            r = e ^ me
            at = 0
            for bit in bits:
                at = at * 2 + (r // (1 << bit)) % 2
            dense[matrix, h, at] = value[e * per : (e + 1) * per, :].astype(bf16)

    fetches[4].wait()
    for h in range(2):
        keep(3, h, dot(att_t_ref[...], d_branch[:, h * half : (h + 1) * half]))
    begin(3, 0)
    for copy in near:
        copy.wait_recv()
    for i, (w, q) in enumerate(turns):
        own[i].wait()
        near_grads[w, q] = (own_grads[i % 2].astype(f32) + near_grads[w, q].astype(f32)).astype(bf16)
        if i + 2 < len(turns):
            own[i + 2].start()
        if q > 0:
            copy_f(w, q).start()
    kept = pltpu.make_async_copy(near_grads.at[:, 0], kept_grads_ref, kept_sem)
    kept.start()
    advance(3)
    fetches[5].wait()
    d_att[...] = dot(d_branch, out_w_ref[...], NT).astype(bf16)
    d_att_t[...] = dot(out_w_ref[...], d_branch, NT).astype(bf16)
    key_bias = jnp.where(pairs_ref[:, 7:8] > 0, 0.0, -1e30)
    scale = LOG2E * HEAD_DIM ** (-0.5)
    pair_width = 2 * HEAD_DIM

    def columns(i, h):
        return slice(i * width + h * half, i * width + (h + 1) * half)

    def attend(pair, _):
        @pl.when(pair == 3)
        def _():
            for i in range(3):
                keep(i, 0, dot(first_t_ref[...], d_qkv[:, columns(i, 0)]))

                @pl.when(core == 1)
                def _():
                    begin(i, 0)

        @pl.when((pair == 5) & (core == 0))
        def _():
            for i in range(3):
                end(i, 0)
                begin(i, 1)

        base = pl.multiple_of(pair * pair_width, pair_width)
        here = pl.ds(base, pair_width)
        q = qkv_ref[:, here]
        k = qkv_ref[:, pl.ds(base + width, pair_width)]
        v = qkv_ref[:, pl.ds(base + 2 * width, pair_width)]
        k_t = k.T
        d_out = d_att[:, here]
        products = att_t_ref[here, :].astype(f32) * d_att_t[here, :].astype(f32)
        lanes = iota((rows, pair_width), 1)
        d_q, d_k, d_v = [], [], []
        for a in range(2):
            mine = (lanes >= HEAD_DIM) == (a == 1)
            k_a = jnp.where(mine, k, jnp.zeros((), bf16))
            v_a = jnp.where(mine, v, jnp.zeros((), bf16))
            part = slice(a * HEAD_DIM, (a + 1) * HEAD_DIM)
            delta = jnp.sum(products[part, :], axis=0, keepdims=True)
            weights = jnp.exp2((dot(k_a, q, NT) + key_bias) * scale - lse_ref[pair][a : a + 1, :])
            d_scores = (weights * (dot(v_a, d_out, NT) - delta)).astype(bf16)
            d_v.append(dot(weights.astype(bf16), d_out))
            d_k.append(dot(d_scores, q))
            d_q.append(dot(k_t[part, :], d_scores))
        low = lanes < HEAD_DIM
        down = HEAD_DIM ** (-0.5)
        d_qkv[:, here] = (jnp.concatenate(d_q, axis=0).T * down).astype(bf16)
        d_qkv[:, pl.ds(base + width, pair_width)] = (jnp.where(low, d_k[0], d_k[1]) * down).astype(bf16)
        d_qkv[:, pl.ds(base + 2 * width, pair_width)] = jnp.where(low, d_v[0], d_v[1]).astype(bf16)
        return 0

    fetches[6].wait()
    fetches[7].wait()
    lax.fori_loop(0, HEADS // 2, attend, 0)
    advance(3)
    for fetch in fetches[8:]:
        fetch.wait()
    def combine_results():
        own_p.wait()
        for copy in returns:
            copy.wait()
        blocks = 3
        lines = rows // blocks

        def combine(i, _):
            part = pl.ds(pl.multiple_of(i * lines, lines), lines)
            facts = pairs_ref[part, :]
            spots = iota((lines, slots), 1)
            output_ref[part, :] = (
                residual_ref[part, :]
                + facts[:, 2:3] * dot(ones_where(spots == facts[:, 0:1].astype(i32)), recv_p[...])
                + facts[:, 3:4] * dot(ones_where(spots == facts[:, 1:2].astype(i32)), recv_p[...])
            ).astype(bf16)
            return 0

        lax.fori_loop(0, blocks, combine, 0)

    ones = jnp.ones((8, rows), bf16)
    for i in range(3):
        keep(i, 1, dot(first_t_ref[...], d_qkv[:, columns(i, 1)]))

        @pl.when(core == 0)
        def _():
            begin(i, 0)

        if i > 0:

            @pl.when(core == 1)
            def _():
                end(i - 1, 0)
                begin(i - 1, 1)

    for i in (0, 2):
        part = slice(i * width, (i + 1) * width)
        small[2 + i // 2 : 3 + i // 2, :] = dot(ones, d_qkv[:, part])[0:1, :]

    @pl.when(core == 1)
    def _():
        end(2, 0)
        begin(2, 1)

    stages[0:3] = [1, 1, 1]
    d_first = dot(d_qkv[...], qkv_w_ref[...], NT)
    n, inverse = standardize(patches_ref[...].astype(f32))
    small[0:1, :] = jnp.sum(d_first * n, axis=0, keepdims=True)
    small[1:2, :] = jnp.sum(d_first, axis=0, keepdims=True)
    begin_small(0)
    m = d_first * flat(gain1_ref)
    grad_patches_ref[...] = (
        d_residual_ref[...]
        + inverse * (m - jnp.mean(m, axis=-1, keepdims=True) - n * jnp.mean(m * n, axis=-1, keepdims=True))
    ).astype(bf16)
    for turn in range(len(bits) + 2):
        for m in [3, 0, 1, 2]:
            advance(m)
        advance_small()
        if turn == 0:
            combine_results()
    while todo:
        advance_small()
    small_sums_ref[...] = small[...]
    for copy in near:
        copy.wait_send()
    kept.wait()
    for q in range(1, chips):
        for w in range(2):
            copy_f(w, q).wait()
    for m in range(4):
        copy_a(m).wait_send()
        for i in range(len(bits)):
            copy_b(m, i).wait_send()
        for q in range(1, chips):
            copy_c(m, q).wait_send()
        pltpu.make_async_remote_copy(
            sums_ref.at[m, core], sums_ref.at[m, 1 - core], e_ss.at[m], e_rs.at[m], partner, MESH
        ).wait()
    for i in range(len(steps)):
        copy_t(i).wait_send()


def run_back(copies, experts, most, *operands):
    rows, width = operands[8].shape
    slots = experts * most
    chips = copies // 2
    block = operands[3].shape[-1]
    shape = jax.ShapeDtypeStruct
    smalls = -(-(8 + experts) // 16) * 16
    per, half = width // experts, width // 2
    bits = experts.bit_length() - 1
    steps = copies.bit_length() - 1 + bits
    return pl.pallas_call(
        partial(back_kernel, copies, experts, most),
        out_shape=(
            shape((rows, width), bf16),
            shape((rows, width), bf16),
            shape((4, 2, per, half), bf16),
            shape((smalls, width), f32),
            shape((2, width + 16, block), bf16),
            shape((2, chips - 1, width + 16, block), bf16),
        ),
        in_specs=[HBM, VMEM, HBM, HBM, VMEM, VMEM] + [HBM] * 6 + [VMEM, HBM, VMEM, VMEM, HBM, HBM, VMEM],
        out_specs=(VMEM,) * 4 + (HBM,) * 2,
        scratch_shapes=[
            pltpu.VMEM((slots, width), bf16),
            pltpu.VMEM((rows, width), bf16),
            pltpu.VMEM((rows, width), f32),
            pltpu.VMEM((rows, width), bf16),
            pltpu.VMEM((width, rows), bf16),
            pltpu.VMEM((width, width), bf16),
            pltpu.VMEM((rows, 3 * width), bf16),
            pltpu.VMEM((width, rows), bf16),
            pltpu.VMEM((width, 3 * width), bf16),
            pltpu.VMEM((rows, width), bf16),
            DMA((10,)),
            pltpu.VMEM((slots, width), bf16),
            pltpu.VMEM((2, width + 16, block), bf16),
            pltpu.VMEM((2, chips, width + 16, block), bf16),
            pltpu.VMEM((rows, 3 * width), bf16),
            pltpu.VMEM((rows, width), bf16),
            pltpu.VMEM((width, rows), bf16),
            pltpu.VMEM((rows, width), f32),
            pltpu.VMEM((4, 2, experts, per, half), bf16),
            pltpu.VMEM((smalls, width), f32),
            pltpu.VMEM((4, experts, per, half), bf16),
            pltpu.VMEM((4, experts, per, half), bf16),
            pltpu.VMEM((4, chips - 1, per, half), bf16),
            pltpu.VMEM((2, steps, smalls, width), bf16),
            DMA((experts,)), DMA((experts,)),
            DMA((2, chips)), DMA((2, chips)),
            DMA((2, chips)), DMA((2, chips)),
            DMA((2,)), DMA(()),
            DMA((4,)), DMA((4,)),
            DMA((4, bits)), DMA((4, bits)),
            DMA((4, chips)), DMA((4, chips)),
            DMA((4,)), DMA((4,)),
            DMA((steps,)), DMA((steps,)),
        ],
        compiler_params=pltpu.CompilerParams(
            collective_id=2, has_side_effects=True, vmem_limit_bytes=VMEM_BYTES
        ),
        name="back",
    )(*operands)


def finish_kernel(
    copies, experts,
    kept_ref, far_ref, sums_ref, small_ref, made_ref, grad_ref,
    output_ref, grad_patches_ref, gain1_ref, bias1_ref, qkv_w_ref, qv_bias_ref, out_w_ref, out_bias_ref, gain2_ref, bias2_ref, router_ref,
    in_w_ref, in_bias_ref, expert_out_ref, expert_out_bias_ref,
    turned, turned_bias,
):
    output_ref[...] = made_ref[...]
    grad_patches_ref[...] = grad_ref[...]
    width = small_ref.shape[1]
    per, half = width // experts, width // 2
    me = lax.axis_index("expert")
    me_dp = lax.axis_index("dp")

    def total(w, part):
        value = kept_ref[w, part, :].astype(f32)
        for q in range(copies // 2 - 1):
            value += far_ref[w, q, part, :].astype(f32)
        return value

    body = slice(0, width)
    in_w_ref[0] = total(0, body)
    expert_out_ref[0] = total(1, body).T
    tail = total(0, slice(width, width + 16))
    in_bias_ref[...] = tail[0:1, :]
    block = tail.shape[1]
    lines = [tail[8 + i : 9 + i, :] for i in range(-(-width // block))]
    bias_row = jnp.concatenate(lines, axis=1)[:, :width]
    turned_bias[...] = jnp.concatenate([bias_row, jnp.zeros((127, width), f32)], axis=0).T
    share = width // copies
    mine = turned_bias[pl.ds(pl.multiple_of(me_dp * share, share), share), :]
    pad = -share % 128
    mine = jnp.concatenate([mine, jnp.zeros((pad, 128), f32)], axis=0) if pad else mine
    expert_out_bias_ref[...] = mine.T[0:1, :share]
    count = small_ref.shape[0]
    turned[...] = jnp.concatenate([small_ref[...], jnp.zeros((128 - count, width), f32)], axis=0).T

    def share_of(start, n):
        value = turned[pl.ds(pl.multiple_of(start, 8), n), :]
        pad = -n % 128
        return (jnp.concatenate([value, jnp.zeros((pad, 128), f32)], axis=0) if pad else value).T

    vectors = share_of(me * per, per)
    for ref, i in [(gain1_ref, 0), (bias1_ref, 1), (out_bias_ref, 4), (gain2_ref, 5), (bias2_ref, 6)]:
        ref[...] = vectors[i : i + 1, :per].reshape(per)
    router_ref[...] = vectors[8 : 8 + experts, :per]
    values = share_of(me % (experts // 2) * 2 * per, 2 * per)
    picked = jnp.where(me < experts // 2, values[2:3, :], values[3:4, :])
    qv_bias_ref[...] = picked[:, : 2 * per].reshape(2 * per)
    for i in range(3):
        for h in range(2):
            qkv_w_ref[:, i * width + h * half : i * width + (h + 1) * half] = sums_ref[i, h].astype(f32)
    for h in range(2):
        out_w_ref[:, h * half : (h + 1) * half] = sums_ref[3, h].astype(f32)


def run_finish(copies, experts, *operands):
    smalls, width = operands[3].shape
    block = operands[0].shape[-1]
    per = width // experts
    shape = jax.ShapeDtypeStruct
    return pl.pallas_call(
        partial(finish_kernel, copies, experts),
        out_shape=(
            shape(operands[4].shape, bf16), shape(operands[5].shape, bf16),
            shape((per,), f32), shape((per,), f32), shape((per, 3 * width), f32), shape((2 * per,), f32),
            shape((per, width), f32), shape((per,), f32), shape((per,), f32), shape((per,), f32),
            shape((experts, per), f32),
            shape((1, width, block), f32), shape((1, block), f32),
            shape((1, block, width), f32), shape((1, width // copies), f32),
        ),
        in_specs=[VMEM] * 6,
        out_specs=(VMEM,) * 15,
        scratch_shapes=[pltpu.VMEM((width, 128), f32), pltpu.VMEM((width, 128), f32)],
        compiler_params=pltpu.CompilerParams(vmem_limit_bytes=VMEM_BYTES),
        name="finish",
    )(*operands)


def local(
    patches, padding, expert_ids, priority, norm1_gain, norm1_bias, qkv_weight, qv_bias, out_weight,
    out_bias, norm2_gain, norm2_bias, router, expert_in, expert_in_bias, expert_out, expert_out_bias,
    cotangent,
):
    row_count, width = patches.shape
    copies, experts = lax.axis_size("dp"), lax.axis_size("expert")
    total_rows = row_count * copies * experts
    capacity = (210 * total_rows + 100 * experts - 1) // (100 * experts)
    most = 8 * row_count // (3 * experts)
    (near_cot, raw_cot, far_slots, x_slots, gate_slots, qkv, att_t, lse, residual, second, first, pairs, probs) = run_front(
        copies, experts, most, capacity,
        patches, cotangent, priority, expert_ids.T, padding, norm1_gain, norm1_bias, qkv_weight, qv_bias,
        out_weight, out_bias, norm2_gain, norm2_bias, router.T,
    )
    d_rows, d_gates, produced, grads = run_experts(
        copies, experts, most,
        x_slots, gate_slots, near_cot, raw_cot, far_slots, expert_in[0], expert_in_bias, expert_out[0], expert_out_bias,
    )
    output, grad_patches, sums, small, kept_grads, far_grads = run_back(
        copies, experts, most,
        d_rows, d_gates, produced, grads, pairs, probs,
        second, residual, patches, cotangent, qkv, att_t, lse, first,
        norm1_gain, norm2_gain, qkv_weight, out_weight, router.T,
    )
    (output, grad_patches, n1_gain, n1_bias, qkv_w, qv, out_w, out_b, n2_gain, n2_bias, router_t, *rest) = run_finish(
        copies, experts, kept_grads, far_grads, sums, small, output, grad_patches
    )
    return (output, grad_patches, n1_gain, n1_bias, qkv_w, qv, out_w, out_b, n2_gain, n2_bias, router_t.T, *rest)


def solution(mesh):
    tokens = P(("dp", "expert"))
    wide = P(("dp", "expert"), None)
    return jax.shard_map(
        local,
        mesh=mesh,
        in_specs=(
            wide, tokens, wide, tokens, P(), P(), P(), P(), P(), P(), P(), P(), P(),
            P("expert", None, None), P("expert", None), P("expert", None, None), P("expert", None), wide,
        ),
        out_specs=(
            wide, wide, P("expert"), P("expert"), P("expert", None), P("expert"), P("expert", None),
            P("expert"), P("expert"), P("expert"), P("expert", None), P("expert", None, "dp"),
            P("expert", "dp"), P("expert", "dp", None), P("expert", "dp"),
        ),
        check_vma=False,
    )
```

```python
from functools import partial

import jax
import jax.numpy as jnp
from jax import lax
from jax.experimental import pallas as pl
from jax.experimental.pallas import tpu as pltpu
from jax.sharding import PartitionSpec as P

HEADS = 12
HEAD_DIM = 64
SEQ_LEN = 576
LOG2E = 1.4426950408889634
EPS = 1e-06
lane_count = 256
MESH = pl.DeviceIdType.MESH
NN = (((1,), (0,)), ((), ()))
NT = (((1,), (1,)), ((), ()))
TN = (((0,), (0,)), ((), ()))
VMEM_BYTES = 63 << 20
bf16 = jnp.bfloat16
f32 = jnp.float32
i32 = jnp.int32


def dot(a, b, dims=NN):
    return lax.dot_general(a, b, dims, preferred_element_type=f32)


def iota(shape, axis):
    return lax.broadcasted_iota(i32, shape, axis)


def flat(ref):
    return ref[...].reshape(1, ref.shape[0])


def ones_where(mask):
    return jnp.where(mask, 1.0, 0.0).astype(bf16)


def standardize(values):
    centred = values - jnp.mean(values, axis=-1, keepdims=True)
    inverse = lax.rsqrt(jnp.mean(centred * centred, axis=-1, keepdims=True) + EPS)
    return centred * inverse, inverse


def greet(peers):
    barrier = pltpu.get_barrier_semaphore()
    for peer in peers:
        pl.semaphore_signal(barrier, inc=1, device_id=peer, device_id_type=MESH)
    pl.semaphore_wait(barrier, len(peers))


def send(src, dst, send_sem, recv_sem, peer):
    copy = pltpu.make_async_remote_copy(
        src_ref=src, dst_ref=dst, send_sem=send_sem, recv_sem=recv_sem,
        device_id=peer, device_id_type=MESH,
    )
    copy.start()
    return copy


def front_kernel(
    copies, experts, most, capacity,
    patches_hbm, cot_hbm, priority_ref, ids_ref, padding_ref, gain1_ref, bias1_ref, qkv_w_hbm, qv_bias_ref,
    out_w_hbm, out_bias_ref, gain2_ref, bias2_ref, router_ref,
    recv_cot_hbm, raw_hbm, far_slots_ref, x_slots_hbm, gate_slots_ref, qkv_hbm, att_t_hbm, lse_ref,
    residual_hbm, second_hbm, first_t_hbm, pairs_ref, probs_ref,
    patches_ref, cot_ref, qkv_w_ref, out_w_ref, x_slots_ref, qkv_ref, att_t_ref, residual_ref, second_ref,
    first_t_ref, fetch_sem, store_sem, cot_send, rows_ref, line_ref, table, counts, cot_ss, cot_rs, near_ss, near_rs, far_ss, far_rs, raw_sem,
):
    me_dp = lax.axis_index("dp")
    me = lax.axis_index("expert")
    rows, width = patches_ref.shape
    ends = [(cot_hbm, cot_ref), (patches_hbm, patches_ref), (qkv_w_hbm, qkv_w_ref), (out_w_hbm, out_w_ref)]
    fetches = [pltpu.make_async_copy(a, b, fetch_sem.at[i]) for i, (a, b) in enumerate(ends)]
    for fetch in fetches:
        fetch.start()
    ends = [
        (qkv_ref, qkv_hbm), (first_t_ref, first_t_hbm), (att_t_ref, att_t_hbm), (residual_ref, residual_hbm),
        (second_ref, second_hbm), (x_slots_ref, x_slots_hbm),
        (cot_send.at[pl.ds(0, most)], recv_cot_hbm.at[pl.ds(0, most)]),
    ]
    stores = [pltpu.make_async_copy(a, b, store_sem.at[i]) for i, (a, b) in enumerate(ends)]
    rows_ref[0:1, :] = priority_ref[...].reshape(1, rows)
    rows_ref[1:3, :] = ids_ref[...]
    rows_ref[3:4, :] = padding_ref[...].reshape(1, rows)
    rows_ref[4:6, :] = jnp.where(rows_ref[3:4, :] > 0, rows_ref[1:3, :], experts)
    rows_ref[6:, :] = jnp.zeros((2, rows), i32)
    cols = rows_ref[...].T
    starts = range(0, rows, lane_count)
    parts = [(start, min(lane_count, rows - start)) for start in starts]

    def spot(fact, i):
        line = fact * len(parts) + i
        return (line, 0) if line < line_ref.shape[0] else (len(parts) - 1, lane_count // 2)

    line_ref[...] = jnp.zeros_like(line_ref)
    for fact, row in enumerate([0, 4, 5]):
        for i, (start, size) in enumerate(parts):
            line, at = spot(fact, i)
            line_ref[line : line + 1, at : at + size] = rows_ref[row : row + 1, start : start + size]
    greet(
        [(me_dp, me ^ o) for o in range(1, experts)]
        + [(me_dp ^ p, me) for p in range(1, copies)]
    )
    near = [
        send(line_ref, table.at[0, o], near_ss.at[o], near_rs.at[o], (me_dp, me ^ o))
        for o in range(1, experts)
    ]
    table[0, 0] = line_ref[...]
    far_half = experts // 2
    raw = send(cot_hbm, raw_hbm, raw_sem.at[0], raw_sem.at[1], (me_dp, me ^ far_half))
    expert_rows = iota((experts, rows), 0)
    before_t = ones_where(iota((rows, rows), 0) < iota((rows, rows), 1))

    def slot_rows(ids, device):
        ids = ids ^ device
        hits = [expert_rows == ids[k : k + 1, :] for k in range(2)]
        place = dot(ones_where(hits[0] | hits[1]), before_t).astype(i32) + expert_rows * most
        none = ids[0:1, :] >= experts
        return [
            jnp.where(none, -1, jnp.sum(jnp.where(hit, place, 0), axis=0, keepdims=True)) for hit in hits
        ]

    slot0_row, slot1_row = slot_rows(rows_ref[4:6, :], me)
    id0_col, id1_col = cols[:, 1:2], cols[:, 2:3]
    def taken(o):
        slots = iota((most, rows), 0) + o * most
        return ones_where((slots == slot0_row) | (slots == slot1_row))

    fetches[0].wait()
    cot_value = cot_ref[...]
    cots = []
    for o in range(far_half):
        picked = dot(taken(o), cot_value).astype(bf16)
        part = pl.ds(o * most, most)
        cot_send[part, :] = picked
        if o == 0:
            stores[6].start()
            continue
        cots.append(
            send(cot_send.at[part], recv_cot_hbm.at[part], cot_ss.at[o], cot_rs.at[o], (me_dp, me ^ o))
        )
    fetches[1].wait()
    inputs = patches_ref[...].astype(f32)
    first = (standardize(inputs)[0] * flat(gain1_ref) + flat(bias1_ref)).astype(bf16)
    first_t_ref[...] = first.T
    stores[1].start()
    fetches[2].wait()
    qkv_ref[:, :width] = (dot(first, qkv_w_ref[:, :width]) + flat(qv_bias_ref)[:, :width]).astype(bf16)
    qkv_ref[:, width : 2 * width] = dot(first, qkv_w_ref[:, width : 2 * width]).astype(bf16)
    qkv_ref[:, 2 * width :] = (
        dot(first, qkv_w_ref[:, 2 * width :]) + flat(qv_bias_ref)[:, width:]
    ).astype(bf16)
    stores[0].start()
    key_bias = jnp.where(cols[:, 3:4] > 0, 0.0, -1e30)
    scale = LOG2E * HEAD_DIM ** (-0.5)
    pair_width = 2 * HEAD_DIM

    far = [
        pltpu.make_async_remote_copy(
            table.at[0], table.at[p], far_ss.at[p], far_rs.at[p], (me_dp ^ p, me), MESH
        )
        for p in range(1, copies)
    ]

    def attend(pair, _):
        @pl.when(pair == 5)
        def _():
            for near_copy in near:
                near_copy.wait_recv()
            for far_copy in far:
                far_copy.start()

        base = pl.multiple_of(pair * pair_width, pair_width)
        q = qkv_ref[:, pl.ds(base, pair_width)]
        k = qkv_ref[:, pl.ds(base + width, pair_width)]
        v_t = qkv_ref[:, pl.ds(base + 2 * width, pair_width)].T
        lanes = iota((rows, pair_width), 1)
        outs, stats = [], []
        for a in range(2):
            k_a = jnp.where((lanes >= HEAD_DIM) == (a == 1), k, jnp.zeros((), bf16))
            scores = dot(k_a, q, NT) + key_bias
            peak = jnp.max(scores, axis=0, keepdims=True)
            raised = jnp.exp2(scores * scale - peak * scale)
            total = jnp.sum(raised, axis=0, keepdims=True)
            out = dot(v_t[a * HEAD_DIM : (a + 1) * HEAD_DIM, :], raised.astype(bf16))
            outs.append(out / total)
            stats.append(peak * scale + jnp.log2(total))
        att_t_ref[pl.ds(base, pair_width), :] = jnp.concatenate(outs, axis=0).astype(bf16)
        lse_ref[pair] = jnp.concatenate(stats + [jnp.zeros((6, rows), f32)], axis=0)
        return 0

    lax.fori_loop(0, HEADS // 2, attend, 0)
    rel0_col, rel1_col = cols[:, 4:5] ^ me, cols[:, 5:6] ^ me
    expert_cols = iota((rows, experts), 1)
    named = ones_where((expert_cols == rel0_col) | (expert_cols == rel1_col))
    before = ones_where(iota((rows, rows), 1) < iota((rows, rows), 0))
    place = dot(before, named).astype(i32) + expert_cols * most
    slot0_col = jnp.sum(jnp.where(expert_cols == rel0_col, place, 0), axis=1, keepdims=True)
    slot1_col = jnp.sum(jnp.where(expert_cols == rel1_col, place, 0), axis=1, keepdims=True)
    none_col = cols[:, 4:5] >= experts
    slot0_col, slot1_col = jnp.where(none_col, -1, slot0_col), jnp.where(none_col, -1, slot1_col)

    far_line = table[0, far_half]
    far_codes = []
    for fact in (1, 2):
        spots = [(spot(fact, i), size) for i, (start, size) in enumerate(parts)]
        pieces = [far_line[line : line + 1, at : at + size] for (line, at), size in spots]
        far_codes.append(jnp.concatenate(pieces, axis=1))
    far0_row, far1_row = slot_rows(jnp.concatenate(far_codes, axis=0), me ^ far_half)
    far_slots_ref[...] = jnp.concatenate([far0_row, far1_row, jnp.zeros((6, rows), i32)], axis=0)
    stores[2].start()
    fetches[3].wait()
    residual = inputs + dot(att_t_ref[...], out_w_ref[...], TN) + flat(out_bias_ref)
    residual_ref[...] = residual
    stores[3].start()
    second = (standardize(residual)[0] * flat(gain2_ref) + flat(bias2_ref)).astype(bf16)
    second_ref[...] = second
    stores[4].start()
    for o in range(experts):
        x_slots_ref[pl.ds(o * most, most), :] = dot(taken(o), second).astype(bf16)
    stores[5].start()
    logits = dot(second, router_ref[...], NT)
    raised = jnp.exp(logits - jnp.max(logits, axis=-1, keepdims=True))
    probs = raised / jnp.sum(raised, axis=-1, keepdims=True)
    probs_ref[...] = probs
    prob0 = jnp.sum(jnp.where(expert_cols == id0_col, probs, 0.0), axis=1, keepdims=True)
    prob1 = jnp.sum(jnp.where(expert_cols == id1_col, probs, 0.0), axis=1, keepdims=True)
    both = prob0 + prob1
    gate0, gate1 = prob0 / both, prob1 / both
    for far_copy in far:
        far_copy.wait_recv()
    counts[...] = jnp.zeros_like(counts)
    rank_col = cols[:, 0:1]

    def count(block, _):
        entry = table[block // experts, block % experts]
        ahead = jnp.zeros((rows, 2 * experts), f32)
        loads = jnp.zeros((8, 2 * experts), f32)
        for i, (start, size) in enumerate(parts):

            def fact(k):
                line, at = spot(k, i)
                return entry[line : line + 1, at : at + size]

            names = iota((experts, size), 0)
            hits = jnp.concatenate([ones_where(names == fact(1)), ones_where(names == fact(2))], axis=0)
            ahead += dot(ones_where(fact(0) < rank_col), hits, NT)
            loads += dot(jnp.ones((8, size), bf16), hits, NT)
        counts[:rows, :] += ahead
        counts[rows:, :] += loads
        return 0

    lax.fori_loop(0, copies * experts, count, 0)
    both_cols = iota((rows, 2 * experts), 1)
    ahead = counts[:rows, :]
    loads = counts[rows : rows + 1, :]
    position0 = jnp.sum(jnp.where(both_cols == id0_col, ahead, 0.0), axis=1, keepdims=True)
    position1 = jnp.sum(
        jnp.where(both_cols == id1_col + experts, ahead, 0.0)
        + jnp.where(both_cols == id1_col, loads, 0.0),
        axis=1,
        keepdims=True,
    )
    real_col = cols[:, 3:4] > 0
    kept0 = jnp.where(real_col & (position0 < capacity), 1.0, 0.0)
    kept1 = jnp.where(real_col & (position1 < capacity), 1.0, 0.0)
    gate0, gate1 = gate0 * kept0, gate1 * kept1
    for o in range(experts):
        slots = iota((rows, most), 1) + o * most
        gates = jnp.where(slots == slot0_col, gate0, 0.0) + jnp.where(slots == slot1_col, gate1, 0.0)
        gate_slots_ref[o] = jnp.sum(gates, axis=0, keepdims=True)
    lanes = iota((rows, 16), 1)
    columns = [slot0_col, slot1_col, gate0, gate1, kept0, kept1, both, cols[:, 3:4], id0_col, id1_col]
    columns = [column.astype(f32) for column in columns]
    packed = jnp.zeros((rows, 16), f32)
    for i, column in enumerate(columns):
        packed = jnp.where(lanes == i, column, packed)
    pairs_ref[...] = packed
    for copy in near + far:
        copy.wait_send()
    for copy in [*cots, raw, *stores]:
        copy.wait()


VMEM = pl.BlockSpec(memory_space=pltpu.VMEM)
HBM = pl.BlockSpec(memory_space=pl.ANY)
DMA = pltpu.SemaphoreType.DMA


def run_front(copies, experts, most, capacity, *operands):
    rows, width = operands[0].shape
    slots = experts * most
    shape = jax.ShapeDtypeStruct
    return pl.pallas_call(
        partial(front_kernel, copies, experts, most, capacity),
        out_shape=(
            shape((slots // 2, width), bf16),
            shape((rows, width), bf16),
            shape((8, rows), i32),
            shape((slots, width), bf16),
            shape((experts, 1, most), f32),
            shape((rows, 3 * width), bf16),
            shape((width, rows), bf16),
            shape((HEADS // 2, 8, rows), f32),
            shape((rows, width), f32),
            shape((rows, width), bf16),
            shape((width, rows), bf16),
            shape((rows, 16), f32),
            shape((rows, experts), f32),
        ),
        in_specs=[HBM] * 2 + [VMEM] * 5 + [HBM, VMEM, HBM] + [VMEM] * 4,
        out_specs=(HBM, HBM, VMEM, HBM, VMEM, HBM, HBM, VMEM, HBM, HBM, HBM, VMEM, VMEM),
        scratch_shapes=[
            pltpu.VMEM((rows, width), bf16),
            pltpu.VMEM((rows, width), bf16),
            pltpu.VMEM((width, 3 * width), bf16),
            pltpu.VMEM((width, width), bf16),
            pltpu.VMEM((slots, width), bf16),
            pltpu.VMEM((rows, 3 * width), bf16),
            pltpu.VMEM((width, rows), bf16),
            pltpu.VMEM((rows, width), f32),
            pltpu.VMEM((rows, width), bf16),
            pltpu.VMEM((width, rows), bf16),
            DMA((4,)), DMA((7,)),
            pltpu.VMEM((slots // 2, width), bf16),
            pltpu.VMEM((8, rows), i32),
            pltpu.VMEM((8, lane_count), i32),
            pltpu.VMEM((copies, experts, 8, lane_count), i32),
            pltpu.VMEM((rows + 8, 2 * experts), f32),
            DMA((experts,)), DMA((experts,)),
            DMA((experts,)), DMA((experts,)),
            DMA((copies,)), DMA((copies,)), DMA((2,)),
        ],
        compiler_params=pltpu.CompilerParams(
            collective_id=0, has_side_effects=True, vmem_limit_bytes=VMEM_BYTES
        ),
        name="front",
    )(*operands)


def gelu_parts(values):
    bell = jnp.exp2(values * values * (-0.5 * LOG2E))
    t = 1.0 / (1.0 + (0.3275911 * 0.5**0.5) * jnp.abs(values))
    tail = t * (0.1274147959 + t * (-0.142248368 + t * (0.7107068705 + t * (-0.7265760135 + t * 0.5307027145))))
    tail = tail * bell
    share = jnp.where(values >= 0, 1.0 - tail, tail)
    return values * share, share + values * bell * 0.3989422804014327


def to_column(row):
    n = row.shape[1]
    return jnp.sum(jnp.where(iota((n, n), 0) == iota((n, n), 1), row, 0.0), axis=1, keepdims=True)


def to_row(column):
    n = column.shape[0]
    return jnp.sum(jnp.where(iota((n, n), 0) == iota((n, n), 1), column, 0.0), axis=0, keepdims=True)


def expert_kernel(
    copies, experts, most, chunks, tile,
    x_ref, gates_ref, near_cot_ref, raw_ref, far_slots_ref, in_w_hbm, in_bias_ref, out_w_hbm, out_bias_ref,
    d_rows_ref, d_gates_ref, produced_ref, grads_ref,
    in_w_ref, out_w_ref, cot_ref, send_cot, recv_x, recv_g, send_d, send_g, hidden, d_pre, x_t, d_t, bias_sum, total_p, total_d, stage,
    x_ss, x_rs, g_ss, g_rs, d_ss, d_rs, dg_ss, dg_rs, own_sem, own_d_sem, stage_sem,
    cot_ss, cot_rs, near_sem, fetch_sem,
):
    me_dp = lax.axis_index("dp")
    me = lax.axis_index("expert")
    width, hidden_width = in_w_ref.shape
    rows = chunks * most
    block = hidden_width // copies

    def chunk(o):
        return pl.ds(pl.multiple_of(o * most, most), most)

    def move_x(o):
        return pltpu.make_async_remote_copy(
            x_ref.at[chunk(o)], recv_x.at[chunk(o)], x_ss.at[o], x_rs.at[o], (me_dp, me ^ o), MESH
        )

    def move_g(o):
        return pltpu.make_async_remote_copy(
            gates_ref.at[o], recv_g.at[o], g_ss.at[o], g_rs.at[o], (me_dp, me ^ o), MESH
        )

    def move_d(o):
        return pltpu.make_async_remote_copy(
            send_d.at[chunk(o)], d_rows_ref.at[chunk(o)], d_ss.at[o], d_rs.at[o], (me_dp, me ^ o), MESH
        )

    def move_dg(o):
        return pltpu.make_async_remote_copy(
            send_g.at[o], d_gates_ref.at[o], dg_ss.at[o], dg_rs.at[o], (me_dp, me ^ o), MESH
        )

    far_half = experts // 2

    def move_cot(j):
        return pltpu.make_async_remote_copy(
            send_cot.at[chunk(j)], cot_ref.at[chunk(far_half + j)], cot_ss.at[j], cot_rs.at[j],
            (me_dp, me ^ j), MESH,
        )

    fetches = [
        pltpu.make_async_copy(in_w_hbm, in_w_ref, fetch_sem.at[0]),
        pltpu.make_async_copy(out_w_hbm, out_w_ref, fetch_sem.at[1]),
    ]
    for fetch in fetches:
        fetch.start()
    own = pltpu.make_async_copy(x_ref.at[chunk(0)], recv_x.at[chunk(0)], own_sem)
    own.start()
    half_slots = near_cot_ref.shape[0]
    near_cot = pltpu.make_async_copy(near_cot_ref, cot_ref.at[pl.ds(0, half_slots)], near_sem)
    near_cot.start()
    greet([(me_dp, me ^ o) for o in range(1, experts)])

    def begin(g):
        for o in range(max(1, g * chunks), (g + 1) * chunks):
            move_g(o).start()
            move_x(o).start()

    groups = experts // chunks
    order = [0, *range(groups // 2, groups), *range(1, groups // 2)]
    begin(order[0])
    begin(order[1])
    for j in [*range(1, far_half), 0]:
        places = iota((most, raw_ref.shape[0]), 0) + (far_half + j) * most
        taken = ones_where((places == far_slots_ref[0:1, :]) | (places == far_slots_ref[1:2, :]))
        picked = dot(taken, raw_ref[...]).astype(bf16)
        if j == 0:
            cot_ref[chunk(far_half), :] = picked
        else:
            send_cot[chunk(j), :] = picked
            move_cot(j).start()
    near_cot.wait()
    for fetch in fetches:
        fetch.wait()
    recv_g[0] = gates_ref[0]
    bias_sum[...] = jnp.zeros_like(bias_sum)
    x_t[width:, :] = jnp.ones_like(x_t[width:, :])
    own.wait()
    own_d = pltpu.make_async_copy(send_d.at[chunk(0)], d_rows_ref.at[chunk(0)], own_d_sem)

    def work(n, _):
        g = n % 2 * (groups // 2) + n // 2
        for j in range(chunks):
            o = g * chunks + j

            @pl.when(o > 0)
            def _():
                move_g(o).wait_recv()
                move_x(o).wait_recv()

            @pl.when(o > far_half)
            def _():
                move_cot(o - far_half).wait_recv()

        at = pl.multiple_of(g * rows, rows)
        here = pl.ds(at, rows)
        gate = jnp.concatenate([to_column(recv_g[g * chunks + j]) for j in range(chunks)], axis=0)
        x = recv_x[here, :]
        cot = cot_ref[here, :].astype(f32)
        d_produced = (cot * gate).astype(bf16)
        bias_sum[0:1, :] += jnp.sum(d_produced.astype(f32), axis=0, keepdims=True)
        x_t[:width, here] = x.T
        d_t[:, here] = d_produced.T
        total_p[...] = jnp.zeros_like(total_p)
        total_d[...] = jnp.zeros_like(total_d)

        def step(n, _):
            cols = pl.ds(pl.multiple_of(n * tile, tile), tile)
            pre = dot(x, in_w_ref[:, cols]) + in_bias_ref[:, cols]
            value, slope = gelu_parts(pre)
            value = value.astype(bf16)
            hidden[here, cols] = value
            total_p[...] += dot(value, out_w_ref[cols, :])
            d_value = (dot(d_produced, out_w_ref[cols, :], NT) * slope).astype(bf16)
            d_pre[here, cols] = d_value
            total_d[...] += dot(d_value, in_w_ref[:, cols], NT)
            return 0

        lax.fori_loop(0, hidden_width // tile, step, 0)

        @pl.when(n == 0)
        def _():
            for later in order[2:]:
                begin(later)

        send_d[here, :] = total_d[...].astype(bf16)
        produced = (total_p[...] + out_bias_ref[...]).astype(bf16)
        produced_ref[here, :] = produced
        d_gate = jnp.sum(produced.astype(f32) * cot, axis=1, keepdims=True)
        for j in range(chunks):
            o = g * chunks + j
            d_gate_row = to_row(d_gate[j * most : (j + 1) * most, :])
            send_g[o] = d_gate_row

            @pl.when(o > 0)
            def _():
                move_d(o).start()
                move_dg(o).start()

            @pl.when(o == 0)
            def _():
                own_d.start()
                d_gates_ref[0] = d_gate_row

        return 0

    lax.fori_loop(0, groups, work, 0)

    def store(w, p):
        return pltpu.make_async_copy(stage.at[w], grads_ref.at[w, p], stage_sem.at[w])

    def weigh(p, _):
        cols = pl.ds(pl.multiple_of((me_dp ^ p) * block, block), block)

        @pl.when(p > 0)
        def _():
            store(0, p - 1).wait()

        total = dot(x_t[...], d_pre[:, cols])
        stage[0, :width, :] = total[:width, :].astype(bf16)
        tail = total[width:, :]
        lines = iota((16, block), 0)
        for i in range(-(-width // block)):
            tail = jnp.where(lines == 8 + i, bias_sum[0:1, i * block : (i + 1) * block], tail)
        stage[0, width:, :] = tail.astype(bf16)
        store(0, p).start()

        @pl.when(p > 0)
        def _():
            store(1, p - 1).wait()

        stage[1, :width, :] = dot(d_t[...], hidden[:, cols]).astype(bf16)
        stage[1, width:, :] = jnp.zeros((16, block), bf16)
        store(1, p).start()
        return 0

    lax.fori_loop(0, copies, weigh, 0)
    store(0, copies - 1).wait()
    store(1, copies - 1).wait()
    own_d.wait()
    for j in range(1, far_half):
        move_cot(j).wait_send()
    for o in range(1, experts):
        move_g(o).wait_send()
        move_x(o).wait_send()
        move_d(o).wait()
        move_dg(o).wait()


def run_experts(copies, experts, most, *operands):
    slots, width = operands[0].shape
    hidden_width = operands[5].shape[1]
    chunks = max(1, min(experts, 384 // most))
    rows = chunks * most
    block = hidden_width // copies
    shape = jax.ShapeDtypeStruct
    return pl.pallas_call(
        partial(expert_kernel, copies, experts, most, chunks, 768),
        out_shape=(
            shape((slots, width), bf16),
            shape((experts, 1, most), f32),
            shape((slots, width), bf16),
            shape((2, copies, width + 16, block), bf16),
        ),
        in_specs=[HBM, VMEM, HBM] + [VMEM] * 2 + [HBM, VMEM] * 2,
        out_specs=(HBM, VMEM, VMEM, HBM),
        scratch_shapes=[
            pltpu.VMEM((width, hidden_width), bf16),
            pltpu.VMEM((hidden_width, width), bf16),
            pltpu.VMEM((slots, width), bf16),
            pltpu.VMEM((slots // 2, width), bf16),
            pltpu.VMEM((slots, width), bf16),
            pltpu.VMEM((experts, 1, most), f32),
            pltpu.VMEM((slots, width), bf16),
            pltpu.VMEM((experts, 1, most), f32),
            pltpu.VMEM((slots, hidden_width), bf16),
            pltpu.VMEM((slots, hidden_width), bf16),
            pltpu.VMEM((width + 16, slots), bf16),
            pltpu.VMEM((width, slots), bf16),
            pltpu.VMEM((8, width), f32),
            pltpu.VMEM((rows, width), f32),
            pltpu.VMEM((rows, width), f32),
            pltpu.VMEM((2, width + 16, block), bf16),
        ]
        + [DMA((experts,))] * 8
        + [DMA(()), DMA(()), DMA((2,)), DMA((experts // 2,)), DMA((experts // 2,)), DMA(()), DMA((2,))],
        compiler_params=pltpu.CompilerParams(
            collective_id=1, has_side_effects=True, vmem_limit_bytes=VMEM_BYTES
        ),
        name="experts",
    )(*operands)


def back_kernel(
    copies, experts, most,
    d_rows_hbm, d_gates_ref, produced_ref, grads_ref, pairs_ref, probs_ref,
    second_hbm, residual_hbm, patches_hbm, cot_hbm, qkv_hbm, att_t_hbm, lse_ref, first_t_hbm,
    gain1_ref, gain2_ref, qkv_w_hbm, out_w_hbm, router_ref,
    output_ref, grad_patches_ref, sums_ref, small_sums_ref, kept_grads_ref, far_grads_ref,
    d_rows_ref, second_ref, residual_ref, cot_ref, att_t_ref, out_w_ref, qkv_ref, first_t_ref, qkv_w_ref,
    patches_ref, fetch_sem,
    recv_p, own_grads, near_grads, d_qkv, d_att, d_att_t, d_residual_ref,
    dense, small, halves, landed, crossed, tiny,
    p_ss, p_rs, n_ss, n_rs, f_ss, f_rs, own_sem, kept_sem,
    a_ss, a_rs, b_ss, b_rs, c_ss, c_rs, e_ss, e_rs, t_ss, t_rs,
):
    me_dp = lax.axis_index("dp")
    me = lax.axis_index("expert")
    rows, width = patches_ref.shape
    ends = [
        (d_rows_hbm, d_rows_ref), (second_hbm, second_ref), (residual_hbm, residual_ref), (cot_hbm, cot_ref),
        (att_t_hbm, att_t_ref), (out_w_hbm, out_w_ref), (qkv_hbm, qkv_ref), (first_t_hbm, first_t_ref),
        (qkv_w_hbm, qkv_w_ref), (patches_hbm, patches_ref),
    ]
    fetches = [pltpu.make_async_copy(a, b, fetch_sem.at[i]) for i, (a, b) in enumerate(ends)]
    for fetch in fetches:
        fetch.start()
    slots = experts * most
    chips = copies // 2
    core = me_dp % 2
    per = width // experts
    half = width // 2
    partner = (me_dp ^ 1, me)
    bits = list(range(experts.bit_length() - 1))
    steps = [(me_dp ^ (1 << i), me) for i in range(copies.bit_length() - 1)]
    steps += [(me_dp, me ^ (1 << i)) for i in range(experts.bit_length() - 1)]

    def copy_a(m):
        return pltpu.make_async_remote_copy(
            dense.at[m, 1 - core], halves.at[m], a_ss.at[m], a_rs.at[m], partner, MESH
        )

    def copy_b(m, i):
        part = pl.ds(experts >> (i + 1), experts >> (i + 1))
        return pltpu.make_async_remote_copy(
            dense.at[m, core, part], landed.at[m, part], b_ss.at[m, i], b_rs.at[m, i],
            (me_dp, me ^ (1 << bits[i])), MESH,
        )

    def copy_c(m, q):
        return pltpu.make_async_remote_copy(
            dense.at[m, core, 0], crossed.at[m, q - 1], c_ss.at[m, q], c_rs.at[m, q],
            (me_dp ^ (2 * q), me), MESH,
        )

    def copy_e(m):
        return pltpu.make_async_remote_copy(
            sums_ref.at[m, core], sums_ref.at[m, core], e_ss.at[m], e_rs.at[m], partner, MESH
        )

    def begin(m, k):
        if k == 0:
            copy_a(m).start()
        elif k <= len(bits):
            copy_b(m, k - 1).start()
        elif k == len(bits) + 1:
            for q in range(1, chips):
                copy_c(m, q).start()
        else:
            copy_e(m).start()

    def end(m, k):
        if k == 0:
            copy_a(m).wait_recv()
            dense[m, core] = (dense[m, core].astype(f32) + halves[m].astype(f32)).astype(bf16)
        elif k <= len(bits):
            copy_b(m, k - 1).wait_recv()
            n = experts >> k
            total = dense[m, core, 0:n].astype(f32) + landed[m, n : 2 * n].astype(f32)
            dense[m, core, 0:n] = total.astype(bf16)
        elif k == len(bits) + 1:
            total = dense[m, core, 0].astype(f32)
            for q in range(1, chips):
                copy_c(m, q).wait_recv()
                total += crossed[m, q - 1].astype(f32)
            sums_ref[m, core] = total.astype(bf16)

    stages = [0] * 4

    def advance(m):
        if stages[m] < len(bits) + 2:
            end(m, stages[m])
            stages[m] += 1
            begin(m, stages[m])

    def copy_t(i):
        return pltpu.make_async_remote_copy(tiny.at[0, i], tiny.at[1, i], t_ss.at[i], t_rs.at[i], steps[i], MESH)

    def begin_small(i):
        tiny[0, i] = small[...].astype(bf16)
        copy_t(i).start()

    todo = list(range(len(steps)))

    def advance_small():
        if todo:
            i = todo.pop(0)
            copy_t(i).wait_recv()
            small[...] += tiny[1, i].astype(f32)
            if i + 1 < len(steps):
                begin_small(i + 1)

    def copy_f(w, q):
        return pltpu.make_async_remote_copy(
            near_grads.at[w, q], far_grads_ref.at[w, q - 1], f_ss.at[w, q], f_rs.at[w, q],
            (me_dp ^ (2 * q), me), MESH,
        )

    greet(
        [(me_dp, me ^ o) for o in range(1, experts)]
        + [partner]
        + [(me_dp ^ (2 * q), me) for q in range(1, chips)]
    )
    near = [
        send(grads_ref.at[w, 2 * q + 1], near_grads.at[w, q], n_ss.at[w, q], n_rs.at[w, q], partner)
        for q in range(chips)
        for w in range(2)
    ]
    turns = [(w, q) for q in [*range(1, chips), 0] for w in range(2)]
    own = [
        pltpu.make_async_copy(grads_ref.at[w, 2 * q], own_grads.at[i % 2], own_sem.at[i % 2])
        for i, (w, q) in enumerate(turns)
    ]
    for copy in own[:2]:
        copy.start()
    returns = []
    for o in range(1, experts):
        part = pl.ds(o * most, most)
        returns.append(
            send(produced_ref.at[part], recv_p.at[part], p_ss.at[o], p_rs.at[o], (me_dp, me ^ o))
        )
    own_p = pltpu.make_async_copy(
        produced_ref.at[pl.ds(0, most)], recv_p.at[pl.ds(0, most)], p_rs.at[0]
    )
    own_p.start()
    slot0, slot1 = pairs_ref[:, 0:1].astype(i32), pairs_ref[:, 1:2].astype(i32)
    kept0, kept1, both = pairs_ref[:, 4:5], pairs_ref[:, 5:6], pairs_ref[:, 6:7]
    places = iota((rows, slots), 1)
    fetches[0].wait()
    d_second = dot(ones_where((places == slot0) | (places == slot1)), d_rows_ref[...])
    d_gate0 = jnp.zeros((rows, 1), f32)
    d_gate1 = jnp.zeros((rows, 1), f32)
    for o in range(experts):
        part = iota((rows, most), 1) + o * most
        line = d_gates_ref[o]
        d_gate0 += jnp.sum(jnp.where(part == slot0, line, 0.0), axis=1, keepdims=True)
        d_gate1 += jnp.sum(jnp.where(part == slot1, line, 0.0), axis=1, keepdims=True)
    d_gate0, d_gate1 = d_gate0 * kept0, d_gate1 * kept1
    probs = probs_ref[...]
    names = iota((rows, experts), 1)
    is0, is1 = names == pairs_ref[:, 8:9].astype(i32), names == pairs_ref[:, 9:10].astype(i32)
    share0 = jnp.sum(jnp.where(is0, probs, 0.0), axis=1, keepdims=True) / both
    share1 = jnp.sum(jnp.where(is1, probs, 0.0), axis=1, keepdims=True) / both
    centre = d_gate0 * share0 + d_gate1 * share1
    d_probs = jnp.where(is0, (d_gate0 - centre) / both, 0.0) + jnp.where(is1, (d_gate1 - centre) / both, 0.0)
    d_logits = (probs * (d_probs - jnp.sum(probs * d_probs, axis=1, keepdims=True))).astype(bf16)
    small[8:, :] = jnp.zeros_like(small[8:, :])
    fetches[1].wait()
    small[8 : 8 + experts, :] = dot(d_logits, second_ref[...], TN)
    d_second += dot(d_logits, router_ref[...])
    fetches[2].wait()
    fetches[3].wait()
    n, inverse = standardize(residual_ref[...])
    small[5:6, :] = jnp.sum(d_second * n, axis=0, keepdims=True)
    small[6:7, :] = jnp.sum(d_second, axis=0, keepdims=True)
    m = d_second * flat(gain2_ref)
    d_residual = cot_ref[...].astype(f32) + inverse * (
        m - jnp.mean(m, axis=-1, keepdims=True) - n * jnp.mean(m * n, axis=-1, keepdims=True)
    )
    d_residual_ref[...] = d_residual
    d_branch = d_residual.astype(bf16)
    small[4:5, :] = jnp.sum(d_branch.astype(f32), axis=0, keepdims=True)
    small[7:8, :] = jnp.zeros((1, width), f32)

    def keep(matrix, h, value):
        for e in range(experts):
            r = e ^ me
            at = 0
            for bit in bits:
                at = at * 2 + (r // (1 << bit)) % 2
            dense[matrix, h, at] = value[e * per : (e + 1) * per, :].astype(bf16)

    fetches[4].wait()
    for h in range(2):
        keep(3, h, dot(att_t_ref[...], d_branch[:, h * half : (h + 1) * half]))
    begin(3, 0)
    for copy in near:
        copy.wait_recv()
    for i, (w, q) in enumerate(turns):
        own[i].wait()
        near_grads[w, q] = (own_grads[i % 2].astype(f32) + near_grads[w, q].astype(f32)).astype(bf16)
        if i + 2 < len(turns):
            own[i + 2].start()
        if q > 0:
            copy_f(w, q).start()
    kept = pltpu.make_async_copy(near_grads.at[:, 0], kept_grads_ref, kept_sem)
    kept.start()
    advance(3)
    fetches[5].wait()
    d_att[...] = dot(d_branch, out_w_ref[...], NT).astype(bf16)
    d_att_t[...] = dot(out_w_ref[...], d_branch, NT).astype(bf16)
    key_bias = jnp.where(pairs_ref[:, 7:8] > 0, 0.0, -1e30)
    scale = LOG2E * HEAD_DIM ** (-0.5)
    pair_width = 2 * HEAD_DIM

    def columns(i, h):
        return slice(i * width + h * half, i * width + (h + 1) * half)

    def attend(pair, _):
        @pl.when(pair == 3)
        def _():
            for i in range(3):
                keep(i, 0, dot(first_t_ref[...], d_qkv[:, columns(i, 0)]))

                @pl.when(core == 1)
                def _():
                    begin(i, 0)

        @pl.when((pair == 5) & (core == 0))
        def _():
            for i in range(3):
                end(i, 0)
                begin(i, 1)

        base = pl.multiple_of(pair * pair_width, pair_width)
        here = pl.ds(base, pair_width)
        q = qkv_ref[:, here]
        k = qkv_ref[:, pl.ds(base + width, pair_width)]
        v = qkv_ref[:, pl.ds(base + 2 * width, pair_width)]
        k_t = k.T
        d_out = d_att[:, here]
        products = att_t_ref[here, :].astype(f32) * d_att_t[here, :].astype(f32)
        lanes = iota((rows, pair_width), 1)
        d_q, d_k, d_v = [], [], []
        for a in range(2):
            mine = (lanes >= HEAD_DIM) == (a == 1)
            k_a = jnp.where(mine, k, jnp.zeros((), bf16))
            v_a = jnp.where(mine, v, jnp.zeros((), bf16))
            part = slice(a * HEAD_DIM, (a + 1) * HEAD_DIM)
            delta = jnp.sum(products[part, :], axis=0, keepdims=True)
            weights = jnp.exp2((dot(k_a, q, NT) + key_bias) * scale - lse_ref[pair][a : a + 1, :])
            d_scores = (weights * (dot(v_a, d_out, NT) - delta)).astype(bf16)
            d_v.append(dot(weights.astype(bf16), d_out))
            d_k.append(dot(d_scores, q))
            d_q.append(dot(k_t[part, :], d_scores))
        low = lanes < HEAD_DIM
        down = HEAD_DIM ** (-0.5)
        d_qkv[:, here] = (jnp.concatenate(d_q, axis=0).T * down).astype(bf16)
        d_qkv[:, pl.ds(base + width, pair_width)] = (jnp.where(low, d_k[0], d_k[1]) * down).astype(bf16)
        d_qkv[:, pl.ds(base + 2 * width, pair_width)] = jnp.where(low, d_v[0], d_v[1]).astype(bf16)
        return 0

    fetches[6].wait()
    fetches[7].wait()
    lax.fori_loop(0, HEADS // 2, attend, 0)
    advance(3)
    for fetch in fetches[8:]:
        fetch.wait()
    def combine_results():
        own_p.wait()
        for copy in returns:
            copy.wait()
        blocks = 3
        lines = rows // blocks

        def combine(i, _):
            part = pl.ds(pl.multiple_of(i * lines, lines), lines)
            facts = pairs_ref[part, :]
            spots = iota((lines, slots), 1)
            output_ref[part, :] = (
                residual_ref[part, :]
                + facts[:, 2:3] * dot(ones_where(spots == facts[:, 0:1].astype(i32)), recv_p[...])
                + facts[:, 3:4] * dot(ones_where(spots == facts[:, 1:2].astype(i32)), recv_p[...])
            ).astype(bf16)
            return 0

        lax.fori_loop(0, blocks, combine, 0)

    ones = jnp.ones((8, rows), bf16)
    for i in range(3):
        keep(i, 1, dot(first_t_ref[...], d_qkv[:, columns(i, 1)]))

        @pl.when(core == 0)
        def _():
            begin(i, 0)

        if i > 0:

            @pl.when(core == 1)
            def _():
                end(i - 1, 0)
                begin(i - 1, 1)

    for i in (0, 2):
        part = slice(i * width, (i + 1) * width)
        small[2 + i // 2 : 3 + i // 2, :] = dot(ones, d_qkv[:, part])[0:1, :]

    @pl.when(core == 1)
    def _():
        end(2, 0)
        begin(2, 1)

    stages[0:3] = [1, 1, 1]
    d_first = dot(d_qkv[...], qkv_w_ref[...], NT)
    n, inverse = standardize(patches_ref[...].astype(f32))
    small[0:1, :] = jnp.sum(d_first * n, axis=0, keepdims=True)
    small[1:2, :] = jnp.sum(d_first, axis=0, keepdims=True)
    begin_small(0)
    m = d_first * flat(gain1_ref)
    grad_patches_ref[...] = (
        d_residual_ref[...]
        + inverse * (m - jnp.mean(m, axis=-1, keepdims=True) - n * jnp.mean(m * n, axis=-1, keepdims=True))
    ).astype(bf16)
    for turn in range(len(bits) + 2):
        for m in [3, 0, 1, 2]:
            advance(m)
        advance_small()
        if turn == 0:
            combine_results()
    while todo:
        advance_small()
    small_sums_ref[...] = small[...]
    for copy in near:
        copy.wait_send()
    kept.wait()
    for q in range(1, chips):
        for w in range(2):
            copy_f(w, q).wait()
    for m in range(4):
        copy_a(m).wait_send()
        for i in range(len(bits)):
            copy_b(m, i).wait_send()
        for q in range(1, chips):
            copy_c(m, q).wait_send()
        pltpu.make_async_remote_copy(
            sums_ref.at[m, core], sums_ref.at[m, 1 - core], e_ss.at[m], e_rs.at[m], partner, MESH
        ).wait()
    for i in range(len(steps)):
        copy_t(i).wait_send()


def run_back(copies, experts, most, *operands):
    rows, width = operands[8].shape
    slots = experts * most
    chips = copies // 2
    block = operands[3].shape[-1]
    shape = jax.ShapeDtypeStruct
    smalls = -(-(8 + experts) // 16) * 16
    per, half = width // experts, width // 2
    bits = experts.bit_length() - 1
    steps = copies.bit_length() - 1 + bits
    return pl.pallas_call(
        partial(back_kernel, copies, experts, most),
        out_shape=(
            shape((rows, width), bf16),
            shape((rows, width), bf16),
            shape((4, 2, per, half), bf16),
            shape((smalls, width), f32),
            shape((2, width + 16, block), bf16),
            shape((2, chips - 1, width + 16, block), bf16),
        ),
        in_specs=[HBM, VMEM, HBM, HBM, VMEM, VMEM] + [HBM] * 6 + [VMEM, HBM, VMEM, VMEM, HBM, HBM, VMEM],
        out_specs=(VMEM,) * 4 + (HBM,) * 2,
        scratch_shapes=[
            pltpu.VMEM((slots, width), bf16),
            pltpu.VMEM((rows, width), bf16),
            pltpu.VMEM((rows, width), f32),
            pltpu.VMEM((rows, width), bf16),
            pltpu.VMEM((width, rows), bf16),
            pltpu.VMEM((width, width), bf16),
            pltpu.VMEM((rows, 3 * width), bf16),
            pltpu.VMEM((width, rows), bf16),
            pltpu.VMEM((width, 3 * width), bf16),
            pltpu.VMEM((rows, width), bf16),
            DMA((10,)),
            pltpu.VMEM((slots, width), bf16),
            pltpu.VMEM((2, width + 16, block), bf16),
            pltpu.VMEM((2, chips, width + 16, block), bf16),
            pltpu.VMEM((rows, 3 * width), bf16),
            pltpu.VMEM((rows, width), bf16),
            pltpu.VMEM((width, rows), bf16),
            pltpu.VMEM((rows, width), f32),
            pltpu.VMEM((4, 2, experts, per, half), bf16),
            pltpu.VMEM((smalls, width), f32),
            pltpu.VMEM((4, experts, per, half), bf16),
            pltpu.VMEM((4, experts, per, half), bf16),
            pltpu.VMEM((4, chips - 1, per, half), bf16),
            pltpu.VMEM((2, steps, smalls, width), bf16),
            DMA((experts,)), DMA((experts,)),
            DMA((2, chips)), DMA((2, chips)),
            DMA((2, chips)), DMA((2, chips)),
            DMA((2,)), DMA(()),
            DMA((4,)), DMA((4,)),
            DMA((4, bits)), DMA((4, bits)),
            DMA((4, chips)), DMA((4, chips)),
            DMA((4,)), DMA((4,)),
            DMA((steps,)), DMA((steps,)),
        ],
        compiler_params=pltpu.CompilerParams(
            collective_id=2, has_side_effects=True, vmem_limit_bytes=VMEM_BYTES
        ),
        name="back",
    )(*operands)


def finish_kernel(
    copies, experts,
    kept_ref, far_ref, sums_ref, small_ref, made_ref, grad_ref,
    output_ref, grad_patches_ref, gain1_ref, bias1_ref, qkv_w_ref, qv_bias_ref, out_w_ref, out_bias_ref, gain2_ref, bias2_ref, router_ref,
    in_w_ref, in_bias_ref, expert_out_ref, expert_out_bias_ref,
    turned, turned_bias,
):
    output_ref[...] = made_ref[...]
    grad_patches_ref[...] = grad_ref[...]
    width = small_ref.shape[1]
    per, half = width // experts, width // 2
    me = lax.axis_index("expert")
    me_dp = lax.axis_index("dp")

    def total(w, part):
        value = kept_ref[w, part, :].astype(f32)
        for q in range(copies // 2 - 1):
            value += far_ref[w, q, part, :].astype(f32)
        return value

    body = slice(0, width)
    in_w_ref[0] = total(0, body)
    expert_out_ref[0] = total(1, body).T
    tail = total(0, slice(width, width + 16))
    in_bias_ref[...] = tail[0:1, :]
    block = tail.shape[1]
    lines = [tail[8 + i : 9 + i, :] for i in range(-(-width // block))]
    bias_row = jnp.concatenate(lines, axis=1)[:, :width]
    turned_bias[...] = jnp.concatenate([bias_row, jnp.zeros((127, width), f32)], axis=0).T
    share = width // copies
    mine = turned_bias[pl.ds(pl.multiple_of(me_dp * share, share), share), :]
    pad = -share % 128
    mine = jnp.concatenate([mine, jnp.zeros((pad, 128), f32)], axis=0) if pad else mine
    expert_out_bias_ref[...] = mine.T[0:1, :share]
    count = small_ref.shape[0]
    turned[...] = jnp.concatenate([small_ref[...], jnp.zeros((128 - count, width), f32)], axis=0).T

    def share_of(start, n):
        value = turned[pl.ds(pl.multiple_of(start, 8), n), :]
        pad = -n % 128
        return (jnp.concatenate([value, jnp.zeros((pad, 128), f32)], axis=0) if pad else value).T

    vectors = share_of(me * per, per)
    for ref, i in [(gain1_ref, 0), (bias1_ref, 1), (out_bias_ref, 4), (gain2_ref, 5), (bias2_ref, 6)]:
        ref[...] = vectors[i : i + 1, :per].reshape(per)
    router_ref[...] = vectors[8 : 8 + experts, :per]
    values = share_of(me % (experts // 2) * 2 * per, 2 * per)
    picked = jnp.where(me < experts // 2, values[2:3, :], values[3:4, :])
    qv_bias_ref[...] = picked[:, : 2 * per].reshape(2 * per)
    for i in range(3):
        for h in range(2):
            qkv_w_ref[:, i * width + h * half : i * width + (h + 1) * half] = sums_ref[i, h].astype(f32)
    for h in range(2):
        out_w_ref[:, h * half : (h + 1) * half] = sums_ref[3, h].astype(f32)


def run_finish(copies, experts, *operands):
    smalls, width = operands[3].shape
    block = operands[0].shape[-1]
    per = width // experts
    shape = jax.ShapeDtypeStruct
    return pl.pallas_call(
        partial(finish_kernel, copies, experts),
        out_shape=(
            shape(operands[4].shape, bf16), shape(operands[5].shape, bf16),
            shape((per,), f32), shape((per,), f32), shape((per, 3 * width), f32), shape((2 * per,), f32),
            shape((per, width), f32), shape((per,), f32), shape((per,), f32), shape((per,), f32),
            shape((experts, per), f32),
            shape((1, width, block), f32), shape((1, block), f32),
            shape((1, block, width), f32), shape((1, width // copies), f32),
        ),
        in_specs=[VMEM] * 6,
        out_specs=(VMEM,) * 15,
        scratch_shapes=[pltpu.VMEM((width, 128), f32), pltpu.VMEM((width, 128), f32)],
        compiler_params=pltpu.CompilerParams(vmem_limit_bytes=VMEM_BYTES),
        name="finish",
    )(*operands)


def local(
    patches, padding, expert_ids, priority, norm1_gain, norm1_bias, qkv_weight, qv_bias, out_weight,
    out_bias, norm2_gain, norm2_bias, router, expert_in, expert_in_bias, expert_out, expert_out_bias,
    cotangent,
):
    row_count, width = patches.shape
    copies, experts = lax.axis_size("dp"), lax.axis_size("expert")
    total_rows = row_count * copies * experts
    capacity = (210 * total_rows + 100 * experts - 1) // (100 * experts)
    most = 8 * row_count // (3 * experts)
    (near_cot, raw_cot, far_slots, x_slots, gate_slots, qkv, att_t, lse, residual, second, first, pairs, probs) = run_front(
        copies, experts, most, capacity,
        patches, cotangent, priority, expert_ids.T, padding, norm1_gain, norm1_bias, qkv_weight, qv_bias,
        out_weight, out_bias, norm2_gain, norm2_bias, router.T,
    )
    d_rows, d_gates, produced, grads = run_experts(
        copies, experts, most,
        x_slots, gate_slots, near_cot, raw_cot, far_slots, expert_in[0], expert_in_bias, expert_out[0], expert_out_bias,
    )
    output, grad_patches, sums, small, kept_grads, far_grads = run_back(
        copies, experts, most,
        d_rows, d_gates, produced, grads, pairs, probs,
        second, residual, patches, cotangent, qkv, att_t, lse, first,
        norm1_gain, norm2_gain, qkv_weight, out_weight, router.T,
    )
    (output, grad_patches, n1_gain, n1_bias, qkv_w, qv, out_w, out_b, n2_gain, n2_bias, router_t, *rest) = run_finish(
        copies, experts, kept_grads, far_grads, sums, small, output, grad_patches
    )
    return (output, grad_patches, n1_gain, n1_bias, qkv_w, qv, out_w, out_b, n2_gain, n2_bias, router_t.T, *rest)


def solution(mesh):
    tokens = P(("dp", "expert"))
    wide = P(("dp", "expert"), None)
    return jax.shard_map(
        local,
        mesh=mesh,
        in_specs=(
            wide, tokens, wide, tokens, P(), P(), P(), P(), P(), P(), P(), P(), P(),
            P("expert", None, None), P("expert", None), P("expert", None, None), P("expert", None), wide,
        ),
        out_specs=(
            wide, wide, P("expert"), P("expert"), P("expert", None), P("expert"), P("expert", None),
            P("expert"), P("expert"), P("expert"), P("expert", None), P("expert", None, "dp"),
            P("expert", "dp"), P("expert", "dp", None), P("expert", "dp"),
        ),
        check_vma=False,
    )
```
